32 devices in a mesh: pp: 2 (over x), cp: 4 (over z), tp: 4 (over y, core).
Axes of the slice: x: 2, y: 2, z: 4, core: 2. Of those that a mesh axis runs over, the one named last changes fastest.
Arguments:
- queries: bfloat16 [2, 512, 8192], P('pp', 'cp', 'tp'), may hold values from -9 to 9
- key_vectors: bfloat16 [2, 512, 512], P('pp', 'cp', 'tp'), may hold values from -6 to 6
- value_vectors: bfloat16 [2, 512, 512], P('pp', 'cp', 'tp'), may hold values from -30 to 30
- block_order: int32 [8], replicated, may hold values from 0 to 7, each once
- norm_gain: bfloat16 [2, 8192], P('pp', 'tp'), may hold values from 0.099609375 to 1.8984375
- kv_weight: bfloat16 [2, 8192, 1024], P('pp', 'tp'), may hold values from -0.0625 to 0.0625
Outputs:
- max_logits: float32 [2, 64], P('pp', 'tp')
- kv_next: bfloat16 [2, 512, 1024], P('pp', 'cp', 'tp')
The draws below stay inside these ranges and needn't reach their ends.
Inputs may be any that keep to these rules, and one draw needn't show every extreme that they name: A permutation; rows 2 c * 64 to (2 c + 2) * 64 - 1 hold the positions of blocks block_order[2 c] and block_order[2 c + 1], in that order.
All inputs are finite; a program needn't handle non-finite values.
Results may differ from the reference program's by a relative error of at most 0.018.
Values may be sent and summed in bfloat16 or wider, within the bound.
No kernel may reach another device: no remote copies, remote signals or barrier semaphores. Data moves between devices by JAX's collectives and lax.ppermute only.
A program may use at most 128 MiB of HBM per device.

```python
import math
import jax
import jax.numpy as jnp
from jax import lax

H = 64
KVH = 4
DH = 128
SECTIONS = 2
TOKENS = 512
BLOCK = 64
N_CP = 4


def draw_queries(key, part):
    base = jnp.clip(jax.random.normal(jax.random.fold_in(key, 1), (SECTIONS, TOKENS, H * DH), jnp.float32), -6.0, 6.0)
    return base.astype(jnp.bfloat16)


def draw_key_vectors(key, part):
    base = jnp.clip(jax.random.normal(jax.random.fold_in(key, 2), (SECTIONS, TOKENS, KVH * DH), jnp.float32), -6.0, 6.0)
    return base.astype(jnp.bfloat16)


def draw_value_vectors(key, part):
    head_ids = (jnp.arange(KVH * DH) // DH).astype(jnp.float32)
    steps_total = max(KVH - 1, 1)
    base = jnp.clip(jax.random.normal(jax.random.fold_in(key, 5), (SECTIONS, TOKENS, KVH * DH), jnp.float32), -4.0, 4.0)
    return (base * 3.0 ** (head_ids / steps_total)).astype(jnp.bfloat16)


def steps_of(own_key, extent, cuts, least, largest):
    def one(dim, blocks):
        heights = jax.random.uniform(jax.random.fold_in(jax.random.fold_in(own_key, 6), dim), (blocks,), jnp.float32, least / len(cuts), largest / len(cuts))
        return jnp.repeat(jnp.exp(heights), extent[dim] // blocks).reshape((-1,) + (1,) * (len(extent) - dim - 1))

    factor_of = one(*cuts[0])
    for cut in cuts[1:]:
        factor_of = factor_of * one(*cut)
    return factor_of


def noise(stream_key, extent, scale, bound, cuts=(), kind=jnp.bfloat16):
    loudness = steps_of(stream_key, extent, cuts, -0.22, 0.18) if cuts else 1.0
    array = jax.random.normal(stream_key, extent, jnp.float32) * scale * loudness
    return jnp.minimum(jnp.maximum(array, -bound), bound).astype(kind)


def setup_inputs(seed: int = 0) -> dict:
    key_list = jax.random.split(jax.random.key(seed), 7)
    return {
        "queries": draw_queries(jax.random.fold_in(key_list[6], 71), 0),
        "key_vectors": draw_key_vectors(jax.random.fold_in(key_list[6], 71), 0),
        "value_vectors": draw_value_vectors(jax.random.fold_in(key_list[6], 71), 0),
        "block_order": jax.random.permutation(key_list[3], 2 * N_CP).astype(jnp.int32),
        "norm_gain": jnp.clip(1.0 + 0.18 * jax.random.normal(key_list[4], (SECTIONS, H * DH), jnp.float32), 0.099609375, 1.8984375).astype(jnp.bfloat16),
        "kv_weight": noise(key_list[5], (SECTIONS, H * DH, 2 * KVH * DH), (H * DH) ** -0.5, 0.0625, ((0, 2), (1, 4))),
    }


def reference(queries, key_vectors, value_vectors, block_order, norm_gain, kv_weight):
    row_ids = jnp.arange(TOKENS, dtype=jnp.int32)
    positions = block_order[row_ids // BLOCK].astype(jnp.int32) * BLOCK + row_ids % BLOCK
    allowed = positions[None, :] <= positions[:, None]
    group_size = H // KVH
    score_scale = 1.0 / math.sqrt(DH)
    highest = lax.Precision.HIGHEST
    contexts = []
    peaks = []
    for section in range(SECTIONS):
        q_all = queries[section].reshape(TOKENS, H, DH).astype(jnp.float32)
        k_all = key_vectors[section].reshape(TOKENS, KVH, DH).astype(jnp.float32)
        v_all = value_vectors[section].reshape(TOKENS, KVH, DH).astype(jnp.float32)

        def one_head(head_index):
            q_head = lax.dynamic_index_in_dim(q_all, head_index, 1, keepdims=False)
            k_head = lax.dynamic_index_in_dim(k_all, head_index // group_size, 1, keepdims=False)
            v_head = lax.dynamic_index_in_dim(v_all, head_index // group_size, 1, keepdims=False)
            scores = jnp.dot(q_head, k_head.T, precision=highest) * score_scale
            masked = jnp.where(allowed, scores, -jnp.inf)
            rowmax = lax.optimization_barrier(jnp.max(masked, axis=1))
            exponent = jnp.where(allowed, jnp.exp(masked - rowmax[:, None]), 0.0)
            probs = exponent.astype(jnp.bfloat16).astype(jnp.float32)
            context = jnp.dot(probs, v_head, precision=highest) / lax.optimization_barrier(jnp.sum(exponent, axis=1))[:, None]
            return (context, jnp.max(rowmax))
        context, peak = lax.map(one_head, jnp.arange(H, dtype=jnp.int32))
        attn = jnp.transpose(context, (1, 0, 2)).reshape(TOKENS, H * DH).astype(jnp.bfloat16)
        contexts.append(attn)
        peaks.append(peak)
    max_logits = jnp.stack(peaks)
    results = []
    for section in range(SECTIONS):
        handed = contexts[(section - 1) % SECTIONS]
        wide = handed.astype(jnp.float32)
        mean_square = lax.optimization_barrier(jnp.mean(wide * wide, axis=1, keepdims=True))
        normed = (wide * lax.rsqrt(mean_square + 1e-05) * norm_gain[section].astype(jnp.float32)[None, :]).astype(jnp.bfloat16)
        results.append(jnp.dot(normed, kv_weight[section], preferred_element_type=jnp.float32).astype(jnp.bfloat16))
    kv_next = jnp.stack(results)
    return (max_logits, kv_next)
```

```python
import math

import jax
import jax.numpy as jnp
from jax import lax
from jax.experimental import pallas as pl
from jax.experimental.pallas import tpu as pltpu
from jax.sharding import PartitionSpec as P

DH = 128
SQUARE_ROWS = 16
MASKED = -1e30
F32 = jnp.float32
BF16 = jnp.bfloat16
WHOLE = pl.BlockSpec(memory_space=pltpu.VMEM)
SCALARS = pl.BlockSpec(memory_space=pltpu.SMEM)


def attention(order_ref, me_ref, q_ref, k_ref, v_ref, ctx_ref, peak_ref, bias, vt):
    rows = q_ref.shape[0]
    sources, part = k_ref.shape[0], k_ref.shape[1]
    keys = sources * part
    block = rows // 2
    kv_local = k_ref.shape[2] // DH
    heads = q_ref.shape[1] // DH
    scale = 1.0 / math.sqrt(DH)
    me = me_ref[0]
    lane = lax.broadcasted_iota(jnp.int32, (1, rows), 1)
    q_block = jnp.where(lane < block, order_ref[2 * me], order_ref[2 * me + 1])
    q_pos = q_block * block + lax.rem(lane, block)
    for b in range(keys // block):
        k_pos = order_ref[b] * block + lax.broadcasted_iota(jnp.int32, (block, 1), 0)
        bias[b * block:(b + 1) * block, :] = jnp.where(k_pos <= q_pos, 0.0, MASKED)
    k_all = k_ref[...].reshape(keys, kv_local * DH)
    v_all = v_ref[...].reshape(keys, kv_local * DH)
    vt[...] = v_all.astype(F32).T.astype(BF16)
    for h in range(heads):
        cols = slice(h * DH, (h + 1) * DH)
        g = h // (heads // kv_local)
        group = slice(g * DH, (g + 1) * DH)
        s = lax.dot_general(k_all[:, group], q_ref[:, cols], (((1,), (1,)), ((), ())), preferred_element_type=F32)
        s = s * scale + bias[...]
        m = jnp.max(s, axis=0, keepdims=True)
        p = jnp.exp(s - m)
        total = jnp.sum(p, axis=0, keepdims=True)
        o = lax.dot_general(vt[group, :], p.astype(BF16), (((1,), (0,)), ((), ())), preferred_element_type=F32)
        ctx_ref[:, cols] = (o / total).T.astype(BF16)
        peak_ref[:, h:h + 1] = jnp.max(m, axis=1, keepdims=True)


def project(ctx_ref, gain_ref, w_ref, out_ref):
    rows = ctx_ref.shape[0]
    peers, cols = out_ref.shape[0], out_ref.shape[2]
    wide = ctx_ref[...].astype(F32)
    squares = jnp.sum(wide * wide, axis=1, keepdims=True)
    scaled = (wide * gain_ref[...].astype(F32)).astype(BF16)
    lanes = jnp.broadcast_to(squares, (rows, 128)).T[:SQUARE_ROWS, :]
    first = lanes.astype(BF16)
    rest = (lanes - first.astype(F32)).astype(BF16)
    for d in range(peers):
        out_ref[d, :rows, :] = jnp.dot(scaled, w_ref[:, d * cols:(d + 1) * cols], preferred_element_type=F32).astype(BF16)
        out_ref[d, rows:, :128] = first
        out_ref[d, rows:, 128:256] = rest
        if cols > 256:
            out_ref[d, rows:, 256:] = jnp.zeros((SQUARE_ROWS, cols - 256), BF16)


def finish(features, parts_ref, out_ref):
    rows = out_ref.shape[0]
    peers = parts_ref.shape[0]
    total = parts_ref[0].astype(F32)
    for d in range(1, peers):
        total = total + parts_ref[d].astype(F32)
    squares = total[rows:rows + 8, :128] + total[rows:rows + 8, 128:256]
    inverse = lax.rsqrt(squares / features + 1e-05)
    column = jnp.broadcast_to(inverse[:1, :], (rows, rows)).T[:, :1]
    out_ref[...] = (total[:rows, :] * column).astype(BF16)


def spread(block, axis):
    copies = jnp.broadcast_to(block[None], (lax.axis_size(axis),) + block.shape)
    return lax.all_to_all(copies, axis, 0, 0)


def shifted(block, axis, distance):
    size = lax.axis_size(axis)
    return lax.ppermute(block, axis, [((i - distance) % size, i) for i in range(size)])


def call(kernel, outs, specs, args, scratch=(), limit=16, name=None):
    return pl.pallas_call(
        kernel,
        out_shape=outs,
        in_specs=specs,
        out_specs=jax.tree.map(lambda _: WHOLE, outs),
        scratch_shapes=scratch,
        name=name,
        compiler_params=pltpu.CompilerParams(vmem_limit_bytes=limit * 2**20),
    )(*args)


def on_device(queries, key_vectors, value_vectors, block_order, norm_gain, kv_weight):
    rows = queries.shape[1]
    features_local = queries.shape[2]
    heads = features_local // DH
    peers = lax.axis_size("tp")
    sources = lax.axis_size("cp")
    keys = sources * rows
    out_cols = kv_weight.shape[2] // peers
    me = lax.axis_index("cp").astype(jnp.int32).reshape(1)
    k_all = spread(key_vectors[0], "cp")
    v_all = spread(value_vectors[0], "cp")
    shape = jax.ShapeDtypeStruct
    context, peak = call(
        attention,
        (shape((rows, features_local), BF16), shape((1, heads), F32)),
        [SCALARS, SCALARS, WHOLE, WHOLE, WHOLE],
        (block_order, me, queries[0], k_all, v_all),
        (pltpu.VMEM((keys, rows), F32), pltpu.VMEM((key_vectors.shape[2], keys), BF16)),
        name="attention",
    )
    handed = shifted(context, "pp", 1)
    max_logits = jnp.max(spread(peak, "cp"), axis=0)
    partial = call(
        project,
        shape((peers, rows + SQUARE_ROWS, out_cols), BF16),
        [WHOLE, WHOLE, WHOLE],
        (handed, norm_gain, kv_weight[0]),
        limit=24,
        name="project",
    )
    parts = lax.all_to_all(partial, "tp", 0, 0)

    def last(parts_ref, out_ref):
        finish(features_local * peers, parts_ref, out_ref)

    kv_next = call(last, shape((rows, out_cols), BF16), [WHOLE], (parts,), name="finish")
    return (max_logits, kv_next[None])


def solution(mesh):
    return jax.shard_map(
        on_device,
        mesh=mesh,
        in_specs=(
            P("pp", "cp", "tp"),
            P("pp", "cp", "tp"),
            P("pp", "cp", "tp"),
            P(),
            P("pp", "tp"),
            P("pp", "tp", None),
        ),
        out_specs=(P("pp", "tp"), P("pp", "cp", "tp")),
        check_vma=False,
    )
```

```python
import functools
import math

import jax
import jax.numpy as jnp
from jax import lax
from jax.experimental import pallas as pl
from jax.experimental.pallas import tpu as pltpu
from jax.sharding import PartitionSpec as P

DH = 128
SQUARE_ROWS = 16
MASKED = -1e30
LOG2E = math.log2(math.e)
F32 = jnp.float32
BF16 = jnp.bfloat16
WHOLE = pl.BlockSpec(memory_space=pltpu.VMEM)
SCALARS = pl.BlockSpec(memory_space=pltpu.SMEM)
OUTSIDE = pl.BlockSpec(memory_space=pl.ANY)


def call(kernel, outs, args, specs=None, scratch=(), limit=16, name=None, cost=None):
    return pl.pallas_call(
        kernel,
        out_shape=outs,
        in_specs=specs or [WHOLE] * len(args),
        out_specs=jax.tree.map(lambda _: WHOLE, outs),
        scratch_shapes=scratch,
        name=name,
        cost_estimate=cost,
        compiler_params=pltpu.CompilerParams(vmem_limit_bytes=limit * 2**20),
    )(*args)


def pair_up(k_ref, v_ref, pair_ref, sems):
    copies = [
        pltpu.make_async_copy(k_ref.at[0], pair_ref.at[0], sems.at[0]),
        pltpu.make_async_copy(v_ref.at[0], pair_ref.at[1], sems.at[1]),
    ]
    for copy in copies:
        copy.start()
    for copy in copies:
        copy.wait()


def prepare(order_ref, q_in_ref, pair_in_ref, q_ref, pair_ref, bias_ref):
    q_ref[...] = q_in_ref[0]
    pair_ref[...] = pair_in_ref[...]
    sources = lax.axis_size("cp")
    me = lax.axis_index("cp")
    rows = q_ref.shape[0]
    block = rows // 2
    lane = lax.broadcasted_iota(jnp.int32, (1, rows), 1)
    q_block = jnp.where(lane < block, order_ref[2 * me], order_ref[2 * me + 1])
    q_pos = q_block * block + lax.rem(lane, block)
    for d in range(sources):
        source = lax.rem(me - d + sources, sources)
        for half in range(2):
            first = d * rows + half * block
            k_pos = order_ref[2 * source + half] * block + lax.broadcasted_iota(jnp.int32, (block, 1), 0)
            bias_ref[first:first + block, :] = jnp.where(k_pos <= q_pos, 0.0, MASKED)


def attend(first_head, sources, q_ref, bias_ref, *refs):
    pairs = refs[:sources]
    before_ref, ctx_ref, peak_ref, vt = refs[sources:] if first_head else (None, *refs[sources:])
    rows = q_ref.shape[0]
    heads = q_ref.shape[1] // DH
    kv_local = pairs[0].shape[2] // DH
    factor = LOG2E / math.sqrt(DH)
    for d in range(sources):
        vt[:, d * rows:(d + 1) * rows] = pairs[d][1].astype(F32).T.astype(BF16)
    if first_head:
        peak_ref[:, :first_head] = before_ref[...]
    for i in range(ctx_ref.shape[1] // DH):
        h = first_head + i
        cols = slice(h * DH, (h + 1) * DH)
        g = h // (heads // kv_local)
        group = slice(g * DH, (g + 1) * DH)
        q = q_ref[:, cols]
        s = jnp.concatenate(
            [lax.dot_general(pair[0, :, group], q, (((1,), (1,)), ((), ())), preferred_element_type=F32) for pair in pairs],
            axis=0,
        )
        s = s * factor + bias_ref[...]
        m = jnp.max(s, axis=0, keepdims=True)
        p = jnp.exp2(s - m)
        total = jnp.sum(p, axis=0, keepdims=True)
        o = jnp.dot(vt[group, :], p.astype(BF16), preferred_element_type=F32)
        ctx_ref[:, i * DH:(i + 1) * DH] = (o * (1.0 / total)).T.astype(BF16)
        peak_ref[:, h:h + 1] = jnp.max(m, axis=1, keepdims=True) * (1.0 / LOG2E)


def project_first(ctx_ref, gain_ref, w_ref, *refs):
    peak_refs, (sum_ref, square_ref, peak_ref) = refs[:-3], refs[-3:]
    peak = peak_refs[0][...]
    for ref in peak_refs[1:]:
        peak = jnp.maximum(peak, ref[...])
    peak_ref[...] = peak
    wide = ctx_ref[...].astype(F32)
    width = wide.shape[1]
    square_ref[...] = jnp.broadcast_to(jnp.sum(wide * wide, axis=1, keepdims=True), square_ref.shape)
    scaled = (wide * gain_ref[:, :width].astype(F32)).astype(BF16)
    sum_ref[...] = jnp.dot(scaled, w_ref[:width, :], preferred_element_type=F32)


def project_last(ctx_ref, gain_ref, w_ref, sum_ref, square_ref, give_ref, keep_ref):
    wide = ctx_ref[...].astype(F32)
    rows, width = wide.shape
    start = w_ref.shape[0] - width
    squares = square_ref[...] + jnp.sum(wide * wide, axis=1, keepdims=True)
    scaled = (wide * gain_ref[:, start:].astype(F32)).astype(BF16)
    lanes = squares.T[:SQUARE_ROWS, :]
    first = lanes.astype(BF16)
    rest = (lanes - first.astype(F32)).astype(BF16)
    groups, cols = give_ref.shape[0], give_ref.shape[2]
    core = lax.rem(lax.axis_index("tp"), 2)
    for ref, side in ((give_ref, 1 - core), (keep_ref, core)):
        for y in range(groups):
            at = pl.ds(pl.multiple_of((2 * y + side) * cols, cols), cols)
            part = sum_ref[:, at] + jnp.dot(scaled, w_ref[start:, at], preferred_element_type=F32)
            ref[y, :rows, :] = part.astype(BF16)
            ref[y, rows:, :rows] = first
            ref[y, rows:, rows:2 * rows] = rest
            if cols > 2 * rows:
                ref[y, rows:, 2 * rows:] = jnp.zeros((SQUARE_ROWS, cols - 2 * rows), BF16)


def merge(keep_ref, got_ref, *give_refs):
    groups = keep_ref.shape[0]
    mine = lax.axis_index("tp") // 2
    for step, ref in enumerate(give_refs):
        y = lax.rem(mine + step, groups)
        total = keep_ref[y].astype(F32) + got_ref[y].astype(F32)
        ref[...] = total.astype(ref.dtype)


def finish(features, keep_ref, *refs):
    out_ref = refs[-1]
    rows = out_ref.shape[0]
    total = keep_ref[...]
    for ref in refs[:-1]:
        total = total + ref[...].astype(F32)
    squares = total[rows:rows + 8, :rows] + total[rows:rows + 8, rows:2 * rows]
    inverse = lax.rsqrt(squares / features + 1e-05)
    column = jnp.broadcast_to(inverse[:1, :], (rows, rows)).T[:, :1]
    out_ref[...] = (total[:rows, :] * column).astype(BF16)


def shifted(block, axis, distance):
    size = lax.axis_size(axis)
    return lax.ppermute(block, axis, [((i - distance) % size, i) for i in range(size)])


def on_device(queries, key_vectors, value_vectors, block_order, norm_gain, kv_weight):
    rows, width = queries.shape[1:]
    heads = width // DH
    peers = lax.axis_size("tp")
    sources = lax.axis_size("cp")
    kv_width = key_vectors.shape[2]
    columns = kv_weight.shape[2]
    out_cols = columns // peers
    shape = jax.ShapeDtypeStruct
    dma = pltpu.SemaphoreType.DMA
    pair = call(
        pair_up, shape((2, rows, kv_width), BF16), (key_vectors, value_vectors), [OUTSIDE] * 2, [dma((2,))], limit=56, name="pair_up"
    )
    pairs = [pair] + [shifted(pair, "cp", d) for d in range(1, sources)]
    q, pairs[0], bias = call(
        prepare,
        (shape((rows, width), BF16), shape(pair.shape, BF16), shape((sources * rows, rows), F32)),
        (block_order, queries, pair),
        [SCALARS, WHOLE, WHOLE],
        name="prepare",
    )
    w = kv_weight[0]
    chunks = 2
    part_heads = heads // chunks
    handed, peaks = [], []
    for c in range(chunks):
        context, peak = call(
            functools.partial(attend, c * part_heads, sources),
            (shape((rows, part_heads * DH), BF16), shape((1, (c + 1) * part_heads), F32)),
            (q, bias, *pairs, *peaks[-1:]),
            scratch=[pltpu.VMEM((kv_width, sources * rows), BF16)],
            name="attend",
        )
        handed.append(shifted(context, "pp", 1))
        peaks.append(peak)
    peak = peaks[-1]
    total, squares, max_logits = call(
        project_first,
        (shape((rows, columns), F32), shape((rows, 128), F32), shape((1, heads), F32)),
        (handed[0], norm_gain, w, peak, *[shifted(peak, "cp", d) for d in range(1, sources)]),
        name="project_first",
    )
    part = shape((peers // 2, rows + SQUARE_ROWS, out_cols), BF16)
    give, keep = call(project_last, (part, part), (handed[1], norm_gain, w, total, squares), name="project_last")
    got = lax.ppermute(give, "tp", [(i, i ^ 1) for i in range(peers)])
    slab = (rows + SQUARE_ROWS, out_cols)
    merged = call(
        merge,
        [shape(slab, F32)] + [shape(slab, BF16)] * (peers // 2 - 1),
        (keep, got),
        name="merge",
    )
    parts = [
        lax.ppermute(block, "tp", [(i, (i + 2 * (step + 1)) % peers) for i in range(peers)])
        for step, block in enumerate(merged[1:])
    ]
    kv_next = call(
        functools.partial(finish, width * peers), shape((rows, out_cols), BF16), (merged[0], *parts), name="finish"
    )
    return (max_logits, kv_next[None])


def solution(mesh):
    return jax.shard_map(
        on_device,
        mesh=mesh,
        in_specs=(
            P("pp", "cp", "tp"),
            P("pp", "cp", "tp"),
            P("pp", "cp", "tp"),
            P(),
            P("pp", "tp"),
            P("pp", "tp", None),
        ),
        out_specs=(P("pp", "tp"), P("pp", "cp", "tp")),
        check_vma=False,
    )
```

```python
import functools
import math

import jax
import jax.numpy as jnp
from jax import lax
from jax.experimental import pallas as pl
from jax.experimental.pallas import tpu as pltpu
from jax.sharding import PartitionSpec as P

DH = 128
CHUNKS = 2
SQUARE_ROWS = 16
MASKED = -1e30
LOG2E = math.log2(math.e)
F32 = jnp.float32
BF16 = jnp.bfloat16
WHOLE = pl.BlockSpec(memory_space=pltpu.VMEM)
SCALARS = pl.BlockSpec(memory_space=pltpu.SMEM)


def call(kernel, outs, args, specs=None, scratch=(), limit=16, name=None, aliases=None, micros=0):
    return pl.pallas_call(
        kernel,
        out_shape=outs,
        in_specs=specs or [WHOLE] * len(args),
        out_specs=jax.tree.map(lambda _: WHOLE, outs),
        scratch_shapes=scratch,
        name=name,
        input_output_aliases=aliases or {},
        cost_estimate=pl.CostEstimate(flops=int(micros * 1e9), bytes_accessed=0, transcendentals=0) if micros else None,
        compiler_params=pltpu.CompilerParams(vmem_limit_bytes=limit * 2**20),
    )(*args)


def bind_kernel(block_ref, *refs):
    refs[-1][...] = block_ref[...]


def bind(block, *after):
    return call(
        bind_kernel,
        jax.ShapeDtypeStruct(block.shape, block.dtype),
        (block, *after),
        [WHOLE] + [pl.BlockSpec(memory_space=pl.ANY)] * len(after),
        name="bind",
    )


def split(q_ref, after, *part_refs):
    width = part_refs[0].shape[1]
    for c, ref in enumerate(part_refs):
        ref[...] = q_ref[0, :, c * width:(c + 1) * width]


def prepare(order_ref, after, bias_ref):
    sources = lax.axis_size("cp")
    me = lax.axis_index("cp")
    rows = bias_ref.shape[1]
    block = rows // 2
    lane = lax.broadcasted_iota(jnp.int32, (1, rows), 1)
    q_block = jnp.where(lane < block, order_ref[2 * me], order_ref[2 * me + 1])
    q_pos = q_block * block + lax.rem(lane, block)
    for d in range(sources):
        source = lax.rem(me - d + sources, sources)
        for half in range(2):
            first = d * rows + half * block
            k_pos = order_ref[2 * source + half] * block + lax.broadcasted_iota(jnp.int32, (block, 1), 0)
            bias_ref[first:first + block, :] = jnp.where(k_pos <= q_pos, 0.0, MASKED)


def attend(first_head, heads, sources, q_ref, gain_ref, bias_ref, *refs):
    pairs = refs[:sources]
    before, (scaled_ref, square_ref, peak_ref, k_all, vt) = refs[sources:-5], refs[-5:]
    rows, width = q_ref.shape
    kv_local = pairs[0].shape[2] // DH
    factor = LOG2E / math.sqrt(DH)
    squares = jnp.zeros((1, rows), F32)
    if before:
        square_in, peak_in = before
        squares = square_in[:1, :]
        peak_ref[:, :first_head] = peak_in[...]
    for d in range(sources):
        part = slice(d * rows, (d + 1) * rows)
        k_all[part, :] = pairs[d][0]
        vt[:, part] = pairs[d][1].astype(F32).T.astype(BF16)
    bias = bias_ref[...]
    for i in range(0, width // DH, 2):
        h = first_head + i
        g = h // (heads // kv_local)
        group = slice(g * DH, (g + 1) * DH)
        q = jnp.concatenate([q_ref[:, i * DH:(i + 1) * DH], q_ref[:, (i + 1) * DH:(i + 2) * DH]], axis=0)
        s = lax.dot_general(k_all[:, group], q, (((1,), (1,)), ((), ())), preferred_element_type=F32)
        s = s * factor + jnp.concatenate([bias, bias], axis=1)
        m = jnp.max(s, axis=0, keepdims=True)
        p = jnp.exp2(s - m)
        total = jnp.sum(p, axis=0, keepdims=True)
        o = jnp.dot(vt[group, :], p.astype(BF16), preferred_element_type=F32)
        o = (o * (1.0 / total)).astype(BF16).astype(F32)
        for j in range(2):
            cols = slice((i + j) * DH, (i + j + 1) * DH)
            lanes = slice(j * rows, (j + 1) * rows)
            one = o[:, lanes]
            squares = squares + jnp.sum(one * one, axis=0, keepdims=True)
            gain = gain_ref[:, (h + j) * DH:(h + j + 1) * DH].astype(F32)
            scaled_ref[:, cols] = (one.T * gain).astype(BF16)
            peak_ref[:, h + j:h + j + 1] = jnp.max(m[:, lanes], axis=1, keepdims=True) * (1.0 / LOG2E)
    square_ref[...] = jnp.broadcast_to(squares, square_ref.shape)


def project(w_ref, square_ref, *refs):
    scaled, (give_ref, keep_ref) = refs[:-2], refs[-2:]
    rows, width = scaled[0].shape
    lanes = jnp.broadcast_to(square_ref[:1, :], (SQUARE_ROWS, rows))
    first = lanes.astype(BF16)
    rest = (lanes - first.astype(F32)).astype(BF16)
    groups, cols = give_ref.shape[0], give_ref.shape[2]
    core = lax.rem(lax.axis_index("tp"), 2)
    for ref, side in ((give_ref, 1 - core), (keep_ref, core)):
        for y in range(groups):
            at = pl.ds(pl.multiple_of((2 * y + side) * cols, cols), cols)
            part = jnp.dot(scaled[0][...], w_ref[:width, at], preferred_element_type=F32)
            for c in range(1, len(scaled)):
                part += jnp.dot(scaled[c][...], w_ref[c * width:(c + 1) * width, at], preferred_element_type=F32)
            ref[y, :rows, :] = part.astype(BF16)
            ref[y, rows:, :rows] = first
            ref[y, rows:, rows:2 * rows] = rest
            if cols > 2 * rows:
                ref[y, rows:, 2 * rows:] = jnp.zeros((SQUARE_ROWS, cols - 2 * rows), BF16)


def merge(keep_ref, got_ref, peak_ref, peak_got, peak_out, *give_refs):
    groups = keep_ref.shape[0]
    mine = lax.axis_index("tp") // 2
    peak_out[...] = jnp.maximum(peak_ref[...], peak_got[...])
    for step, ref in enumerate(give_refs):
        y = lax.rem(mine + step, groups)
        total = keep_ref[y].astype(F32) + got_ref[y].astype(F32)
        ref[...] = total.astype(ref.dtype)


def finish(features, peak_ref, peak_got, keep_ref, *refs):
    peak_out, out_ref = refs[-2:]
    rows = out_ref.shape[0]
    peak_out[...] = jnp.maximum(peak_ref[...], peak_got[...])
    total = keep_ref[...]
    for ref in refs[:-2]:
        total = total + ref[...].astype(F32)
    squares = total[rows:rows + 8, :rows] + total[rows:rows + 8, rows:2 * rows]
    inverse = lax.rsqrt(squares / features + 1e-05)
    column = jnp.broadcast_to(inverse[:1, :], (rows, rows)).T[:, :1]
    out_ref[...] = (total[:rows, :] * column).astype(BF16)


def shifted(block, axis, distance):
    size = lax.axis_size(axis)
    return lax.ppermute(block, axis, [((i - distance) % size, i) for i in range(size)])


def partner(index, step, size):
    return (index + step) % size if size & (size - 1) else index ^ step


def swapped(block, axis, step):
    size = lax.axis_size(axis)
    return lax.ppermute(block, axis, [(i, partner(i, step, size)) for i in range(size)])


def returned(block, step):
    sections, sources = lax.axis_size("pp"), lax.axis_size("cp")
    route = [
        (s * sources + c, (s - 1) % sections * sources + partner(c, step, sources))
        for s in range(sections)
        for c in range(sources)
    ]
    return lax.ppermute(block, ("pp", "cp"), route)


def on_device(queries, key_vectors, value_vectors, block_order, norm_gain, kv_weight):
    rows, width = queries.shape[1:]
    heads = width // DH
    peers = lax.axis_size("tp")
    sources = lax.axis_size("cp")
    kv_width = key_vectors.shape[2]
    columns = kv_weight.shape[2]
    out_cols = columns // peers
    shape = jax.ShapeDtypeStruct
    steps = [2**i for i in range((sources - 1).bit_length())]

    pair_here = jnp.concatenate([key_vectors, value_vectors])
    pair = shifted(pair_here, "pp", 1)
    part_width = width // CHUNKS
    parts = call(
        split, [shape((rows, part_width), BF16)] * CHUNKS, (queries, pair_here), [WHOLE, pl.BlockSpec(memory_space=pl.ANY)], name="split"
    )
    parts = [shifted(part, "pp", 1) for part in parts]
    pairs = [pair] + [shifted(pair, "cp", d) for d in range(1, sources)]
    bias = call(
        prepare,
        shape((sources * rows, rows), F32),
        (block_order, pair),
        [SCALARS, pl.BlockSpec(memory_space=pl.ANY)],
        name="prepare",
        micros=4,
    )
    scaled, before = [], ()
    for c in range(CHUNKS):
        first = c * part_width // DH
        part, *before = call(
            functools.partial(attend, first, heads, sources),
            (
                shape((rows, part_width), BF16),
                shape((8, rows), F32),
                shape((1, first + part_width // DH), F32),
            ),
            (parts[c], norm_gain, bias, *pairs, *before),
            scratch=[pltpu.VMEM((sources * rows, kv_width), BF16), pltpu.VMEM((kv_width, sources * rows), BF16)],
            name="attend",
            micros=1.5,
        )
        scaled.append(part)
    squares, peak = before
    slab = shape((peers // 2, rows + SQUARE_ROWS, out_cols), BF16)
    give, keep = call(project, (slab, slab), (kv_weight[0], squares, *scaled), name="project", micros=1)
    peak = bind(peak, give)
    got = lax.ppermute(give, "tp", [(i, i ^ 1) for i in range(peers)])
    slab = (rows + SQUARE_ROWS, out_cols)
    peak, mine, *others = call(
        merge,
        [shape((1, heads), F32), shape(slab, F32)] + [shape(slab, BF16)] * (peers // 2 - 1),
        (keep, got, shifted(peak, "pp", -1), returned(peak, steps[0])),
        name="merge",
    )
    for step in steps[1:-1]:
        peak = jnp.maximum(peak, swapped(peak, "cp", step))
    others = [
        lax.ppermute(block, "tp", [(i, (i + 2 * (step + 1)) % peers) for i in range(peers)])
        for step, block in enumerate(others)
    ]
    max_logits, kv_next = call(
        functools.partial(finish, width * peers),
        (shape((1, heads), F32), shape((rows, out_cols), BF16)),
        (peak, swapped(peak, "cp", steps[-1]), mine, *others),
        name="finish",
    )
    return (max_logits, kv_next[None])


def solution(mesh):
    return jax.shard_map(
        on_device,
        mesh=mesh,
        in_specs=(
            P("pp", "cp", "tp"),
            P("pp", "cp", "tp"),
            P("pp", "cp", "tp"),
            P(),
            P("pp", "tp"),
            P("pp", "tp", None),
        ),
        out_specs=(P("pp", "tp"), P("pp", "cp", "tp")),
        check_vma=False,
    )
```

```python
import functools
import math

import jax
import jax.numpy as jnp
from jax import lax
from jax.experimental import pallas as pl
from jax.experimental.pallas import tpu as pltpu
from jax.sharding import PartitionSpec as P

DH = 128
LANES = 128
SQUARE_ROWS = 16
MASKED = -(2.0**100)
LOG2E = math.log2(math.e)
F32 = jnp.float32
BF16 = jnp.bfloat16
WHOLE = pl.BlockSpec(memory_space=pltpu.VMEM)
SCALARS = pl.BlockSpec(memory_space=pltpu.SMEM)


def call(kernel, outs, args, specs=None, scratch=(), limit=16, name=None, aliases=None, micros=0):
    return pl.pallas_call(
        kernel,
        out_shape=outs,
        in_specs=specs or [WHOLE] * len(args),
        out_specs=jax.tree.map(lambda _: WHOLE, outs),
        scratch_shapes=scratch,
        name=name,
        input_output_aliases=aliases or {},
        cost_estimate=pl.CostEstimate(flops=int(micros * 1e9), bytes_accessed=0, transcendentals=0) if micros else None,
        compiler_params=pltpu.CompilerParams(vmem_limit_bytes=limit * 2**20),
    )(*args)


def bind_kernel(block_ref, *refs):
    refs[-1][...] = block_ref[...]


def bind(block, *after):
    return call(
        bind_kernel,
        jax.ShapeDtypeStruct(block.shape, block.dtype),
        (block, *after),
        [WHOLE] + [pl.BlockSpec(memory_space=pl.ANY)] * len(after),
        name="bind",
    )


def prepare(order_ref, after, feature_ref):
    sources = lax.axis_size("cp")
    me = lax.axis_index("cp")
    block = feature_ref.shape[1] // (2 * sources)
    row = lax.broadcasted_iota(jnp.int32, (block, LANES), 0)
    lane = lax.broadcasted_iota(jnp.int32, (block, LANES), 1)
    for side in range(2):
        mine = order_ref[2 * me + side]
        for d in range(sources):
            source = lax.rem(me - d + sources, sources)
            for half in range(2):
                other = order_ref[2 * source + half]
                column = jnp.where(other == mine, row, jnp.where(other > mine, block, -1))
                first = (2 * d + half) * block
                feature_ref[side, first:first + block, :] = jnp.where(lane == column, 1.0, 0.0).astype(BF16)


def attend(sources, q_ref, gain_ref, feature_ref, *refs):
    pairs = refs[:sources]
    scaled_ref, square_ref, peak_ref, k_all, vt = refs[sources:]
    rows, width = q_ref.shape[1:]
    block = rows // 2
    heads = width // DH
    kv_local = pairs[0].shape[2] // DH
    tile = 256 // block
    scale = 1.0 / math.sqrt(DH)
    ahead = lax.rem(lax.broadcasted_iota(jnp.int32, (tile * block, LANES), 0), block)
    lane = lax.broadcasted_iota(jnp.int32, (tile * block, LANES), 1)
    blocked = jnp.where((lane > ahead) & (lane <= block), MASKED, 0.0).astype(BF16)
    squares = [jnp.zeros((1, tile * block), F32)] * 2
    vt[DH:, :] = jnp.ones((vt.shape[0] - DH, vt.shape[1]), BF16)
    for side in range(2):
        k_all[side, :, DH:] = feature_ref[side]
    for g in range(kv_local):
        group = slice(g * DH, (g + 1) * DH)
        for d in range(sources):
            part = slice(d * rows, (d + 1) * rows)
            for side in range(2):
                k_all[side, part, :DH] = pairs[d][0, :, group]
            vt[:DH, part] = pairs[d][1, :, group].astype(F32).T.astype(BF16)
        for first in range(g * heads // kv_local, (g + 1) * heads // kv_local, tile):
            peaks = []
            for side in range(2):
                tokens = slice(side * block, (side + 1) * block)
                q = jnp.concatenate([q_ref[0, tokens, h * DH:(h + 1) * DH] for h in range(first, first + tile)], axis=0)
                q = jnp.concatenate([q, blocked], axis=1)
                s = lax.dot_general(k_all[side], q, (((1,), (1,)), ((), ())), preferred_element_type=F32)
                m = jnp.max(s, axis=0, keepdims=True)
                p = jnp.exp2((s - m) * (scale * LOG2E)).astype(BF16)
                o = jnp.dot(vt[...], p, preferred_element_type=F32)
                o = (o[:DH, :] * (1.0 / o[DH:DH + 1, :])).astype(BF16)
                wide = o.astype(F32)
                squares[side] = squares[side] + jnp.sum(wide * wide, axis=0, keepdims=True)
                peaks.append(m)
                turned = o.T.astype(F32)
                for j in range(tile):
                    cols = slice((first + j) * DH, (first + j + 1) * DH)
                    one = turned[j * block:(j + 1) * block, :]
                    scaled_ref[tokens, cols] = (one * gain_ref[:, cols].astype(F32)).astype(BF16)
            peak = jnp.maximum(*peaks)
            for j in range(tile):
                one = jnp.max(peak[:, j * block:(j + 1) * block], axis=1, keepdims=True)
                peak_ref[:, first + j:first + j + 1] = one * scale
    for side in range(2):
        total = squares[side][:, :block]
        for j in range(1, tile):
            total = total + squares[side][:, j * block:(j + 1) * block]
        square_ref[:, side * block:(side + 1) * block] = jnp.broadcast_to(total, (8, block))


def project(w_ref, square_ref, scaled_ref, give_ref, keep_ref):
    rows = scaled_ref.shape[0]
    lanes = jnp.broadcast_to(square_ref[:1, :], (SQUARE_ROWS, rows))
    first = lanes.astype(BF16)
    rest = (lanes - first.astype(F32)).astype(BF16)
    groups, cols = give_ref.shape[0], give_ref.shape[2]
    core = lax.rem(lax.axis_index("tp"), 2)
    for ref, side in ((give_ref, 1 - core), (keep_ref, core)):
        for y in range(groups):
            at = pl.ds(pl.multiple_of((2 * y + side) * cols, cols), cols)
            part = jnp.dot(scaled_ref[...], w_ref[:, at], preferred_element_type=F32)
            ref[y, :rows, :] = part.astype(BF16)
            ref[y, rows:, :rows] = first
            ref[y, rows:, rows:2 * rows] = rest
            if cols > 2 * rows:
                ref[y, rows:, 2 * rows:] = jnp.zeros((SQUARE_ROWS, cols - 2 * rows), BF16)


def merge(keep_ref, got_ref, peak_ref, peak_got, peak_out, *give_refs):
    groups = keep_ref.shape[0]
    mine = lax.axis_index("tp") // 2
    peak_out[...] = jnp.maximum(peak_ref[...], peak_got[...])
    for step, ref in enumerate(give_refs):
        y = lax.rem(mine + step, groups)
        total = keep_ref[y].astype(F32) + got_ref[y].astype(F32)
        ref[...] = total.astype(ref.dtype)


def finish(features, peak_ref, peak_got, keep_ref, *refs):
    peak_out, out_ref = refs[-2:]
    rows = out_ref.shape[0]
    peak_out[...] = jnp.maximum(peak_ref[...], peak_got[...])
    total = keep_ref[...]
    for ref in refs[:-2]:
        total = total + ref[...].astype(F32)
    squares = total[rows:rows + 8, :rows] + total[rows:rows + 8, rows:2 * rows]
    inverse = lax.rsqrt(squares / features + 1e-05)
    column = jnp.broadcast_to(inverse[:1, :], (rows, rows)).T[:, :1]
    out_ref[...] = (total[:rows, :] * column).astype(BF16)


def shifted(block, axis, distance):
    size = lax.axis_size(axis)
    return lax.ppermute(block, axis, [((i - distance) % size, i) for i in range(size)])


def partner(index, step, size):
    return (index + step) % size if size & (size - 1) else index ^ step


def swapped(block, axis, step):
    size = lax.axis_size(axis)
    return lax.ppermute(block, axis, [(i, partner(i, step, size)) for i in range(size)])


def returned(block, step):
    sections, sources = lax.axis_size("pp"), lax.axis_size("cp")
    route = [
        (s * sources + c, (s - 1) % sections * sources + partner(c, step, sources))
        for s in range(sections)
        for c in range(sources)
    ]
    return lax.ppermute(block, ("pp", "cp"), route)


def on_device(queries, key_vectors, value_vectors, block_order, norm_gain, kv_weight):
    rows, width = queries.shape[1:]
    heads = width // DH
    peers = lax.axis_size("tp")
    sources = lax.axis_size("cp")
    kv_width = key_vectors.shape[2]
    columns = kv_weight.shape[2]
    out_cols = columns // peers
    shape = jax.ShapeDtypeStruct
    steps = [2**i for i in range((sources - 1).bit_length())]

    pair_here = jnp.stack([key_vectors[0], value_vectors[0]])
    pair = shifted(pair_here, "pp", 1)
    q = shifted(queries, "pp", 1)
    pairs = [pair] + [shifted(pair, "cp", d) for d in range(1, sources)]
    features = call(
        prepare,
        shape((2, sources * rows, LANES), BF16),
        (block_order, pair),
        [SCALARS, pl.BlockSpec(memory_space=pl.ANY)],
        name="prepare",
        micros=4,
    )
    scaled, squares, peak = call(
        functools.partial(attend, sources),
        (shape((rows, width), BF16), shape((8, rows), F32), shape((1, heads), F32)),
        (q, norm_gain, features, *pairs),
        scratch=[pltpu.VMEM((2, sources * rows, DH + LANES), BF16), pltpu.VMEM((DH + 16, sources * rows), BF16)],
        limit=28,
        name="attend",
        micros=3,
    )
    slab = shape((peers // 2, rows + SQUARE_ROWS, out_cols), BF16)
    give, keep = call(project, (slab, slab), (kv_weight[0], squares, scaled), name="project", micros=1)
    peak = bind(peak, give)
    got = lax.ppermute(give, "tp", [(i, i ^ 1) for i in range(peers)])
    slab = (rows + SQUARE_ROWS, out_cols)
    peak, mine, *others = call(
        merge,
        [shape((1, heads), F32), shape(slab, F32)] + [shape(slab, BF16)] * (peers // 2 - 1),
        (keep, got, shifted(peak, "pp", -1), returned(peak, steps[0])),
        name="merge",
    )
    for step in steps[1:-1]:
        peak = jnp.maximum(peak, swapped(peak, "cp", step))
    others = [
        lax.ppermute(block, "tp", [(i, (i + 2 * (step + 1)) % peers) for i in range(peers)])
        for step, block in enumerate(others)
    ]
    max_logits, kv_next = call(
        functools.partial(finish, width * peers),
        (shape((1, heads), F32), shape((rows, out_cols), BF16)),
        (peak, swapped(peak, "cp", steps[-1]), mine, *others),
        name="finish",
    )
    return (max_logits, kv_next[None])


def solution(mesh):
    return jax.shard_map(
        on_device,
        mesh=mesh,
        in_specs=(
            P("pp", "cp", "tp"),
            P("pp", "cp", "tp"),
            P("pp", "cp", "tp"),
            P(),
            P("pp", "tp"),
            P("pp", "tp", None),
        ),
        out_specs=(P("pp", "tp"), P("pp", "cp", "tp")),
        check_vma=False,
    )
```

```python
import functools
import math

import jax
import jax.numpy as jnp
from jax import lax
from jax.experimental import pallas as pl
from jax.experimental.pallas import tpu as pltpu
from jax.sharding import PartitionSpec as P

DH = 128
LANES = 128
CHUNKS = 2
SQUARE_ROWS = 16
MASKED = -(2.0**100)
LOG2E = math.log2(math.e)
F32 = jnp.float32
BF16 = jnp.bfloat16
WHOLE = pl.BlockSpec(memory_space=pltpu.VMEM)
OUTSIDE = pl.BlockSpec(memory_space=pl.ANY)
SCALARS = pl.BlockSpec(memory_space=pltpu.SMEM)


def call(kernel, outs, args, specs=None, scratch=(), limit=16, name=None, aliases=None, micros=0):
    return pl.pallas_call(
        kernel,
        out_shape=outs,
        in_specs=specs or [WHOLE] * len(args),
        out_specs=jax.tree.map(lambda _: WHOLE, outs),
        scratch_shapes=scratch,
        name=name,
        input_output_aliases=aliases or {},
        cost_estimate=pl.CostEstimate(flops=int(micros * 1e9), bytes_accessed=0, transcendentals=0) if micros else None,
        compiler_params=pltpu.CompilerParams(vmem_limit_bytes=limit * 2**20),
    )(*args)


def partner(index, step, size):
    return (index + step) % size if size & (size - 1) else index ^ step


def swapped(block, axis, step):
    size = lax.axis_size(axis)
    return lax.ppermute(block, axis, [(i, partner(i, step, size)) for i in range(size)])


def shifted(block, axis, distance):
    size = lax.axis_size(axis)
    return lax.ppermute(block, axis, [((i - distance) % size, i) for i in range(size)])


def prepare(order_ref, q_ref, after, q_out, feature_ref):
    q_out[...] = q_ref[0]
    sources = lax.axis_size("cp")
    me = lax.axis_index("cp")
    block = feature_ref.shape[1] // (2 * sources)
    row = lax.broadcasted_iota(jnp.int32, (block, LANES), 0)
    lane = lax.broadcasted_iota(jnp.int32, (block, LANES), 1)
    for side in range(2):
        mine = order_ref[2 * me + side]
        for d in range(sources):
            source = lax.rem(me - d + sources, sources) if sources & (sources - 1) else me ^ d
            for half in range(2):
                other = order_ref[2 * source + half]
                column = jnp.where(other == mine, row, jnp.where(other > mine, block, -1))
                first = (2 * d + half) * block
                feature_ref[side, first:first + block, :] = jnp.where(lane == column, 1.0, 0.0).astype(BF16)


def attend(first_head, heads, sources, q_ref, feature_ref, *refs):
    pairs = refs[:sources]
    before, (ctx_ref, peak_ref, k_all, vt) = refs[sources:-4], refs[-4:]
    rows = q_ref.shape[0]
    block = rows // 2
    kv_local = pairs[0].shape[1] // (2 * DH)
    count = ctx_ref.shape[1] // DH
    tile = LANES // block
    scale = 1.0 / math.sqrt(DH)
    ahead = lax.rem(lax.broadcasted_iota(jnp.int32, (tile * block, LANES), 0), block)
    lane = lax.broadcasted_iota(jnp.int32, (tile * block, LANES), 1)
    blocked = jnp.where((lane > ahead) & (lane <= block), MASKED, 0.0).astype(BF16)
    if before:
        peak_ref[:, :first_head] = before[0][...]
    vt[kv_local * DH:, :] = jnp.ones((vt.shape[0] - kv_local * DH, vt.shape[1]), BF16)
    for side in range(2):
        k_all[side, :, kv_local * DH:] = feature_ref[side]
    for d in range(sources):
        part = slice(d * rows, (d + 1) * rows)
        for side in range(2):
            k_all[side, part, :kv_local * DH] = pairs[d][:, :kv_local * DH]
        vt[:kv_local * DH, part] = pairs[d][:, kv_local * DH:].astype(F32).T.astype(BF16)

    def scores(i, side):
        tokens = slice(side * block, (side + 1) * block)
        places = [slice((first_head + i + j) * DH, (first_head + i + j + 1) * DH) for j in range(tile)]
        q = jnp.concatenate([q_ref[tokens, place] for place in places], axis=0)
        q = jnp.concatenate([q, blocked], axis=1)
        g = (first_head + i) // (heads // kv_local)
        if kv_local == 1:
            k = k_all[side]
        else:
            k = jnp.concatenate([k_all[side, :, g * DH:(g + 1) * DH], k_all[side, :, kv_local * DH:]], axis=1)
        return lax.dot_general(k, q, (((1,), (1,)), ((), ())), preferred_element_type=F32)

    def context(i, side, s):
        g = (first_head + i) // (heads // kv_local)
        m = jnp.max(s, axis=0, keepdims=True)
        p = jnp.exp2((s - m) * (scale * LOG2E)).astype(BF16)
        if kv_local == 1:
            v = vt[...]
        else:
            v = jnp.concatenate([vt[g * DH:(g + 1) * DH, :], vt[kv_local * DH:, :]], axis=0)
        return m, jnp.dot(v, p, preferred_element_type=F32)

    def store(i, side, o):
        turned = (o[:DH, :] * (1.0 / o[DH:DH + 1, :])).astype(BF16).T
        for j in range(tile):
            ctx_ref[side * block:(side + 1) * block, (i + j) * DH:(i + j + 1) * DH] = turned[j * block:(j + 1) * block, :]

    steps = [(i, side) for i in range(0, count, tile) for side in range(2)]
    peaks = {}
    waiting, unstored = scores(*steps[0]), None
    for n, (i, side) in enumerate(steps):
        s = waiting
        if n + 1 < len(steps):
            waiting = scores(*steps[n + 1])
        m, o = context(i, side, s)
        if unstored:
            store(*unstored)
        unstored = (i, side, o)
        peaks[i] = jnp.maximum(peaks[i], m) if side else m
    store(*unstored)
    for i, peak in peaks.items():
        for j in range(tile):
            h = first_head + i + j
            one = jnp.max(peak[:, j * block:(j + 1) * block], axis=1, keepdims=True)
            peak_ref[:, h:h + 1] = one * scale


def weigh(w_ref, gain_ref, after, out_ref):
    features, columns = w_ref.shape
    for f in range(0, features, LANES):
        gain = jnp.broadcast_to(gain_ref[:, f:f + LANES].astype(F32), (LANES, LANES)).T
        for c in range(0, columns, LANES):
            out_ref[f:f + LANES, c:c + LANES] = (w_ref[f:f + LANES, c:c + LANES].astype(F32) * gain).astype(BF16)


def square_sums(ctx_ref):
    total = None
    for c in range(0, ctx_ref.shape[1], LANES):
        wide = ctx_ref[:, c:c + LANES].astype(F32)
        total = wide * wide if total is None else total + wide * wide
    return jnp.broadcast_to(jnp.sum(total, axis=1, keepdims=True), total.shape)


def project_first(ctx_ref, w_ref, peak_ref, peak_got, sum_ref, square_ref, peak_out):
    peak_out[...] = jnp.maximum(peak_ref[...], peak_got[...])
    square_ref[...] = square_sums(ctx_ref)
    sum_ref[...] = jnp.dot(ctx_ref[...], w_ref[:ctx_ref.shape[1], :], preferred_element_type=F32)


def project_last(ctx_ref, w_ref, sum_ref, square_ref, give_ref, keep_ref):
    rows, width = ctx_ref.shape
    start = w_ref.shape[0] - width
    squares = square_ref[...] + square_sums(ctx_ref)
    lanes = squares.T[:SQUARE_ROWS, :]
    first = lanes.astype(BF16)
    rest = (lanes - first.astype(F32)).astype(BF16)
    groups, cols = give_ref.shape[0], give_ref.shape[2]
    core = lax.rem(lax.axis_index("tp"), 2)
    for ref, side in ((give_ref, 1 - core), (keep_ref, core)):
        for y in range(groups):
            at = pl.ds(pl.multiple_of((2 * y + side) * cols, cols), cols)
            part = sum_ref[:, at] + jnp.dot(ctx_ref[...], w_ref[start:, at], preferred_element_type=F32)
            ref[y, :rows, :] = part.astype(BF16)
            ref[y, rows:, :rows] = first
            ref[y, rows:, rows:2 * rows] = rest
            if cols > 2 * rows:
                ref[y, rows:, 2 * rows:] = jnp.zeros((SQUARE_ROWS, cols - 2 * rows), BF16)


def merge(keep_ref, got_ref, *give_refs):
    groups = keep_ref.shape[0]
    mine = lax.axis_index("tp") // 2
    for step, ref in enumerate(give_refs):
        y = lax.rem(mine + step, groups)
        total = keep_ref[y].astype(F32) + got_ref[y].astype(F32)
        ref[...] = total.astype(ref.dtype)


def finish(features, keep_ref, *refs):
    out_ref = refs[-1]
    rows = out_ref.shape[0]
    total = keep_ref[...]
    for ref in refs[:-1]:
        total = total + ref[...].astype(F32)
    squares = total[rows:rows + 8, :rows] + total[rows:rows + 8, rows:2 * rows]
    inverse = lax.rsqrt(squares / features + 1e-05)
    column = jnp.broadcast_to(inverse[:1, :], (rows, rows)).T[:, :1]
    out_ref[...] = (total[:rows, :] * column).astype(BF16)


def on_device(queries, key_vectors, value_vectors, block_order, norm_gain, kv_weight):
    rows, width = queries.shape[1:]
    heads = width // DH
    peers = lax.axis_size("tp")
    sources = lax.axis_size("cp")
    kv_width = key_vectors.shape[2]
    columns = kv_weight.shape[2]
    out_cols = columns // peers
    shape = jax.ShapeDtypeStruct
    steps = [2**i for i in range((sources - 1).bit_length())]

    pair = jnp.concatenate([key_vectors[0], value_vectors[0]], axis=1)
    pairs = [pair] + [swapped(pair, "cp", d) for d in range(1, sources)]
    q, features = call(
        prepare,
        (shape((rows, width), BF16), shape((2, sources * rows, LANES), BF16)),
        (block_order, queries, pair),
        [SCALARS, WHOLE, OUTSIDE],
        name="prepare",
        micros=1,
    )
    part_heads = heads // CHUNKS
    handed, peaks = [], []
    for c in range(CHUNKS):
        context, peak = call(
            functools.partial(attend, c * part_heads, heads, sources),
            (shape((rows, part_heads * DH), BF16), shape((1, (c + 1) * part_heads), F32)),
            (q, features, *pairs, *peaks[-1:]),
            scratch=[
                pltpu.VMEM((2, sources * rows, kv_width + LANES), BF16),
                pltpu.VMEM((kv_width + 16, sources * rows), BF16),
            ],
            limit=24,
            name="attend",
            micros=1.5,
        )
        handed.append(shifted(context, "pp", 1))
        peaks.append(peak)
    w = call(
        weigh,
        shape((width, columns), BF16),
        (kv_weight[0], norm_gain, context),
        [WHOLE, WHOLE, OUTSIDE],
        name="weigh",
        micros=2,
    )
    peak = peaks[-1]
    for step in steps[:-1]:
        peak = jnp.maximum(peak, swapped(peak, "cp", step))
    total, squares, max_logits = call(
        project_first,
        (shape((rows, columns), F32), shape((rows, LANES), F32), shape((1, heads), F32)),
        (handed[0], w, peak, swapped(peak, "cp", steps[-1])),
        name="project_first",
        micros=0.7,
    )
    slab = shape((peers // 2, rows + SQUARE_ROWS, out_cols), BF16)
    give, keep = call(
        project_last, (slab, slab), (handed[1], w, total, squares), name="project_last", micros=0.5
    )
    got = lax.ppermute(give, "tp", [(i, i ^ 1) for i in range(peers)])
    slab = (rows + SQUARE_ROWS, out_cols)
    mine, *others = call(
        merge,
        [shape(slab, F32)] + [shape(slab, BF16)] * (peers // 2 - 1),
        (keep, got),
        name="merge",
    )
    others = [
        lax.ppermute(block, "tp", [(i, (i + 2 * (step + 1)) % peers) for i in range(peers)])
        for step, block in enumerate(others)
    ]
    kv_next = call(
        functools.partial(finish, width * peers), shape((rows, out_cols), BF16), (mine, *others), name="finish"
    )
    return (max_logits, kv_next[None])


def solution(mesh):
    return jax.shard_map(
        on_device,
        mesh=mesh,
        in_specs=(
            P("pp", "cp", "tp"),
            P("pp", "cp", "tp"),
            P("pp", "cp", "tp"),
            P(),
            P("pp", "tp"),
            P("pp", "tp", None),
        ),
        out_specs=(P("pp", "tp"), P("pp", "cp", "tp")),
        check_vma=False,
    )
```

```python
import functools
import math

import jax
import jax.numpy as jnp
from jax import lax
from jax.experimental import pallas as pl
from jax.experimental.pallas import tpu as pltpu
from jax.sharding import PartitionSpec as P

DH = 128
LANES = 128
CHUNKS = 2
SQUARE_ROWS = 16
MASKED = -1e30
F32 = jnp.float32
BF16 = jnp.bfloat16
WHOLE = pl.BlockSpec(memory_space=pltpu.VMEM)
OUTSIDE = pl.BlockSpec(memory_space=pl.ANY)
SCALARS = pl.BlockSpec(memory_space=pltpu.SMEM)


def call(kernel, outs, args, specs=None, scratch=(), limit=16, name=None, aliases=None, micros=0):
    return pl.pallas_call(
        kernel,
        out_shape=outs,
        in_specs=specs or [WHOLE] * len(args),
        out_specs=jax.tree.map(lambda _: WHOLE, outs),
        scratch_shapes=scratch,
        name=name,
        input_output_aliases=aliases or {},
        cost_estimate=pl.CostEstimate(flops=int(micros * 1e9), bytes_accessed=0, transcendentals=0) if micros else None,
        compiler_params=pltpu.CompilerParams(vmem_limit_bytes=limit * 2**20),
    )(*args)


def partner(index, step, size):
    return (index + step) % size if size & (size - 1) else index ^ step


def swapped(block, axis, step):
    size = lax.axis_size(axis)
    return lax.ppermute(block, axis, [(i, partner(i, step, size)) for i in range(size)])


def shifted(block, axis, distance):
    size = lax.axis_size(axis)
    return lax.ppermute(block, axis, [((i - distance) % size, i) for i in range(size)])


def source_of(d, me, sources):
    return lax.rem(me - d + sources, sources) if sources & (sources - 1) else me ^ d


def fill_bias(order_ref, bias, distances):
    sources = lax.axis_size("cp")
    me = lax.axis_index("cp")
    rows = bias.shape[1]
    block = rows // 2
    lane = lax.broadcasted_iota(jnp.int32, (1, rows), 1)
    q_block = jnp.where(lane < block, order_ref[2 * me], order_ref[2 * me + 1])
    q_pos = q_block * block + lax.rem(lane, block)
    for n, d in enumerate(distances):
        source = source_of(d, me, sources)
        for half in range(2):
            first = n * rows + half * block
            k_pos = order_ref[2 * source + half] * block + lax.broadcasted_iota(jnp.int32, (block, 1), 0)
            bias[first:first + block, :] = jnp.where(k_pos <= q_pos, 0.0, MASKED)


def gather_pairs(pairs, k_all, vt):
    kv_width = k_all.shape[1]
    for n, pair in enumerate(pairs):
        rows = pair.shape[0]
        part = slice(n * rows, (n + 1) * rows)
        k_all[part, :] = pair[:, :kv_width]
        vt[:, part] = pair[:, kv_width:].astype(F32).T.astype(BF16)


def scores_of(h, heads, q_ref, k_all, bias):
    g = h // (heads * DH // k_all.shape[1])
    q = q_ref[0, :, h * DH:(h + 1) * DH]
    s = lax.dot_general(
        k_all[:, g * DH:(g + 1) * DH], q, (((1,), (1,)), ((), ())), preferred_element_type=F32
    )
    return s * (1.0 / math.sqrt(DH)) + bias[...]


def values_of(h, heads, vt, p):
    g = h // (heads * DH // vt.shape[0])
    return jnp.dot(vt[g * DH:(g + 1) * DH, :], p.astype(BF16), preferred_element_type=F32)


def attend_near(distances, order_ref, q_ref, *refs):
    pairs, (o_ref, m_ref, l_ref, bias, k_all, vt) = refs[:-6], refs[-6:]
    heads = q_ref.shape[2] // DH
    fill_bias(order_ref, bias, distances)
    gather_pairs(pairs, k_all, vt)
    for h in range(heads):
        s = scores_of(h, heads, q_ref, k_all, bias)
        m = jnp.max(s, axis=0, keepdims=True)
        p = jnp.exp(s - m)
        m_ref[h:h + 1, :] = m
        l_ref[h:h + 1, :] = jnp.sum(p, axis=0, keepdims=True)
        o_ref[h * DH:(h + 1) * DH, :] = values_of(h, heads, vt, p)


def attend_far(first_head, distances, order_ref, q_ref, o_ref, m_ref, l_ref, *refs):
    pairs, refs = refs[:len(distances)], refs[len(distances):]
    before, (ctx_ref, peak_ref, bias, k_all, vt) = refs[:-5], refs[-5:]
    heads = q_ref.shape[2] // DH
    fill_bias(order_ref, bias, distances)
    gather_pairs(pairs, k_all, vt)
    if before:
        peak_ref[:, :first_head] = before[0][...]
    for i in range(ctx_ref.shape[1] // DH):
        h = first_head + i
        s = scores_of(h, heads, q_ref, k_all, bias)
        m_near = m_ref[h:h + 1, :]
        m = jnp.maximum(m_near, jnp.max(s, axis=0, keepdims=True))
        p = jnp.exp(s - m)
        shrink = jnp.exp(m_near - m)
        total = l_ref[h:h + 1, :] * shrink + jnp.sum(p, axis=0, keepdims=True)
        inverse = 1.0 / total
        o = o_ref[h * DH:(h + 1) * DH, :] * (shrink * inverse) + values_of(h, heads, vt, p) * inverse
        ctx_ref[:, i * DH:(i + 1) * DH] = o.T.astype(BF16)
        peak_ref[:, h:h + 1] = jnp.max(m, axis=1, keepdims=True)


def weigh(w_ref, gain_ref, after, out_ref):
    features, columns = w_ref.shape
    for f in range(0, features, LANES):
        gain = jnp.broadcast_to(gain_ref[:, f:f + LANES].astype(F32), (LANES, LANES)).T
        for c in range(0, columns, LANES):
            out_ref[f:f + LANES, c:c + LANES] = (w_ref[f:f + LANES, c:c + LANES].astype(F32) * gain).astype(BF16)


def square_sums(ctx_ref):
    total = None
    for c in range(0, ctx_ref.shape[1], LANES):
        wide = ctx_ref[:, c:c + LANES].astype(F32)
        total = wide * wide if total is None else total + wide * wide
    return jnp.broadcast_to(jnp.sum(total, axis=1, keepdims=True), total.shape)


def larger(left_ref, right_ref, after, out_ref):
    out_ref[...] = jnp.maximum(left_ref[...], right_ref[...])


def project_first(ctx_ref, w_ref, sum_ref, square_ref):
    square_ref[...] = square_sums(ctx_ref)
    sum_ref[...] = jnp.dot(ctx_ref[...], w_ref[:ctx_ref.shape[1], :], preferred_element_type=F32)


def project_last(ctx_ref, w_ref, sum_ref, square_ref, peak_ref, peak_got, give_ref, keep_ref, peak_out):
    peak_out[...] = jnp.maximum(peak_ref[...], peak_got[...])
    rows, width = ctx_ref.shape
    start = w_ref.shape[0] - width
    squares = square_ref[...] + square_sums(ctx_ref)
    lanes = squares.T[:SQUARE_ROWS, :]
    first = lanes.astype(BF16)
    rest = (lanes - first.astype(F32)).astype(BF16)
    groups, cols = give_ref.shape[0], give_ref.shape[2]
    core = lax.rem(lax.axis_index("tp"), 2)
    for ref, side in ((give_ref, 1 - core), (keep_ref, core)):
        for y in range(groups):
            at = pl.ds(pl.multiple_of((2 * y + side) * cols, cols), cols)
            part = sum_ref[:, at] + jnp.dot(ctx_ref[...], w_ref[start:, at], preferred_element_type=F32)
            ref[y, :rows, :] = part.astype(BF16)
            ref[y, rows:, :rows] = first
            ref[y, rows:, rows:2 * rows] = rest
            if cols > 2 * rows:
                ref[y, rows:, 2 * rows:] = jnp.zeros((SQUARE_ROWS, cols - 2 * rows), BF16)


def merge(keep_ref, got_ref, *give_refs):
    groups = keep_ref.shape[0]
    mine = lax.axis_index("tp") // 2
    for step, ref in enumerate(give_refs):
        y = lax.rem(mine + step, groups)
        total = keep_ref[y].astype(F32) + got_ref[y].astype(F32)
        ref[...] = total.astype(ref.dtype)


def finish(features, keep_ref, *refs):
    out_ref = refs[-1]
    rows = out_ref.shape[0]
    total = keep_ref[...]
    for ref in refs[:-1]:
        total = total + ref[...].astype(F32)
    squares = total[rows:rows + 8, :rows] + total[rows:rows + 8, rows:2 * rows]
    inverse = lax.rsqrt(squares / features + 1e-05)
    column = jnp.broadcast_to(inverse[:1, :], (rows, rows)).T[:, :1]
    out_ref[...] = (total[:rows, :] * column).astype(BF16)


def on_device(queries, key_vectors, value_vectors, block_order, norm_gain, kv_weight):
    rows, width = queries.shape[1:]
    heads = width // DH
    peers = lax.axis_size("tp")
    sources = lax.axis_size("cp")
    kv_width = key_vectors.shape[2]
    columns = kv_weight.shape[2]
    out_cols = columns // peers
    shape = jax.ShapeDtypeStruct
    steps = [2**i for i in range((sources - 1).bit_length())]

    pair = jnp.concatenate([key_vectors[0], value_vectors[0]], axis=1)
    half = max(1, sources // 2)
    moved = {d: swapped(pair, "cp", d) for d in [*range(half, sources), *range(1, half)]}
    near, far = list(range(half)), list(range(half, sources))
    pairs = [pair] + [moved[d] for d in range(1, sources)]

    def scratch(distances):
        keys = len(distances) * rows
        return [pltpu.VMEM((keys, rows), F32), pltpu.VMEM((keys, kv_width), BF16), pltpu.VMEM((kv_width, keys), BF16)]

    state = call(
        functools.partial(attend_near, near),
        (shape((width, rows), F32), shape((heads, rows), F32), shape((heads, rows), F32)),
        (block_order, queries, *pairs[:half]),
        [SCALARS] + [WHOLE] * (1 + half),
        scratch=scratch(near),
        limit=24,
        name="attend_near",
        micros=1.5,
    )
    part_heads = heads // CHUNKS
    handed, peaks = [], []
    for c in range(CHUNKS):
        args = (block_order, queries, *state, *pairs[half:], *peaks[-1:])
        context, peak = call(
            functools.partial(attend_far, c * part_heads, far),
            (shape((rows, part_heads * DH), BF16), shape((1, (c + 1) * part_heads), F32)),
            args,
            [SCALARS] + [WHOLE] * (len(args) - 1),
            scratch=scratch(far),
            limit=24,
            name="attend_far",
            micros=0.9,
        )
        handed.append(shifted(context, "pp", 1))
        peaks.append(peak)
    w = call(
        weigh,
        shape((width, columns), BF16),
        (kv_weight[0], norm_gain, context),
        [WHOLE, WHOLE, OUTSIDE],
        name="weigh",
        micros=2,
    )
    peak = peaks[-1]
    for step in steps[:-1]:
        peak = call(
            larger, shape((1, heads), F32), (peak, swapped(peak, "cp", step), w), [WHOLE, WHOLE, OUTSIDE], name="larger"
        )
    total, squares = call(
        project_first,
        (shape((rows, columns), F32), shape((rows, LANES), F32)),
        (handed[0], w),
        name="project_first",
        micros=0.8,
    )
    slab = shape((peers // 2, rows + SQUARE_ROWS, out_cols), BF16)
    give, keep, max_logits = call(
        project_last,
        (slab, slab, shape((1, heads), F32)),
        (handed[1], w, total, squares, peak, swapped(peak, "cp", steps[-1])),
        name="project_last",
        micros=0.5,
    )
    got = lax.ppermute(give, "tp", [(i, i ^ 1) for i in range(peers)])
    slab = (rows + SQUARE_ROWS, out_cols)
    mine, *others = call(
        merge,
        [shape(slab, F32)] + [shape(slab, BF16)] * (peers // 2 - 1),
        (keep, got),
        name="merge",
    )
    others = [
        lax.ppermute(block, "tp", [(i, (i + 2 * (step + 1)) % peers) for i in range(peers)])
        for step, block in enumerate(others)
    ]
    kv_next = call(
        functools.partial(finish, width * peers), shape((rows, out_cols), BF16), (mine, *others), name="finish"
    )
    return (max_logits, kv_next[None])


def solution(mesh):
    return jax.shard_map(
        on_device,
        mesh=mesh,
        in_specs=(
            P("pp", "cp", "tp"),
            P("pp", "cp", "tp"),
            P("pp", "cp", "tp"),
            P(),
            P("pp", "tp"),
            P("pp", "tp", None),
        ),
        out_specs=(P("pp", "tp"), P("pp", "cp", "tp")),
        check_vma=False,
    )
```

```python
import functools
import math

import jax
import jax.numpy as jnp
from jax import lax
from jax.experimental import pallas as pl
from jax.experimental.pallas import tpu as pltpu
from jax.sharding import PartitionSpec as P

DH = 128
LANES = 128
SQUARE_ROWS = 16
MASKED = -(2.0**100)
LOG2E = math.log2(math.e)
F32 = jnp.float32
BF16 = jnp.bfloat16
WHOLE = pl.BlockSpec(memory_space=pltpu.VMEM)
OUTSIDE = pl.BlockSpec(memory_space=pl.ANY)
SCALARS = pl.BlockSpec(memory_space=pltpu.SMEM)


def call(kernel, outs, args, specs=None, scratch=(), limit=16, name=None, aliases=None, micros=0):
    return pl.pallas_call(
        kernel,
        out_shape=outs,
        in_specs=specs or [WHOLE] * len(args),
        out_specs=jax.tree.map(lambda _: WHOLE, outs),
        scratch_shapes=scratch,
        name=name,
        input_output_aliases=aliases or {},
        cost_estimate=pl.CostEstimate(flops=int(micros * 1e9), bytes_accessed=0, transcendentals=0) if micros else None,
        compiler_params=pltpu.CompilerParams(vmem_limit_bytes=limit * 2**20),
    )(*args)


def partner(index, step, size):
    return (index + step) % size if size & (size - 1) else index ^ step


def swapped(block, axis, step):
    size = lax.axis_size(axis)
    return lax.ppermute(block, axis, [(i, partner(i, step, size)) for i in range(size)])


def shifted(block, axis, distance):
    size = lax.axis_size(axis)
    return lax.ppermute(block, axis, [((i - distance) % size, i) for i in range(size)])


def returned(block, step):
    sections, sources = lax.axis_size("pp"), lax.axis_size("cp")
    route = [
        (s * sources + c, (s - 1) % sections * sources + partner(c, step, sources))
        for s in range(sections)
        for c in range(sources)
    ]
    return lax.ppermute(block, ("pp", "cp"), route)


def bind_kernel(block_ref, after, out_ref):
    out_ref[...] = block_ref[...]


def bind(block, after):
    return call(
        bind_kernel, jax.ShapeDtypeStruct(block.shape, block.dtype), (block, after), [WHOLE, OUTSIDE], name="bind"
    )


def source_of(d, me, sources):
    return lax.rem(me - d + sources, sources) if sources & (sources - 1) else me ^ d


def take(first, q_ref, after, part_ref):
    part_ref[...] = q_ref[0, :, first:first + part_ref.shape[1]]


def prepare(order_ref, after, feature_ref):
    sources = lax.axis_size("cp")
    me = lax.axis_index("cp")
    rows = feature_ref.shape[2] // sources
    block = rows // 2
    feature = lax.broadcasted_iota(jnp.int32, (LANES, rows), 0)
    key = lax.broadcasted_iota(jnp.int32, (LANES, rows), 1)
    place = lax.rem(key, block)
    for side in range(2):
        mine = order_ref[2 * me + side]
        for d in range(sources):
            source = source_of(d, me, sources)
            other = jnp.where(key < block, order_ref[2 * source], order_ref[2 * source + 1])
            chosen = jnp.where(other == mine, place, jnp.where(other > mine, block, -1))
            feature_ref[side, :, d * rows:(d + 1) * rows] = jnp.where(feature == chosen, 1.0, 0.0).astype(BF16)


def attend(first_head, heads, sources, q_ref, feature_ref, *refs):
    pairs = refs[:sources]
    before, (ctx_ref, peak_ref, kt, v_all) = refs[sources:-4], refs[-4:]
    rows, width = q_ref.shape
    keys = v_all.shape[0]
    block = rows // 2
    kv_local = pairs[0].shape[1] // (2 * DH)
    group = heads // kv_local
    count = width // DH
    scale = 1.0 / math.sqrt(DH)
    if before:
        peak_ref[:, :first_head] = before[0][...]
    v_all[:, DH:] = jnp.ones((keys, DH), BF16)
    for side in range(2):
        kt[side, DH:, :] = feature_ref[side]
    held = None
    together = max(1, min(count, 12 * 512 // keys))
    peaks = {}
    spans = []
    for i in range(0, count, together):
        while i < count and (not spans or spans[-1][1] < min(i + together, count)):
            start = spans[-1][1] if spans else 0
            limit = ((first_head + start) // group + 1) * group - first_head
            spans.append((start, min(start + together, count, limit)))
    for start, stop in spans:
        g = (first_head + start) // group
        if g != held:
            held = g
            for d, pair in enumerate(pairs):
                part = slice(d * rows, (d + 1) * rows)
                turned = pair[:, g * DH:(g + 1) * DH].astype(F32).T.astype(BF16)
                kt[0, :DH, part] = turned
                kt[1, :DH, part] = turned
                v_all[part, :DH] = pair[:, (kv_local + g) * DH:(kv_local + g + 1) * DH]
        n = stop - start
        token = lax.rem(lax.broadcasted_iota(jnp.int32, (n * block, LANES), 0), block)
        lane = lax.broadcasted_iota(jnp.int32, (n * block, LANES), 1)
        blocked = jnp.where((lane > token) & (lane <= block), MASKED, 0.0).astype(BF16)
        for side in range(2):
            tokens = slice(side * block, (side + 1) * block)
            q = jnp.concatenate([q_ref[tokens, h * DH:(h + 1) * DH] for h in range(start, stop)], axis=0)
            q = jnp.concatenate([q, blocked], axis=1)
            s = jnp.dot(q, kt[side], preferred_element_type=F32)
            m = jnp.max(s, axis=1, keepdims=True)
            p = jnp.exp2((s - m) * (scale * LOG2E)).astype(BF16)
            o = jnp.dot(p, v_all[...], preferred_element_type=F32)
            o = (o[:, :DH] * (1.0 / o[:, DH:])).astype(BF16)
            for j in range(n):
                lines = slice(j * block, (j + 1) * block)
                ctx_ref[tokens, (start + j) * DH:(start + j + 1) * DH] = o[lines, :]
                one = jnp.max(m[lines, :], axis=0, keepdims=True)
                peaks[start + j] = jnp.maximum(peaks[start + j], one) if side else one
    for i, peak in peaks.items():
        peak_ref[:, first_head + i:first_head + i + 1] = peak * scale


def weigh(w_ref, gain_ref, after, out_ref):
    features, columns = w_ref.shape
    for f in range(0, features, LANES):
        gain = jnp.broadcast_to(gain_ref[:, f:f + LANES].astype(F32), (LANES, LANES)).T
        for c in range(0, columns, LANES):
            out_ref[f:f + LANES, c:c + LANES] = (w_ref[f:f + LANES, c:c + LANES].astype(F32) * gain).astype(BF16)


def square_sums(ctx_ref):
    total = None
    for c in range(0, ctx_ref.shape[1], LANES):
        wide = ctx_ref[:, c:c + LANES].astype(F32)
        total = wide * wide if total is None else total + wide * wide
    return jnp.broadcast_to(jnp.sum(total, axis=1, keepdims=True), total.shape)


def project_first(ctx_ref, w_ref, sum_ref, square_ref):
    square_ref[...] = square_sums(ctx_ref)
    sum_ref[...] = jnp.dot(ctx_ref[...], w_ref[:ctx_ref.shape[1], :], preferred_element_type=F32)


def project_last(ctx_ref, w_ref, sum_ref, square_ref, give_ref, keep_ref):
    rows, width = ctx_ref.shape
    start = w_ref.shape[0] - width
    squares = square_ref[...] + square_sums(ctx_ref)
    lanes = squares.T[:SQUARE_ROWS, :]
    first = lanes.astype(BF16)
    rest = (lanes - first.astype(F32)).astype(BF16)
    groups, cols = give_ref.shape[0], give_ref.shape[2]
    core = lax.rem(lax.axis_index("tp"), 2)
    for ref, side in ((give_ref, 1 - core), (keep_ref, core)):
        for y in range(groups):
            at = pl.ds(pl.multiple_of((2 * y + side) * cols, cols), cols)
            part = sum_ref[:, at] + jnp.dot(ctx_ref[...], w_ref[start:, at], preferred_element_type=F32)
            ref[y, :rows, :] = part.astype(BF16)
            ref[y, rows:, :rows] = first
            ref[y, rows:, rows:2 * rows] = rest
            if cols > 2 * rows:
                ref[y, rows:, 2 * rows:] = jnp.zeros((SQUARE_ROWS, cols - 2 * rows), BF16)


def merge(keep_ref, got_ref, peak_ref, peak_got, peak_out, *give_refs):
    peak_out[...] = jnp.maximum(peak_ref[...], peak_got[...])
    groups = keep_ref.shape[0]
    mine = lax.axis_index("tp") // 2
    for step, ref in enumerate(give_refs):
        y = lax.rem(mine + step, groups)
        total = keep_ref[y].astype(F32) + got_ref[y].astype(F32)
        ref[...] = total.astype(ref.dtype)


def finish(features, peak_ref, peak_got, keep_ref, *refs):
    peak_out, out_ref = refs[-2:]
    peak_out[...] = jnp.maximum(peak_ref[...], peak_got[...])
    rows = out_ref.shape[0]
    total = keep_ref[...]
    for ref in refs[:-2]:
        total = total + ref[...].astype(F32)
    squares = total[rows:rows + 8, :rows] + total[rows:rows + 8, rows:2 * rows]
    inverse = lax.rsqrt(squares / features + 1e-05)
    column = jnp.broadcast_to(inverse[:1, :], (rows, rows)).T[:, :1]
    out_ref[...] = (total[:rows, :] * column).astype(BF16)


def on_device(queries, key_vectors, value_vectors, block_order, norm_gain, kv_weight):
    rows, width = queries.shape[1:]
    heads = width // DH
    peers = lax.axis_size("tp")
    sources = lax.axis_size("cp")
    kv_width = key_vectors.shape[2]
    columns = kv_weight.shape[2]
    out_cols = columns // peers
    shape = jax.ShapeDtypeStruct
    steps = [2**i for i in range((sources - 1).bit_length())]

    pair_here = jnp.concatenate([key_vectors[0], value_vectors[0]], axis=1)
    pair = shifted(pair_here, "pp", 1)
    cut = heads * 3 // 4
    counts = [cut, heads - cut]
    starts = [0, cut]
    crossed = []
    for start, count, after in zip(starts, counts, [pair_here, pair]):
        part = call(
            functools.partial(take, start * DH),
            shape((rows, count * DH), BF16),
            (queries, after),
            [WHOLE, OUTSIDE],
            name="take",
            micros=3,
        )
        crossed.append(shifted(part, "pp", 1))
    moved = {d: swapped(pair, "cp", d) for d in reversed(range(1, sources))}
    pairs = [pair] + [moved[d] for d in range(1, sources)]
    features = call(
        prepare,
        shape((2, LANES, sources * rows), BF16),
        (block_order, pair),
        [SCALARS, OUTSIDE],
        name="prepare",
        micros=0.5,
    )
    contexts, peaks = [], []
    for start, count, part in zip(starts, counts, crossed):
        context, peak = call(
            functools.partial(attend, start, heads, sources),
            (shape((rows, count * DH), BF16), shape((1, start + count), F32)),
            (part, features, *pairs, *peaks[-1:]),
            scratch=[
                pltpu.VMEM((2, DH + LANES, sources * rows), BF16),
                pltpu.VMEM((sources * rows, 2 * DH), BF16),
            ],
            limit=32,
            name="attend",
            micros=count * 0.14,
        )
        contexts.append(context)
        peaks.append(peak)
        if start == 0:
            w = call(
                weigh,
                shape((width, columns), BF16),
                (kv_weight[0], norm_gain, context),
                [WHOLE, WHOLE, OUTSIDE],
                name="weigh",
                micros=1,
            )
            total, squares = call(
                project_first,
                (shape((rows, columns), F32), shape((rows, LANES), F32)),
                (context, w),
                name="project_first",
                micros=0.7,
            )
    slab = shape((peers // 2, rows + SQUARE_ROWS, out_cols), BF16)
    give, keep = call(
        project_last, (slab, slab), (contexts[-1], w, total, squares), name="project_last", micros=0.5
    )
    got = lax.ppermute(give, "tp", [(i, i ^ 1) for i in range(peers)])
    peak = bind(peaks[-1], give)
    slab = (rows + SQUARE_ROWS, out_cols)
    peak, mine, *others = call(
        merge,
        [shape((1, heads), F32), shape(slab, F32)] + [shape(slab, BF16)] * (peers // 2 - 1),
        (keep, got, shifted(peak, "pp", -1), returned(peak, steps[0])),
        name="merge",
    )
    for step in steps[1:-1]:
        peak = jnp.maximum(peak, swapped(peak, "cp", step))
    others = [
        lax.ppermute(block, "tp", [(i, (i + 2 * (step + 1)) % peers) for i in range(peers)])
        for step, block in enumerate(others)
    ]
    max_logits, kv_next = call(
        functools.partial(finish, width * peers),
        (shape((1, heads), F32), shape((rows, out_cols), BF16)),
        (peak, swapped(peak, "cp", steps[-1]), mine, *others),
        name="finish",
    )
    return (max_logits, kv_next[None])


def solution(mesh):
    return jax.shard_map(
        on_device,
        mesh=mesh,
        in_specs=(
            P("pp", "cp", "tp"),
            P("pp", "cp", "tp"),
            P("pp", "cp", "tp"),
            P(),
            P("pp", "tp"),
            P("pp", "tp", None),
        ),
        out_specs=(P("pp", "tp"), P("pp", "cp", "tp")),
        check_vma=False,
    )
```

```python
import functools
import math

import jax
import jax.numpy as jnp
from jax import lax
from jax.experimental import pallas as pl
from jax.experimental.pallas import tpu as pltpu
from jax.sharding import PartitionSpec as P

DH = 128
LANES = 128
SQUARE_ROWS = 16
MASKED = -(2.0**100)
LOG2E = math.log2(math.e)
F32 = jnp.float32
BF16 = jnp.bfloat16
WHOLE = pl.BlockSpec(memory_space=pltpu.VMEM)
OUTSIDE = pl.BlockSpec(memory_space=pl.ANY)
SCALARS = pl.BlockSpec(memory_space=pltpu.SMEM)


def call(kernel, outs, args, specs=None, scratch=(), limit=16, name=None, aliases=None, micros=0):
    return pl.pallas_call(
        kernel,
        out_shape=outs,
        in_specs=specs or [WHOLE] * len(args),
        out_specs=jax.tree.map(lambda _: WHOLE, outs),
        scratch_shapes=scratch,
        name=name,
        input_output_aliases=aliases or {},
        cost_estimate=pl.CostEstimate(flops=int(micros * 1e9), bytes_accessed=0, transcendentals=0) if micros else None,
        compiler_params=pltpu.CompilerParams(vmem_limit_bytes=limit * 2**20),
    )(*args)


def partner(index, step, size):
    return (index + step) % size if size & (size - 1) else index ^ step


def swapped(block, axis, step):
    size = lax.axis_size(axis)
    return lax.ppermute(block, axis, [(i, partner(i, step, size)) for i in range(size)])


def shifted(block, axis, distance):
    size = lax.axis_size(axis)
    return lax.ppermute(block, axis, [((i - distance) % size, i) for i in range(size)])


def returned(block, step):
    sections, sources = lax.axis_size("pp"), lax.axis_size("cp")
    route = [
        (s * sources + c, (s - 1) % sections * sources + partner(c, step, sources))
        for s in range(sections)
        for c in range(sources)
    ]
    return lax.ppermute(block, ("pp", "cp"), route)


def bind_kernel(block_ref, after, out_ref):
    out_ref[...] = block_ref[...]


def bind(block, after):
    return call(
        bind_kernel, jax.ShapeDtypeStruct(block.shape, block.dtype), (block, after), [WHOLE, OUTSIDE], name="bind"
    )


def source_of(d, me, sources):
    return lax.rem(me - d + sources, sources) if sources & (sources - 1) else me ^ d


def take(first, q_ref, after, part_ref):
    part_ref[...] = q_ref[0, :, first:first + part_ref.shape[1]]


def prepare(order_ref, after, feature_ref):
    sources = lax.axis_size("cp")
    me = lax.axis_index("cp")
    rows = feature_ref.shape[2] // sources
    block = rows // 2
    feature = lax.broadcasted_iota(jnp.int32, (LANES, rows), 0)
    key = lax.broadcasted_iota(jnp.int32, (LANES, rows), 1)
    place = lax.rem(key, block)
    for side in range(2):
        mine = order_ref[2 * me + side]
        for d in range(sources):
            source = source_of(d, me, sources)
            other = jnp.where(key < block, order_ref[2 * source], order_ref[2 * source + 1])
            chosen = jnp.where(other == mine, place, jnp.where(other > mine, block, -1))
            feature_ref[side, :, d * rows:(d + 1) * rows] = jnp.where(feature == chosen, 1.0, 0.0).astype(BF16)


def touch(block_ref, out_ref):
    out_ref[...] = jnp.zeros(out_ref.shape, F32)


def arrange(feature_ref, *refs):
    pairs, (kt_ref, v_ref) = refs[:-2], refs[-2:]
    rows = pairs[0].shape[0]
    for g in range(v_ref.shape[0]):
        v_ref[g, :, DH:] = jnp.ones((v_ref.shape[1], DH), BF16)
        for side in range(2):
            kt_ref[g, side, DH:, :] = feature_ref[side]
        for d, pair in enumerate(pairs):
            part = slice(d * rows, (d + 1) * rows)
            turned = pair[:, g * DH:(g + 1) * DH].astype(F32).T.astype(BF16)
            for side in range(2):
                kt_ref[g, side, :DH, part] = turned
            first = (v_ref.shape[0] + g) * DH
            v_ref[g, part, :DH] = pair[:, first:first + DH]


def attend(first_head, heads, q_ref, kt_ref, v_ref, *refs):
    before, (ctx_ref, peak_ref) = refs[:-2], refs[-2:]
    rows, width = q_ref.shape
    keys = v_ref.shape[1]
    block = rows // 2
    group = heads // v_ref.shape[0]
    count = width // DH
    scale = 1.0 / math.sqrt(DH)
    if before:
        peak_ref[:, :first_head] = before[0][...]
    together = max(1, min(count, 12 * 512 // keys))
    peaks = {}
    start = 0
    while start < count:
        g = (first_head + start) // group
        stop = min(start + together, count, (g + 1) * group - first_head)
        n = stop - start
        token = lax.rem(lax.broadcasted_iota(jnp.int32, (n * block, LANES), 0), block)
        lane = lax.broadcasted_iota(jnp.int32, (n * block, LANES), 1)
        blocked = jnp.where((lane > token) & (lane <= block), MASKED, 0.0).astype(BF16)
        for side in range(2):
            tokens = slice(side * block, (side + 1) * block)
            q = jnp.concatenate([q_ref[tokens, h * DH:(h + 1) * DH] for h in range(start, stop)], axis=0)
            q = jnp.concatenate([q, blocked], axis=1)
            s = jnp.dot(q, kt_ref[g, side], preferred_element_type=F32)
            m = jnp.max(s, axis=1, keepdims=True)
            p = jnp.exp2((s - m) * (scale * LOG2E)).astype(BF16)
            o = jnp.dot(p, v_ref[g], preferred_element_type=F32)
            o = (o[:, :DH] * (1.0 / o[:, DH:])).astype(BF16)
            for j in range(n):
                lines = slice(j * block, (j + 1) * block)
                ctx_ref[tokens, (start + j) * DH:(start + j + 1) * DH] = o[lines, :]
                one = jnp.max(m[lines, :], axis=0, keepdims=True)
                peaks[start + j] = jnp.maximum(peaks[start + j], one) if side else one
        start = stop
    for i, peak in peaks.items():
        peak_ref[:, first_head + i:first_head + i + 1] = peak * scale


def weigh(w_ref, gain_ref, after, out_ref):
    features, columns = w_ref.shape
    for f in range(0, features, LANES):
        gain = jnp.broadcast_to(gain_ref[:, f:f + LANES].astype(F32), (LANES, LANES)).T
        for c in range(0, columns, LANES):
            out_ref[f:f + LANES, c:c + LANES] = (w_ref[f:f + LANES, c:c + LANES].astype(F32) * gain).astype(BF16)


def square_sums(ctx_ref):
    total = None
    for c in range(0, ctx_ref.shape[1], LANES):
        wide = ctx_ref[:, c:c + LANES].astype(F32)
        total = wide * wide if total is None else total + wide * wide
    return jnp.broadcast_to(jnp.sum(total, axis=1, keepdims=True), total.shape)


def project_first(ctx_ref, w_ref, sum_ref, square_ref):
    square_ref[...] = square_sums(ctx_ref)
    sum_ref[...] = jnp.dot(ctx_ref[...], w_ref[:ctx_ref.shape[1], :], preferred_element_type=F32)


def project_last(ctx_ref, w_ref, sum_ref, square_ref, give_ref, keep_ref):
    rows, width = ctx_ref.shape
    start = w_ref.shape[0] - width
    squares = square_ref[...] + square_sums(ctx_ref)
    lanes = squares.T[:SQUARE_ROWS, :]
    first = lanes.astype(BF16)
    rest = (lanes - first.astype(F32)).astype(BF16)
    groups, cols = give_ref.shape[0], give_ref.shape[2]
    core = lax.rem(lax.axis_index("tp"), 2)
    for ref, side in ((give_ref, 1 - core), (keep_ref, core)):
        for y in range(groups):
            at = pl.ds(pl.multiple_of((2 * y + side) * cols, cols), cols)
            part = sum_ref[:, at] + jnp.dot(ctx_ref[...], w_ref[start:, at], preferred_element_type=F32)
            ref[y, :rows, :] = part.astype(BF16)
            ref[y, rows:, :rows] = first
            ref[y, rows:, rows:2 * rows] = rest
            if cols > 2 * rows:
                ref[y, rows:, 2 * rows:] = jnp.zeros((SQUARE_ROWS, cols - 2 * rows), BF16)


def merge(keep_ref, got_ref, peak_ref, peak_got, peak_out, *give_refs):
    peak_out[...] = jnp.maximum(peak_ref[...], peak_got[...])
    groups = keep_ref.shape[0]
    mine = lax.axis_index("tp") // 2
    for step, ref in enumerate(give_refs):
        y = lax.rem(mine + step, groups)
        total = keep_ref[y].astype(F32) + got_ref[y].astype(F32)
        ref[...] = total.astype(ref.dtype)


def finish(features, peak_ref, peak_got, keep_ref, *refs):
    peak_out, out_ref = refs[-2:]
    peak_out[...] = jnp.maximum(peak_ref[...], peak_got[...])
    rows = out_ref.shape[0]
    total = keep_ref[...]
    for ref in refs[:-2]:
        total = total + ref[...].astype(F32)
    squares = total[rows:rows + 8, :rows] + total[rows:rows + 8, rows:2 * rows]
    inverse = lax.rsqrt(squares / features + 1e-05)
    column = jnp.broadcast_to(inverse[:1, :], (rows, rows)).T[:, :1]
    out_ref[...] = (total[:rows, :] * column).astype(BF16)


def on_device(queries, key_vectors, value_vectors, block_order, norm_gain, kv_weight):
    rows, width = queries.shape[1:]
    heads = width // DH
    peers = lax.axis_size("tp")
    sources = lax.axis_size("cp")
    kv_width = key_vectors.shape[2]
    columns = kv_weight.shape[2]
    out_cols = columns // peers
    shape = jax.ShapeDtypeStruct
    steps = [2**i for i in range((sources - 1).bit_length())]

    pair_here = jnp.concatenate([key_vectors[0], value_vectors[0]], axis=1)
    pair = shifted(pair_here, "pp", 1)
    cut = heads * 3 // 4
    counts = [cut, heads - cut]
    starts = [0, cut]
    crossed = []

    def cross(start, count, after, micros):
        part = call(
            functools.partial(take, start * DH),
            shape((rows, count * DH), BF16),
            (queries, after),
            [WHOLE, OUTSIDE],
            name="take",
            micros=micros,
        )
        crossed.append(shifted(part, "pp", 1))

    mark = call(touch, shape((8, LANES), F32), (pair_here,), [OUTSIDE], name="touch", micros=3)
    cross(starts[0], counts[0], mark, 3)
    moved = {d: swapped(pair, "cp", d) for d in reversed(range(1, sources))}
    pairs = [pair] + [moved[d] for d in range(1, sources)]
    cross(starts[1], counts[1], moved[1], 0)
    features = call(
        prepare,
        shape((2, LANES, sources * rows), BF16),
        (block_order, pair),
        [SCALARS, OUTSIDE],
        name="prepare",
        micros=2,
    )
    kv_local = kv_width // DH
    kt, v_all = call(
        arrange,
        (shape((kv_local, 2, DH + LANES, sources * rows), BF16), shape((kv_local, sources * rows, 2 * DH), BF16)),
        (features, *pairs),
        name="arrange",
        micros=2,
    )
    w = call(
        weigh,
        shape((width, columns), BF16),
        (kv_weight[0], norm_gain, kt),
        [WHOLE, WHOLE, OUTSIDE],
        name="weigh",
        micros=1,
    )
    contexts, peaks = [], []
    for start, count, part in zip(starts, counts, crossed):
        context, peak = call(
            functools.partial(attend, start, heads),
            (shape((rows, count * DH), BF16), shape((1, start + count), F32)),
            (part, kt, v_all, *peaks[-1:]),
            limit=32,
            name="attend",
            micros=count * 0.12,
        )
        contexts.append(context)
        peaks.append(peak)
        if start == 0:
            total, squares = call(
                project_first,
                (shape((rows, columns), F32), shape((rows, LANES), F32)),
                (context, w),
                name="project_first",
                micros=0.7,
            )
    slab = shape((peers // 2, rows + SQUARE_ROWS, out_cols), BF16)
    give, keep = call(
        project_last, (slab, slab), (contexts[-1], w, total, squares), name="project_last", micros=0.5
    )
    got = lax.ppermute(give, "tp", [(i, i ^ 1) for i in range(peers)])
    peak = bind(peaks[-1], give)
    slab = (rows + SQUARE_ROWS, out_cols)
    peak, mine, *others = call(
        merge,
        [shape((1, heads), F32), shape(slab, F32)] + [shape(slab, BF16)] * (peers // 2 - 1),
        (keep, got, shifted(peak, "pp", -1), returned(peak, steps[0])),
        name="merge",
    )
    for step in steps[1:-1]:
        peak = jnp.maximum(peak, swapped(peak, "cp", step))
    others = [
        lax.ppermute(block, "tp", [(i, (i + 2 * (step + 1)) % peers) for i in range(peers)])
        for step, block in enumerate(others)
    ]
    max_logits, kv_next = call(
        functools.partial(finish, width * peers),
        (shape((1, heads), F32), shape((rows, out_cols), BF16)),
        (peak, swapped(peak, "cp", steps[-1]), mine, *others),
        name="finish",
    )
    return (max_logits, kv_next[None])


def solution(mesh):
    return jax.shard_map(
        on_device,
        mesh=mesh,
        in_specs=(
            P("pp", "cp", "tp"),
            P("pp", "cp", "tp"),
            P("pp", "cp", "tp"),
            P(),
            P("pp", "tp"),
            P("pp", "tp", None),
        ),
        out_specs=(P("pp", "tp"), P("pp", "cp", "tp")),
        check_vma=False,
    )
```

```python
import functools
import math

import jax
import jax.numpy as jnp
from jax import lax
from jax.experimental import pallas as pl
from jax.experimental.pallas import tpu as pltpu
from jax.sharding import PartitionSpec as P

DH = 128
LANES = 128
SQUARE_ROWS = 16
MASKED = -(2.0**100)
LOG2E = math.log2(math.e)
F32 = jnp.float32
BF16 = jnp.bfloat16
WHOLE = pl.BlockSpec(memory_space=pltpu.VMEM)
OUTSIDE = pl.BlockSpec(memory_space=pl.ANY)
SCALARS = pl.BlockSpec(memory_space=pltpu.SMEM)


def call(kernel, outs, args, specs=None, scratch=(), limit=16, name=None, aliases=None, micros=0):
    return pl.pallas_call(
        kernel,
        out_shape=outs,
        in_specs=specs or [WHOLE] * len(args),
        out_specs=jax.tree.map(lambda _: WHOLE, outs),
        scratch_shapes=scratch,
        name=name,
        input_output_aliases=aliases or {},
        cost_estimate=pl.CostEstimate(flops=int(micros * 1e9), bytes_accessed=0, transcendentals=0) if micros else None,
        compiler_params=pltpu.CompilerParams(vmem_limit_bytes=limit * 2**20),
    )(*args)


def partner(index, step, size):
    return (index + step) % size if size & (size - 1) else index ^ step


def swapped(block, axis, step):
    size = lax.axis_size(axis)
    return lax.ppermute(block, axis, [(i, partner(i, step, size)) for i in range(size)])


def shifted(block, axis, distance):
    size = lax.axis_size(axis)
    return lax.ppermute(block, axis, [((i - distance) % size, i) for i in range(size)])


def bind_kernel(block_ref, after, out_ref):
    out_ref[...] = block_ref[...]


def bind(block, after):
    return call(
        bind_kernel, jax.ShapeDtypeStruct(block.shape, block.dtype), (block, after), [WHOLE, OUTSIDE], name="bind"
    )


def source_of(d, me, sources):
    return lax.rem(me - d + sources, sources) if sources & (sources - 1) else me ^ d


def take(first, q_ref, after, part_ref):
    part_ref[...] = q_ref[0, :, first:first + part_ref.shape[1]]


def prepare(order_ref, after, feature_ref):
    sources = lax.axis_size("cp")
    me = lax.axis_index("cp")
    rows = feature_ref.shape[2] // sources
    block = rows // 2
    feature = lax.broadcasted_iota(jnp.int32, (LANES, rows), 0)
    key = lax.broadcasted_iota(jnp.int32, (LANES, rows), 1)
    place = lax.rem(key, block)
    for side in range(2):
        mine = order_ref[2 * me + side]
        for d in range(sources):
            source = source_of(d, me, sources)
            other = jnp.where(key < block, order_ref[2 * source], order_ref[2 * source + 1])
            chosen = jnp.where(other == mine, place, jnp.where(other > mine, block, -1))
            feature_ref[side, :, d * rows:(d + 1) * rows] = jnp.where(feature == chosen, 1.0, 0.0).astype(BF16)


def touch(block_ref, out_ref):
    out_ref[...] = jnp.zeros(out_ref.shape, F32)


def join(pair_ref, here_ref, out_ref):
    width = pair_ref.shape[1]
    out_ref[:, :width] = pair_ref[...]
    out_ref[:, width:] = here_ref[:, :width // 2]


def arrange(feature_ref, *refs):
    triples, (kt_ref, v_ref, own_ref) = refs[:-3], refs[-3:]
    rows = triples[0].shape[0]
    kv_local = v_ref.shape[0]
    for g in range(kv_local):
        v_ref[g, :, DH:] = jnp.ones((v_ref.shape[1], DH), BF16)
        for ref in (kt_ref, own_ref):
            for side in range(2):
                ref[g, side, DH:, :] = feature_ref[side]
        for d, triple in enumerate(triples):
            part = slice(d * rows, (d + 1) * rows)
            for ref, first in ((kt_ref, g * DH), (own_ref, (2 * kv_local + g) * DH)):
                turned = triple[:, first:first + DH].astype(F32).T.astype(BF16)
                for side in range(2):
                    ref[g, side, :DH, part] = turned
            first = (kv_local + g) * DH
            v_ref[g, part, :DH] = triple[:, first:first + DH]


def spans(first_head, count, group, together):
    start = 0
    while start < count:
        g = (first_head + start) // group
        stop = min(start + together, count, (g + 1) * group - first_head)
        yield g, start, stop
        start = stop


def stacked(q_ref, start, stop, side):
    block = q_ref.shape[0] // 2
    shape = ((stop - start) * block, LANES)
    token = lax.rem(lax.broadcasted_iota(jnp.int32, shape, 0), block)
    lane = lax.broadcasted_iota(jnp.int32, shape, 1)
    blocked = jnp.where((lane > token) & (lane <= block), MASKED, 0.0).astype(BF16)
    tokens = slice(side * block, (side + 1) * block)
    q = jnp.concatenate([q_ref[tokens, h * DH:(h + 1) * DH] for h in range(start, stop)], axis=0)
    return jnp.concatenate([q, blocked], axis=1)


def maxima(q_ref, own_ref, peak_ref):
    q_ref = q_ref.at[0]
    block = q_ref.shape[0] // 2
    heads = q_ref.shape[1] // DH
    keys = own_ref.shape[3]
    for g, start, stop in spans(0, heads, heads // own_ref.shape[0], max(1, 8 * 512 // keys)):
        tops = []
        for side in range(2):
            s = jnp.dot(stacked(q_ref, start, stop, side), own_ref[g, side], preferred_element_type=F32)
            top = s[:, :LANES]
            for c in range(LANES, keys, LANES):
                top = jnp.maximum(top, s[:, c:c + LANES])
            tops.append(top)
        top = jnp.maximum(*tops)
        for j in range(stop - start):
            one = jnp.max(top[j * block:(j + 1) * block, :], axis=0, keepdims=True)
            h = start + j
            peak_ref[:, h:h + 1] = jnp.max(one, axis=1, keepdims=True) * (1.0 / math.sqrt(DH))


def attend(first_head, heads, q_ref, kt_ref, v_ref, after, ctx_ref):
    rows, width = q_ref.shape
    keys = v_ref.shape[1]
    block = rows // 2
    count = width // DH
    scale = 1.0 / math.sqrt(DH)
    for g, start, stop in spans(first_head, count, heads // v_ref.shape[0], max(1, 12 * 512 // keys)):
        scores = [
            jnp.dot(stacked(q_ref, start, stop, side), kt_ref[g, side], preferred_element_type=F32) for side in range(2)
        ]
        probs = []
        for s in scores:
            m = jnp.max(s, axis=1, keepdims=True)
            probs.append(jnp.exp2((s - m) * (scale * LOG2E)).astype(BF16))
        for side in range(2):
            o = jnp.dot(probs[side], v_ref[g], preferred_element_type=F32)
            o = (o[:, :DH] * (1.0 / o[:, DH:])).astype(BF16)
            for j in range(stop - start):
                ctx_ref[side * block:(side + 1) * block, (start + j) * DH:(start + j + 1) * DH] = o[
                    j * block:(j + 1) * block, :
                ]


def weigh(w_ref, gain_ref, after, out_ref):
    features, columns = w_ref.shape
    for f in range(0, features, LANES):
        gain = jnp.broadcast_to(gain_ref[:, f:f + LANES].astype(F32), (LANES, LANES)).T
        for c in range(0, columns, LANES):
            out_ref[f:f + LANES, c:c + LANES] = (w_ref[f:f + LANES, c:c + LANES].astype(F32) * gain).astype(BF16)


def square_sums(ctx_ref):
    total = None
    for c in range(0, ctx_ref.shape[1], LANES):
        wide = ctx_ref[:, c:c + LANES].astype(F32)
        total = wide * wide if total is None else total + wide * wide
    return jnp.broadcast_to(jnp.sum(total, axis=1, keepdims=True), total.shape)


def project_first(ctx_ref, w_ref, sum_ref, square_ref):
    square_ref[...] = square_sums(ctx_ref)
    sum_ref[...] = jnp.dot(ctx_ref[...], w_ref[:ctx_ref.shape[1], :], preferred_element_type=F32)


def project_last(ctx_ref, w_ref, sum_ref, square_ref, give_ref, keep_ref):
    rows, width = ctx_ref.shape
    start = w_ref.shape[0] - width
    squares = square_ref[...] + square_sums(ctx_ref)
    lanes = squares.T[:SQUARE_ROWS, :]
    first = lanes.astype(BF16)
    rest = (lanes - first.astype(F32)).astype(BF16)
    groups, cols = give_ref.shape[0], give_ref.shape[2]
    core = lax.rem(lax.axis_index("tp"), 2)
    for ref, side in ((give_ref, 1 - core), (keep_ref, core)):
        for y in range(groups):
            at = pl.ds(pl.multiple_of((2 * y + side) * cols, cols), cols)
            part = sum_ref[:, at] + jnp.dot(ctx_ref[...], w_ref[start:, at], preferred_element_type=F32)
            ref[y, :rows, :] = part.astype(BF16)
            ref[y, rows:, :rows] = first
            ref[y, rows:, rows:2 * rows] = rest
            if cols > 2 * rows:
                ref[y, rows:, 2 * rows:] = jnp.zeros((SQUARE_ROWS, cols - 2 * rows), BF16)


def merge(keep_ref, got_ref, peak_ref, peak_got, peak_out, *give_refs):
    peak_out[...] = jnp.maximum(peak_ref[...], peak_got[...])
    groups = keep_ref.shape[0]
    mine = lax.axis_index("tp") // 2
    for step, ref in enumerate(give_refs):
        y = lax.rem(mine + step, groups)
        total = keep_ref[y].astype(F32) + got_ref[y].astype(F32)
        ref[...] = total.astype(ref.dtype)


def finish(features, peak_ref, peak_got, keep_ref, *refs):
    peak_out, out_ref = refs[-2:]
    peak_out[...] = jnp.maximum(peak_ref[...], peak_got[...])
    rows = out_ref.shape[0]
    total = keep_ref[...]
    for ref in refs[:-2]:
        total = total + ref[...].astype(F32)
    squares = total[rows:rows + 8, :rows] + total[rows:rows + 8, rows:2 * rows]
    inverse = lax.rsqrt(squares / features + 1e-05)
    column = jnp.broadcast_to(inverse[:1, :], (rows, rows)).T[:, :1]
    out_ref[...] = (total[:rows, :] * column).astype(BF16)


def on_device(queries, key_vectors, value_vectors, block_order, norm_gain, kv_weight):
    rows, width = queries.shape[1:]
    heads = width // DH
    peers = lax.axis_size("tp")
    sources = lax.axis_size("cp")
    kv_width = key_vectors.shape[2]
    columns = kv_weight.shape[2]
    out_cols = columns // peers
    shape = jax.ShapeDtypeStruct
    steps = [2**i for i in range((sources - 1).bit_length())]

    pair_here = jnp.concatenate([key_vectors[0], value_vectors[0]], axis=1)
    pair = shifted(pair_here, "pp", 1)
    cut = heads * 3 // 4
    counts = [cut, heads - cut]
    starts = [0, cut]
    crossed = []

    def cross(start, count, after, micros):
        part = call(
            functools.partial(take, start * DH),
            shape((rows, count * DH), BF16),
            (queries, after),
            [WHOLE, OUTSIDE],
            name="take",
            micros=micros,
        )
        crossed.append(shifted(part, "pp", 1))

    mark = call(touch, shape((8, LANES), F32), (pair_here,), [OUTSIDE], name="touch", micros=3)
    cross(starts[0], counts[0], mark, 3)
    triple = call(join, shape((rows, 3 * kv_width), BF16), (pair, pair_here), name="join")
    moved = {d: swapped(triple, "cp", d) for d in reversed(range(1, sources))}
    triples = [triple] + [moved[d] for d in range(1, sources)]
    cross(starts[1], counts[1], triple, 0)
    features = call(
        prepare,
        shape((2, LANES, sources * rows), BF16),
        (block_order, triple),
        [SCALARS, OUTSIDE],
        name="prepare",
        micros=3,
    )
    w = call(
        weigh,
        shape((width, columns), BF16),
        (kv_weight[0], norm_gain, features),
        [WHOLE, WHOLE, OUTSIDE],
        name="weigh",
        micros=1,
    )
    kv_local = kv_width // DH
    turned = shape((kv_local, 2, DH + LANES, sources * rows), BF16)
    kt, v_all, own = call(
        arrange,
        (turned, shape((kv_local, sources * rows, 2 * DH), BF16), turned),
        (features, *triples),
        name="arrange",
        micros=0.2,
    )
    peak = call(maxima, shape((1, heads), F32), (queries, own), limit=32, name="maxima", micros=0.7)
    contexts, after = [], peak
    for start, count, part in zip(starts, counts, crossed):
        context = call(
            functools.partial(attend, start, heads),
            shape((rows, count * DH), BF16),
            (part, kt, v_all, after),
            [WHOLE, WHOLE, WHOLE, OUTSIDE],
            limit=32,
            name="attend",
            micros=count * 0.12,
        )
        contexts.append(context)
        if start == 0:
            total, squares = call(
                project_first,
                (shape((rows, columns), F32), shape((rows, LANES), F32)),
                (context, w),
                name="project_first",
                micros=0.7,
            )
            after = squares
    slab = shape((peers // 2, rows + SQUARE_ROWS, out_cols), BF16)
    give, keep = call(
        project_last, (slab, slab), (contexts[-1], w, total, squares), name="project_last", micros=0.5
    )
    got = lax.ppermute(give, "tp", [(i, i ^ 1) for i in range(peers)])
    peak = bind(peak, give)
    slab = (rows + SQUARE_ROWS, out_cols)
    peak, mine, *others = call(
        merge,
        [shape((1, heads), F32), shape(slab, F32)] + [shape(slab, BF16)] * (peers // 2 - 1),
        (keep, got, peak, swapped(peak, "cp", steps[0])),
        name="merge",
    )
    for step in steps[1:-1]:
        peak = jnp.maximum(peak, swapped(peak, "cp", step))
    others = [
        lax.ppermute(block, "tp", [(i, (i + 2 * (step + 1)) % peers) for i in range(peers)])
        for step, block in enumerate(others)
    ]
    max_logits, kv_next = call(
        functools.partial(finish, width * peers),
        (shape((1, heads), F32), shape((rows, out_cols), BF16)),
        (peak, swapped(peak, "cp", steps[-1]), mine, *others),
        name="finish",
    )
    return (max_logits, kv_next[None])


def solution(mesh):
    return jax.shard_map(
        on_device,
        mesh=mesh,
        in_specs=(
            P("pp", "cp", "tp"),
            P("pp", "cp", "tp"),
            P("pp", "cp", "tp"),
            P(),
            P("pp", "tp"),
            P("pp", "tp", None),
        ),
        out_specs=(P("pp", "tp"), P("pp", "cp", "tp")),
        check_vma=False,
    )
```

```python
import functools
import math

import jax
import jax.numpy as jnp
from jax import lax
from jax.experimental import pallas as pl
from jax.experimental.pallas import tpu as pltpu
from jax.sharding import PartitionSpec as P

DH = 128
LANES = 128
SQUARE_ROWS = 16
MASKED = -(2.0**100)
LOG2E = math.log2(math.e)
F32 = jnp.float32
BF16 = jnp.bfloat16
WHOLE = pl.BlockSpec(memory_space=pltpu.VMEM)
OUTSIDE = pl.BlockSpec(memory_space=pl.ANY)
SCALARS = pl.BlockSpec(memory_space=pltpu.SMEM)


def call(kernel, outs, args, specs=None, scratch=(), limit=16, name=None, aliases=None, micros=0):
    return pl.pallas_call(
        kernel,
        out_shape=outs,
        in_specs=specs or [WHOLE] * len(args),
        out_specs=jax.tree.map(lambda _: WHOLE, outs),
        scratch_shapes=scratch,
        name=name,
        input_output_aliases=aliases or {},
        cost_estimate=pl.CostEstimate(flops=int(micros * 1e9), bytes_accessed=0, transcendentals=0) if micros else None,
        compiler_params=pltpu.CompilerParams(vmem_limit_bytes=limit * 2**20),
    )(*args)


def partner(index, step, size):
    return (index + step) % size if size & (size - 1) else index ^ step


def swapped(block, axis, step):
    size = lax.axis_size(axis)
    return lax.ppermute(block, axis, [(i, partner(i, step, size)) for i in range(size)])


def shifted(block, axis, distance):
    size = lax.axis_size(axis)
    return lax.ppermute(block, axis, [((i - distance) % size, i) for i in range(size)])


def bind_kernel(block_ref, after, out_ref):
    out_ref[...] = block_ref[...]


def bind(block, after):
    return call(
        bind_kernel, jax.ShapeDtypeStruct(block.shape, block.dtype), (block, after), [WHOLE, OUTSIDE], name="bind"
    )


def source_of(d, me, sources):
    return lax.rem(me - d + sources, sources) if sources & (sources - 1) else me ^ d


def take(first, q_ref, after, part_ref):
    part_ref[...] = q_ref[0, :, first:first + part_ref.shape[1]]


def prepare(order_ref, after, feature_ref):
    sources = lax.axis_size("cp")
    me = lax.axis_index("cp")
    rows = feature_ref.shape[2] // sources
    block = rows // 2
    feature = lax.broadcasted_iota(jnp.int32, (LANES, rows), 0)
    key = lax.broadcasted_iota(jnp.int32, (LANES, rows), 1)
    place = lax.rem(key, block)
    for side in range(2):
        mine = order_ref[2 * me + side]
        for d in range(sources):
            source = source_of(d, me, sources)
            other = jnp.where(key < block, order_ref[2 * source], order_ref[2 * source + 1])
            chosen = jnp.where(other == mine, place, jnp.where(other > mine, block, -1))
            feature_ref[side, :, d * rows:(d + 1) * rows] = jnp.where(feature == chosen, 1.0, 0.0).astype(BF16)


def touch(block_ref, out_ref):
    out_ref[...] = jnp.zeros(out_ref.shape, F32)


def join(pair_ref, here_ref, out_ref):
    width = pair_ref.shape[1]
    out_ref[:, :width] = pair_ref[...]
    out_ref[:, width:] = here_ref[:, :width // 2]


def arrange(after, feature_ref, *refs):
    triples, (kt_ref, v_ref, own_ref) = refs[:-3], refs[-3:]
    rows = triples[0].shape[0]
    kv_local = v_ref.shape[0]
    for g in range(kv_local):
        v_ref[g, :, DH:] = jnp.ones((v_ref.shape[1], DH), BF16)
        for ref in (kt_ref, own_ref):
            for side in range(2):
                ref[g, side, DH:, :] = feature_ref[side]
        for d, triple in enumerate(triples):
            part = slice(d * rows, (d + 1) * rows)
            for ref, first in ((kt_ref, g * DH), (own_ref, (2 * kv_local + g) * DH)):
                turned = triple[:, first:first + DH].astype(F32).T.astype(BF16)
                for side in range(2):
                    ref[g, side, :DH, part] = turned
            first = (kv_local + g) * DH
            v_ref[g, part, :DH] = triple[:, first:first + DH]


def spans(first_head, count, group, together):
    start = 0
    while start < count:
        g = (first_head + start) // group
        stop = min(start + together, count, (g + 1) * group - first_head)
        yield g, start, stop
        start = stop


def stacked(q_ref, start, stop, side):
    block = q_ref.shape[0] // 2
    shape = ((stop - start) * block, LANES)
    token = lax.rem(lax.broadcasted_iota(jnp.int32, shape, 0), block)
    lane = lax.broadcasted_iota(jnp.int32, shape, 1)
    blocked = jnp.where((lane > token) & (lane <= block), MASKED, 0.0).astype(BF16)
    tokens = slice(side * block, (side + 1) * block)
    q = jnp.concatenate([q_ref[tokens, h * DH:(h + 1) * DH] for h in range(start, stop)], axis=0)
    return jnp.concatenate([q, blocked], axis=1)


def maxima(q_ref, own_ref, peak_ref):
    q_ref = q_ref.at[0]
    block = q_ref.shape[0] // 2
    heads = q_ref.shape[1] // DH
    keys = own_ref.shape[3]
    for g, start, stop in spans(0, heads, heads // own_ref.shape[0], max(1, 8 * 512 // keys)):
        tops = []
        for side in range(2):
            s = jnp.dot(stacked(q_ref, start, stop, side), own_ref[g, side], preferred_element_type=F32)
            top = s[:, :LANES]
            for c in range(LANES, keys, LANES):
                top = jnp.maximum(top, s[:, c:c + LANES])
            tops.append(top)
        top = jnp.maximum(*tops)
        for j in range(stop - start):
            one = jnp.max(top[j * block:(j + 1) * block, :], axis=0, keepdims=True)
            h = start + j
            peak_ref[:, h:h + 1] = jnp.max(one, axis=1, keepdims=True) * (1.0 / math.sqrt(DH))


def attend(first_head, heads, q_ref, kt_ref, v_ref, after, ctx_ref):
    rows, width = q_ref.shape
    keys = v_ref.shape[1]
    block = rows // 2
    count = width // DH
    scale = 1.0 / math.sqrt(DH)
    for g, start, stop in spans(first_head, count, heads // v_ref.shape[0], max(1, 12 * 512 // keys)):
        scores = [
            jnp.dot(stacked(q_ref, start, stop, side), kt_ref[g, side], preferred_element_type=F32) for side in range(2)
        ]
        probs = []
        for s in scores:
            m = jnp.max(s, axis=1, keepdims=True)
            probs.append(jnp.exp2((s - m) * (scale * LOG2E)).astype(BF16))
        for side in range(2):
            o = jnp.dot(probs[side], v_ref[g], preferred_element_type=F32)
            o = (o[:, :DH] * (1.0 / o[:, DH:])).astype(BF16)
            for j in range(stop - start):
                ctx_ref[side * block:(side + 1) * block, (start + j) * DH:(start + j + 1) * DH] = o[
                    j * block:(j + 1) * block, :
                ]


def weigh(w_ref, gain_ref, after, out_ref):
    features, columns = w_ref.shape
    for f in range(0, features, LANES):
        gain = jnp.broadcast_to(gain_ref[:, f:f + LANES].astype(F32), (LANES, LANES)).T
        for c in range(0, columns, LANES):
            out_ref[f:f + LANES, c:c + LANES] = (w_ref[f:f + LANES, c:c + LANES].astype(F32) * gain).astype(BF16)


def square_sums(ctx_ref):
    total = None
    for c in range(0, ctx_ref.shape[1], LANES):
        wide = ctx_ref[:, c:c + LANES].astype(F32)
        total = wide * wide if total is None else total + wide * wide
    return jnp.broadcast_to(jnp.sum(total, axis=1, keepdims=True), total.shape)


def project_first(ctx_ref, w_ref, sum_ref, square_ref):
    square_ref[...] = square_sums(ctx_ref)
    sum_ref[...] = jnp.dot(ctx_ref[...], w_ref[:ctx_ref.shape[1], :], preferred_element_type=F32)


def project_last(ctx_ref, w_ref, sum_ref, square_ref, after, give_ref, keep_ref):
    rows, width = ctx_ref.shape
    start = w_ref.shape[0] - width
    squares = square_ref[...] + square_sums(ctx_ref)
    lanes = squares.T[:SQUARE_ROWS, :]
    first = lanes.astype(BF16)
    rest = (lanes - first.astype(F32)).astype(BF16)
    groups, cols = give_ref.shape[0], give_ref.shape[2]
    core = lax.rem(lax.axis_index("tp"), 2)
    for ref, side in ((give_ref, 1 - core), (keep_ref, core)):
        for y in range(groups):
            at = pl.ds(pl.multiple_of((2 * y + side) * cols, cols), cols)
            part = sum_ref[:, at] + jnp.dot(ctx_ref[...], w_ref[start:, at], preferred_element_type=F32)
            ref[y, :rows, :] = part.astype(BF16)
            ref[y, rows:, :rows] = first
            ref[y, rows:, rows:2 * rows] = rest
            if cols > 2 * rows:
                ref[y, rows:, 2 * rows:] = jnp.zeros((SQUARE_ROWS, cols - 2 * rows), BF16)


def larger(left_ref, right_ref, after, out_ref):
    out_ref[...] = jnp.maximum(left_ref[...], right_ref[...])


def merge(keep_ref, got_ref, *give_refs):
    groups = keep_ref.shape[0]
    mine = lax.axis_index("tp") // 2
    for step, ref in enumerate(give_refs):
        y = lax.rem(mine + step, groups)
        total = keep_ref[y].astype(F32) + got_ref[y].astype(F32)
        ref[...] = total.astype(ref.dtype)


def finish(features, peak_ref, peak_got, keep_ref, *refs):
    peak_out, out_ref = refs[-2:]
    peak_out[...] = jnp.maximum(peak_ref[...], peak_got[...])
    rows = out_ref.shape[0]
    total = keep_ref[...]
    for ref in refs[:-2]:
        total = total + ref[...].astype(F32)
    squares = total[rows:rows + 8, :rows] + total[rows:rows + 8, rows:2 * rows]
    inverse = lax.rsqrt(squares / features + 1e-05)
    column = jnp.broadcast_to(inverse[:1, :], (rows, rows)).T[:, :1]
    out_ref[...] = (total[:rows, :] * column).astype(BF16)


def on_device(queries, key_vectors, value_vectors, block_order, norm_gain, kv_weight):
    rows, width = queries.shape[1:]
    heads = width // DH
    peers = lax.axis_size("tp")
    sources = lax.axis_size("cp")
    kv_width = key_vectors.shape[2]
    columns = kv_weight.shape[2]
    out_cols = columns // peers
    shape = jax.ShapeDtypeStruct
    steps = [2**i for i in range((sources - 1).bit_length())]

    pair_here = jnp.concatenate([key_vectors[0], value_vectors[0]], axis=1)
    pair = shifted(pair_here, "pp", 1)
    cut = heads * 3 // 4
    counts = [cut, heads - cut]
    starts = [0, cut]
    crossed = []

    def cross(start, count, after, micros):
        part = call(
            functools.partial(take, start * DH),
            shape((rows, count * DH), BF16),
            (queries, after),
            [WHOLE, OUTSIDE],
            name="take",
            micros=micros,
        )
        crossed.append(shifted(part, "pp", 1))

    mark = call(touch, shape((8, LANES), F32), (pair_here,), [OUTSIDE], name="touch", micros=3)
    cross(starts[0], counts[0], mark, 3)
    triple = call(join, shape((rows, 3 * kv_width), BF16), (pair, pair_here), name="join")
    moved = {d: swapped(triple, "cp", d) for d in reversed(range(1, sources))}
    triples = [triple] + [moved[d] for d in range(1, sources)]
    cross(starts[1], counts[1], triple, 0)
    features = call(
        prepare,
        shape((2, LANES, sources * rows), BF16),
        (block_order, mark),
        [SCALARS, OUTSIDE],
        name="prepare",
        micros=3,
    )
    w = call(
        weigh,
        shape((width, columns), BF16),
        (kv_weight[0], norm_gain, moved[sources - 1]),
        [WHOLE, WHOLE, OUTSIDE],
        name="weigh",
        micros=1,
    )
    kv_local = kv_width // DH
    turned = shape((kv_local, 2, DH + LANES, sources * rows), BF16)
    kt, v_all, own = call(
        arrange,
        (turned, shape((kv_local, sources * rows, 2 * DH), BF16), turned),
        (w, features, *triples),
        [OUTSIDE] + [WHOLE] * (1 + sources),
        name="arrange",
        micros=0.2,
    )
    peak = call(maxima, shape((1, heads), F32), (queries, own), limit=32, name="maxima", micros=0.7)
    contexts, after = [], peak
    for start, count, part in zip(starts, counts, crossed):
        context = call(
            functools.partial(attend, start, heads),
            shape((rows, count * DH), BF16),
            (part, kt, v_all, after),
            [WHOLE, WHOLE, WHOLE, OUTSIDE],
            limit=32,
            name="attend",
            micros=count * 0.12,
        )
        contexts.append(context)
        if start == 0:
            total, squares = call(
                project_first,
                (shape((rows, columns), F32), shape((rows, LANES), F32)),
                (context, w),
                name="project_first",
                micros=0.7,
            )
            after = squares
    for step in steps[:-1]:
        peak = call(
            larger,
            shape((1, heads), F32),
            (peak, swapped(peak, "cp", step), squares),
            [WHOLE, WHOLE, OUTSIDE],
            name="larger",
        )
    slab = shape((peers // 2, rows + SQUARE_ROWS, out_cols), BF16)
    give, keep = call(
        project_last,
        (slab, slab),
        (contexts[-1], w, total, squares, peak),
        [WHOLE] * 4 + [OUTSIDE],
        name="project_last",
        micros=0.5,
    )
    got = lax.ppermute(give, "tp", [(i, i ^ 1) for i in range(peers)])
    peak = bind(peak, give)
    slab = (rows + SQUARE_ROWS, out_cols)
    mine, *others = call(
        merge, [shape(slab, F32)] + [shape(slab, BF16)] * (peers // 2 - 1), (keep, got), name="merge"
    )
    others = [
        lax.ppermute(block, "tp", [(i, (i + 2 * (step + 1)) % peers) for i in range(peers)])
        for step, block in enumerate(others)
    ]
    max_logits, kv_next = call(
        functools.partial(finish, width * peers),
        (shape((1, heads), F32), shape((rows, out_cols), BF16)),
        (peak, swapped(peak, "cp", steps[-1]), mine, *others),
        name="finish",
    )
    return (max_logits, kv_next[None])


def solution(mesh):
    return jax.shard_map(
        on_device,
        mesh=mesh,
        in_specs=(
            P("pp", "cp", "tp"),
            P("pp", "cp", "tp"),
            P("pp", "cp", "tp"),
            P(),
            P("pp", "tp"),
            P("pp", "tp", None),
        ),
        out_specs=(P("pp", "tp"), P("pp", "cp", "tp")),
        check_vma=False,
    )
```

```python
import functools
import math

import jax
import jax.numpy as jnp
from jax import lax
from jax.experimental import pallas as pl
from jax.experimental.pallas import tpu as pltpu
from jax.sharding import PartitionSpec as P

DH = 128
LANES = 128
SQUARE_ROWS = 16
MASKED = -(2.0**100)
LOG2E = math.log2(math.e)
F32 = jnp.float32
BF16 = jnp.bfloat16
WHOLE = pl.BlockSpec(memory_space=pltpu.VMEM)
OUTSIDE = pl.BlockSpec(memory_space=pl.ANY)
SCALARS = pl.BlockSpec(memory_space=pltpu.SMEM)


def call(kernel, outs, args, specs=None, scratch=(), limit=16, name=None, aliases=None, micros=0):
    return pl.pallas_call(
        kernel,
        out_shape=outs,
        in_specs=specs or [WHOLE] * len(args),
        out_specs=jax.tree.map(lambda _: WHOLE, outs),
        scratch_shapes=scratch,
        name=name,
        input_output_aliases=aliases or {},
        cost_estimate=pl.CostEstimate(flops=int(micros * 1e9), bytes_accessed=0, transcendentals=0) if micros else None,
        compiler_params=pltpu.CompilerParams(vmem_limit_bytes=limit * 2**20),
    )(*args)


def partner(index, step, size):
    return (index + step) % size if size & (size - 1) else index ^ step


def swapped(block, axis, step):
    size = lax.axis_size(axis)
    return lax.ppermute(block, axis, [(i, partner(i, step, size)) for i in range(size)])


def shifted(block, axis, distance):
    size = lax.axis_size(axis)
    return lax.ppermute(block, axis, [((i - distance) % size, i) for i in range(size)])


def bind_kernel(block_ref, after, out_ref):
    out_ref[...] = block_ref[...]


def bind(block, after):
    return call(
        bind_kernel, jax.ShapeDtypeStruct(block.shape, block.dtype), (block, after), [WHOLE, OUTSIDE], name="bind"
    )


def source_of(d, me, sources):
    return lax.rem(me - d + sources, sources) if sources & (sources - 1) else me ^ d


def take(first, q_ref, after, part_ref):
    part_ref[...] = q_ref[0, :, first:first + part_ref.shape[1]]


def prepare(order_ref, *refs):
    feature_ref = refs[-1]
    sources = lax.axis_size("cp")
    me = lax.axis_index("cp")
    rows = feature_ref.shape[2] // sources
    block = rows // 2
    feature = lax.broadcasted_iota(jnp.int32, (LANES, rows), 0)
    key = lax.broadcasted_iota(jnp.int32, (LANES, rows), 1)
    place = lax.rem(key, block)
    for side in range(2):
        mine = order_ref[2 * me + side]
        for d in range(sources):
            source = source_of(d, me, sources)
            other = jnp.where(key < block, order_ref[2 * source], order_ref[2 * source + 1])
            chosen = jnp.where(other == mine, place, jnp.where(other > mine, block, -1))
            feature_ref[side, :, d * rows:(d + 1) * rows] = jnp.where(feature == chosen, 1.0, 0.0).astype(BF16)


def touch(block_ref, out_ref):
    out_ref[...] = jnp.zeros(out_ref.shape, F32)


def first_part(block_ref, after, out_ref):
    out_ref[...] = block_ref[:, :out_ref.shape[1]]


def join(pair_ref, here_ref, out_ref):
    width = pair_ref.shape[1]
    out_ref[:, :width] = pair_ref[...]
    out_ref[:, width:] = here_ref[:, :width // 2]


def arrange(sources, after, feature_ref, *refs):
    pairs, owns, (kt_ref, v_ref, own_ref) = refs[:sources], refs[sources:-3], refs[-3:]
    rows = pairs[0].shape[0]
    kv_local = v_ref.shape[0]
    width = kv_local * DH
    for g in range(kv_local):
        v_ref[g, :, DH:] = jnp.ones((v_ref.shape[1], DH), BF16)
        for ref in (kt_ref, own_ref):
            for side in range(2):
                ref[g, side, DH:, :] = feature_ref[side]
        for d, (pair, own) in enumerate(zip(pairs, owns)):
            part = slice(d * rows, (d + 1) * rows)
            column = slice(g * DH, (g + 1) * DH)
            for ref, keys in ((kt_ref, pair[:, column]), (own_ref, own[:, own.shape[1] - width:][:, column])):
                turned = keys.astype(F32).T.astype(BF16)
                for side in range(2):
                    ref[g, side, :DH, part] = turned
            v_ref[g, part, :DH] = pair[:, width + g * DH:width + (g + 1) * DH]


def spans(first_head, count, group, together):
    start = 0
    while start < count:
        g = (first_head + start) // group
        stop = min(start + together, count, (g + 1) * group - first_head)
        yield g, start, stop
        start = stop


def stacked(q_ref, start, stop, side):
    block = q_ref.shape[0] // 2
    shape = ((stop - start) * block, LANES)
    token = lax.rem(lax.broadcasted_iota(jnp.int32, shape, 0), block)
    lane = lax.broadcasted_iota(jnp.int32, shape, 1)
    blocked = jnp.where((lane > token) & (lane <= block), MASKED, 0.0).astype(BF16)
    tokens = slice(side * block, (side + 1) * block)
    q = jnp.concatenate([q_ref[tokens, h * DH:(h + 1) * DH] for h in range(start, stop)], axis=0)
    return jnp.concatenate([q, blocked], axis=1)


def maxima(q_ref, own_ref, peak_ref):
    q_ref = q_ref.at[0]
    block = q_ref.shape[0] // 2
    heads = q_ref.shape[1] // DH
    keys = own_ref.shape[3]
    for g, start, stop in spans(0, heads, heads // own_ref.shape[0], max(1, 8 * 512 // keys)):
        tops = []
        for side in range(2):
            s = jnp.dot(stacked(q_ref, start, stop, side), own_ref[g, side], preferred_element_type=F32)
            top = s[:, :LANES]
            for c in range(LANES, keys, LANES):
                top = jnp.maximum(top, s[:, c:c + LANES])
            tops.append(top)
        top = jnp.maximum(*tops)
        for j in range(stop - start):
            one = jnp.max(top[j * block:(j + 1) * block, :], axis=0, keepdims=True)
            h = start + j
            peak_ref[:, h:h + 1] = jnp.max(one, axis=1, keepdims=True) * (1.0 / math.sqrt(DH))


def attend(first_head, heads, q_ref, kt_ref, v_ref, after, ctx_ref):
    rows, width = q_ref.shape
    keys = v_ref.shape[1]
    block = rows // 2
    count = width // DH
    scale = 1.0 / math.sqrt(DH)
    for g, start, stop in spans(first_head, count, heads // v_ref.shape[0], max(1, 12 * 512 // keys)):
        scores = [
            jnp.dot(stacked(q_ref, start, stop, side), kt_ref[g, side], preferred_element_type=F32) for side in range(2)
        ]
        probs = []
        for s in scores:
            m = jnp.max(s, axis=1, keepdims=True)
            probs.append(jnp.exp2((s - m) * (scale * LOG2E)).astype(BF16))
        for side in range(2):
            o = jnp.dot(probs[side], v_ref[g], preferred_element_type=F32)
            o = (o[:, :DH] * (1.0 / o[:, DH:])).astype(BF16)
            for j in range(stop - start):
                ctx_ref[side * block:(side + 1) * block, (start + j) * DH:(start + j + 1) * DH] = o[
                    j * block:(j + 1) * block, :
                ]


def weigh(w_ref, gain_ref, after, out_ref):
    features, columns = w_ref.shape
    for f in range(0, features, LANES):
        gain = jnp.broadcast_to(gain_ref[:, f:f + LANES].astype(F32), (LANES, LANES)).T
        for c in range(0, columns, LANES):
            out_ref[f:f + LANES, c:c + LANES] = (w_ref[f:f + LANES, c:c + LANES].astype(F32) * gain).astype(BF16)


def square_sums(ctx_ref):
    total = None
    for c in range(0, ctx_ref.shape[1], LANES):
        wide = ctx_ref[:, c:c + LANES].astype(F32)
        total = wide * wide if total is None else total + wide * wide
    return jnp.broadcast_to(jnp.sum(total, axis=1, keepdims=True), total.shape)


def project_first(ctx_ref, w_ref, sum_ref, square_ref):
    square_ref[...] = square_sums(ctx_ref)
    sum_ref[...] = jnp.dot(ctx_ref[...], w_ref[:ctx_ref.shape[1], :], preferred_element_type=F32)


def project_last(ctx_ref, w_ref, sum_ref, square_ref, after, give_ref, keep_ref):
    rows, width = ctx_ref.shape
    start = w_ref.shape[0] - width
    squares = square_ref[...] + square_sums(ctx_ref)
    lanes = squares.T[:SQUARE_ROWS, :]
    first = lanes.astype(BF16)
    rest = (lanes - first.astype(F32)).astype(BF16)
    groups, cols = give_ref.shape[0], give_ref.shape[2]
    core = lax.rem(lax.axis_index("tp"), 2)
    for ref, side in ((give_ref, 1 - core), (keep_ref, core)):
        for y in range(groups):
            at = pl.ds(pl.multiple_of((2 * y + side) * cols, cols), cols)
            part = sum_ref[:, at] + jnp.dot(ctx_ref[...], w_ref[start:, at], preferred_element_type=F32)
            ref[y, :rows, :] = part.astype(BF16)
            ref[y, rows:, :rows] = first
            ref[y, rows:, rows:2 * rows] = rest
            if cols > 2 * rows:
                ref[y, rows:, 2 * rows:] = jnp.zeros((SQUARE_ROWS, cols - 2 * rows), BF16)


def larger(left_ref, right_ref, after, out_ref):
    out_ref[...] = jnp.maximum(left_ref[...], right_ref[...])


def merge(keep_ref, got_ref, *give_refs):
    groups = keep_ref.shape[0]
    mine = lax.axis_index("tp") // 2
    for step, ref in enumerate(give_refs):
        y = lax.rem(mine + step, groups)
        total = keep_ref[y].astype(F32) + got_ref[y].astype(F32)
        ref[...] = total.astype(ref.dtype)


def finish(features, peak_ref, peak_got, keep_ref, *refs):
    peak_out, out_ref = refs[-2:]
    peak_out[...] = jnp.maximum(peak_ref[...], peak_got[...])
    rows = out_ref.shape[0]
    total = keep_ref[...]
    for ref in refs[:-2]:
        total = total + ref[...].astype(F32)
    squares = total[rows:rows + 8, :rows] + total[rows:rows + 8, rows:2 * rows]
    inverse = lax.rsqrt(squares / features + 1e-05)
    column = jnp.broadcast_to(inverse[:1, :], (rows, rows)).T[:, :1]
    out_ref[...] = (total[:rows, :] * column).astype(BF16)


def on_device(queries, key_vectors, value_vectors, block_order, norm_gain, kv_weight):
    rows, width = queries.shape[1:]
    heads = width // DH
    peers = lax.axis_size("tp")
    sources = lax.axis_size("cp")
    kv_width = key_vectors.shape[2]
    columns = kv_weight.shape[2]
    out_cols = columns // peers
    shape = jax.ShapeDtypeStruct
    steps = [2**i for i in range((sources - 1).bit_length())]

    pair_here = jnp.concatenate([key_vectors[0], value_vectors[0]], axis=1)
    pair = shifted(pair_here, "pp", 1)
    cut = heads * 3 // 4
    counts = [cut, heads - cut]
    starts = [0, cut]
    crossed = []

    def cross(start, count, after, micros):
        part = call(
            functools.partial(take, start * DH),
            shape((rows, count * DH), BF16),
            (queries, after),
            [WHOLE, OUTSIDE],
            name="take",
            micros=micros,
        )
        crossed.append(shifted(part, "pp", 1))
        return part

    mark = call(touch, shape((8, LANES), F32), (pair_here,), [OUTSIDE], name="touch", micros=3)
    first_queries = cross(starts[0], counts[0], mark, 3)
    own_here = call(
        first_part, shape((rows, kv_width), BF16), (pair_here, first_queries), [WHOLE, OUTSIDE], name="own_keys", micros=3
    )
    own_moved = {d: swapped(own_here, "cp", d) for d in reversed(range(2, sources))}
    features = call(
        prepare,
        shape((2, LANES, sources * rows), BF16),
        (block_order, mark, *own_moved.values()),
        [SCALARS] + [OUTSIDE] * (1 + len(own_moved)),
        name="prepare",
        micros=3,
    )
    triple = call(join, shape((rows, 3 * kv_width), BF16), (pair, pair_here), name="join")
    moved = {d: swapped(pair, "cp", d) for d in reversed(range(2, sources))}
    moved[1] = swapped(triple, "cp", 1)
    pairs = [pair] + [moved[d] for d in range(1, sources)]
    owns = [own_here, moved[1]] + [own_moved[d] for d in range(2, sources)]
    cross(starts[1], counts[1], features, 0)
    w = call(
        weigh,
        shape((width, columns), BF16),
        (kv_weight[0], norm_gain, moved[sources - 1]),
        [WHOLE, WHOLE, OUTSIDE],
        name="weigh",
    )
    kv_local = kv_width // DH
    turned = shape((kv_local, 2, DH + LANES, sources * rows), BF16)
    kt, v_all, own = call(
        functools.partial(arrange, sources),
        (turned, shape((kv_local, sources * rows, 2 * DH), BF16), turned),
        (w, features, *pairs, *owns),
        [OUTSIDE] + [WHOLE] * (1 + 2 * sources),
        name="arrange",
        micros=0.2,
    )
    peak = call(maxima, shape((1, heads), F32), (queries, own), limit=32, name="maxima", micros=0.7)
    contexts, after = [], peak
    for start, count, part in zip(starts, counts, crossed):
        context = call(
            functools.partial(attend, start, heads),
            shape((rows, count * DH), BF16),
            (part, kt, v_all, after),
            [WHOLE, WHOLE, WHOLE, OUTSIDE],
            limit=32,
            name="attend",
            micros=count * 0.12,
        )
        contexts.append(context)
        if start == 0:
            total, squares = call(
                project_first,
                (shape((rows, columns), F32), shape((rows, LANES), F32)),
                (context, w),
                name="project_first",
                micros=0.7,
            )
            after = squares
    for step in steps[:-1]:
        peak = call(
            larger,
            shape((1, heads), F32),
            (peak, swapped(peak, "cp", step), squares),
            [WHOLE, WHOLE, OUTSIDE],
            name="larger",
        )
    slab = shape((peers // 2, rows + SQUARE_ROWS, out_cols), BF16)
    give, keep = call(
        project_last,
        (slab, slab),
        (contexts[-1], w, total, squares, peak),
        [WHOLE] * 4 + [OUTSIDE],
        name="project_last",
        micros=0.5,
    )
    got = lax.ppermute(give, "tp", [(i, i ^ 1) for i in range(peers)])
    peak = bind(peak, give)
    slab = (rows + SQUARE_ROWS, out_cols)
    mine, *others = call(
        merge, [shape(slab, F32)] + [shape(slab, BF16)] * (peers // 2 - 1), (keep, got), name="merge"
    )
    others = [
        lax.ppermute(block, "tp", [(i, (i + 2 * (step + 1)) % peers) for i in range(peers)])
        for step, block in enumerate(others)
    ]
    max_logits, kv_next = call(
        functools.partial(finish, width * peers),
        (shape((1, heads), F32), shape((rows, out_cols), BF16)),
        (peak, swapped(peak, "cp", steps[-1]), mine, *others),
        name="finish",
    )
    return (max_logits, kv_next[None])


def solution(mesh):
    return jax.shard_map(
        on_device,
        mesh=mesh,
        in_specs=(
            P("pp", "cp", "tp"),
            P("pp", "cp", "tp"),
            P("pp", "cp", "tp"),
            P(),
            P("pp", "tp"),
            P("pp", "tp", None),
        ),
        out_specs=(P("pp", "tp"), P("pp", "cp", "tp")),
        check_vma=False,
    )
```

```python
import functools
import math

import jax
import jax.numpy as jnp
from jax import lax
from jax.experimental import pallas as pl
from jax.experimental.pallas import tpu as pltpu
from jax.sharding import PartitionSpec as P

DH = 128
LANES = 128
SQUARE_ROWS = 16
MASKED = -(2.0**100)
LOG2E = math.log2(math.e)
F32 = jnp.float32
BF16 = jnp.bfloat16
WHOLE = pl.BlockSpec(memory_space=pltpu.VMEM)
OUTSIDE = pl.BlockSpec(memory_space=pl.ANY)
SCALARS = pl.BlockSpec(memory_space=pltpu.SMEM)


def call(kernel, outs, args, specs=None, scratch=(), limit=16, name=None, aliases=None, micros=0):
    return pl.pallas_call(
        kernel,
        out_shape=outs,
        in_specs=specs or [WHOLE] * len(args),
        out_specs=jax.tree.map(lambda _: WHOLE, outs),
        scratch_shapes=scratch,
        name=name,
        input_output_aliases=aliases or {},
        cost_estimate=pl.CostEstimate(flops=int(micros * 1e9), bytes_accessed=0, transcendentals=0) if micros else None,
        compiler_params=pltpu.CompilerParams(vmem_limit_bytes=limit * 2**20),
    )(*args)


def partner(index, step, size):
    return (index + step) % size if size & (size - 1) else index ^ step


def swapped(block, axis, step):
    size = lax.axis_size(axis)
    return lax.ppermute(block, axis, [(i, partner(i, step, size)) for i in range(size)])


def shifted(block, axis, distance):
    size = lax.axis_size(axis)
    return lax.ppermute(block, axis, [((i - distance) % size, i) for i in range(size)])


def bind_kernel(block_ref, after, out_ref):
    out_ref[...] = block_ref[...]


def bind(block, after):
    return call(
        bind_kernel, jax.ShapeDtypeStruct(block.shape, block.dtype), (block, after), [WHOLE, OUTSIDE], name="bind"
    )


def source_of(d, me, sources):
    return lax.rem(me - d + sources, sources) if sources & (sources - 1) else me ^ d


def take(first, q_ref, after, part_ref):
    part_ref[...] = q_ref[0, :, first:first + part_ref.shape[1]]


def prepare(order_ref, after, feature_ref):
    sources = lax.axis_size("cp")
    me = lax.axis_index("cp")
    rows = feature_ref.shape[2] // sources
    block = rows // 2
    feature = lax.broadcasted_iota(jnp.int32, (LANES, rows), 0)
    key = lax.broadcasted_iota(jnp.int32, (LANES, rows), 1)
    place = lax.rem(key, block)
    for side in range(2):
        mine = order_ref[2 * me + side]
        for d in range(sources):
            source = source_of(d, me, sources)
            other = jnp.where(key < block, order_ref[2 * source], order_ref[2 * source + 1])
            chosen = jnp.where(other == mine, place, jnp.where(other > mine, block, -1))
            feature_ref[side, :, d * rows:(d + 1) * rows] = jnp.where(feature == chosen, 1.0, 0.0).astype(BF16)


def touch(block_ref, out_ref):
    out_ref[...] = jnp.zeros(out_ref.shape, F32)


def join(pair_ref, here_ref, out_ref):
    width = pair_ref.shape[1]
    out_ref[:, :width] = pair_ref[...]
    out_ref[:, width:] = here_ref[:, :width // 2]


def arrange(after, feature_ref, *refs):
    triples, (kt_ref, v_ref, own_ref) = refs[-4::-1], refs[-3:]
    rows = triples[0].shape[0]
    kv_local = v_ref.shape[0]
    for g in range(kv_local):
        v_ref[g, :, DH:] = jnp.ones((v_ref.shape[1], DH), BF16)
        for ref in (kt_ref, own_ref):
            for side in range(2):
                ref[g, side, DH:, :] = feature_ref[side]
        for d, triple in enumerate(triples):
            part = slice(d * rows, (d + 1) * rows)
            for ref, first in ((kt_ref, g * DH), (own_ref, (2 * kv_local + g) * DH)):
                turned = triple[:, first:first + DH].astype(F32).T.astype(BF16)
                for side in range(2):
                    ref[g, side, :DH, part] = turned
            first = (kv_local + g) * DH
            v_ref[g, part, :DH] = triple[:, first:first + DH]


def spans(first_head, count, group, together):
    start = 0
    while start < count:
        g = (first_head + start) // group
        stop = min(start + together, count, (g + 1) * group - first_head)
        yield g, start, stop
        start = stop


def stacked(q_ref, start, stop, side):
    block = q_ref.shape[0] // 2
    shape = ((stop - start) * block, LANES)
    token = lax.rem(lax.broadcasted_iota(jnp.int32, shape, 0), block)
    lane = lax.broadcasted_iota(jnp.int32, shape, 1)
    blocked = jnp.where((lane > token) & (lane <= block), MASKED, 0.0).astype(BF16)
    tokens = slice(side * block, (side + 1) * block)
    q = jnp.concatenate([q_ref[tokens, h * DH:(h + 1) * DH] for h in range(start, stop)], axis=0)
    return jnp.concatenate([q, blocked], axis=1)


def maxima(q_ref, own_ref, peak_ref):
    q_ref = q_ref.at[0]
    block = q_ref.shape[0] // 2
    heads = q_ref.shape[1] // DH
    keys = own_ref.shape[3]
    for g, start, stop in spans(0, heads, heads // own_ref.shape[0], max(1, 8 * 512 // keys)):
        tops = []
        for side in range(2):
            s = jnp.dot(stacked(q_ref, start, stop, side), own_ref[g, side], preferred_element_type=F32)
            top = s[:, :LANES]
            for c in range(LANES, keys, LANES):
                top = jnp.maximum(top, s[:, c:c + LANES])
            tops.append(top)
        top = jnp.maximum(*tops)
        for j in range(stop - start):
            one = jnp.max(top[j * block:(j + 1) * block, :], axis=0, keepdims=True)
            h = start + j
            peak_ref[:, h:h + 1] = jnp.max(one, axis=1, keepdims=True) * (1.0 / math.sqrt(DH))


def attend(first_head, heads, q_ref, kt_ref, v_ref, after, ctx_ref):
    rows, width = q_ref.shape
    keys = v_ref.shape[1]
    block = rows // 2
    count = width // DH
    scale = 1.0 / math.sqrt(DH)
    for g, start, stop in spans(first_head, count, heads // v_ref.shape[0], max(1, 12 * 512 // keys)):
        scores = [
            jnp.dot(stacked(q_ref, start, stop, side), kt_ref[g, side], preferred_element_type=F32) for side in range(2)
        ]
        probs = []
        for s in scores:
            m = jnp.max(s, axis=1, keepdims=True)
            probs.append(jnp.exp2((s - m) * (scale * LOG2E)).astype(BF16))
        for side in range(2):
            o = jnp.dot(probs[side], v_ref[g], preferred_element_type=F32)
            o = (o[:, :DH] * (1.0 / o[:, DH:])).astype(BF16)
            for j in range(stop - start):
                ctx_ref[side * block:(side + 1) * block, (start + j) * DH:(start + j + 1) * DH] = o[
                    j * block:(j + 1) * block, :
                ]


def weigh(w_ref, gain_ref, after, out_ref):
    features, columns = w_ref.shape
    for f in range(0, features, LANES):
        gain = jnp.broadcast_to(gain_ref[:, f:f + LANES].astype(F32), (LANES, LANES)).T
        for c in range(0, columns, LANES):
            out_ref[f:f + LANES, c:c + LANES] = (w_ref[f:f + LANES, c:c + LANES].astype(F32) * gain).astype(BF16)


def square_sums(ctx_ref):
    total = None
    for c in range(0, ctx_ref.shape[1], LANES):
        wide = ctx_ref[:, c:c + LANES].astype(F32)
        total = wide * wide if total is None else total + wide * wide
    return jnp.broadcast_to(jnp.sum(total, axis=1, keepdims=True), total.shape)


def project_first(ctx_ref, w_ref, sum_ref, square_ref):
    square_ref[...] = square_sums(ctx_ref)
    sum_ref[...] = jnp.dot(ctx_ref[...], w_ref[:ctx_ref.shape[1], :], preferred_element_type=F32)


def project_last(ctx_ref, w_ref, sum_ref, square_ref, after, give_ref, keep_ref):
    rows, width = ctx_ref.shape
    start = w_ref.shape[0] - width
    squares = square_ref[...] + square_sums(ctx_ref)
    lanes = squares.T[:SQUARE_ROWS, :]
    first = lanes.astype(BF16)
    rest = (lanes - first.astype(F32)).astype(BF16)
    groups, cols = give_ref.shape[0], give_ref.shape[2]
    core = lax.rem(lax.axis_index("tp"), 2)
    for ref, side in ((give_ref, 1 - core), (keep_ref, core)):
        for y in range(groups):
            at = pl.ds(pl.multiple_of((2 * y + side) * cols, cols), cols)
            part = sum_ref[:, at] + jnp.dot(ctx_ref[...], w_ref[start:, at], preferred_element_type=F32)
            ref[y, :rows, :] = part.astype(BF16)
            ref[y, rows:, :rows] = first
            ref[y, rows:, rows:2 * rows] = rest
            if cols > 2 * rows:
                ref[y, rows:, 2 * rows:] = jnp.zeros((SQUARE_ROWS, cols - 2 * rows), BF16)


def larger(left_ref, right_ref, after, out_ref):
    out_ref[...] = jnp.maximum(left_ref[...], right_ref[...])


def merge(keep_ref, got_ref, *give_refs):
    groups = keep_ref.shape[0]
    mine = lax.axis_index("tp") // 2
    for step, ref in enumerate(give_refs):
        y = lax.rem(mine + step, groups)
        total = keep_ref[y].astype(F32) + got_ref[y].astype(F32)
        ref[...] = total.astype(ref.dtype)


def finish(features, peak_ref, peak_got, keep_ref, *refs):
    peak_out, out_ref = refs[-2:]
    peak_out[...] = jnp.maximum(peak_ref[...], peak_got[...])
    rows = out_ref.shape[0]
    total = keep_ref[...]
    for ref in refs[:-2]:
        total = total + ref[...].astype(F32)
    squares = total[rows:rows + 8, :rows] + total[rows:rows + 8, rows:2 * rows]
    inverse = lax.rsqrt(squares / features + 1e-05)
    column = jnp.broadcast_to(inverse[:1, :], (rows, rows)).T[:, :1]
    out_ref[...] = (total[:rows, :] * column).astype(BF16)


def on_device(queries, key_vectors, value_vectors, block_order, norm_gain, kv_weight):
    rows, width = queries.shape[1:]
    heads = width // DH
    peers = lax.axis_size("tp")
    sources = lax.axis_size("cp")
    kv_width = key_vectors.shape[2]
    columns = kv_weight.shape[2]
    out_cols = columns // peers
    shape = jax.ShapeDtypeStruct
    steps = [2**i for i in range((sources - 1).bit_length())]

    pair_here = jnp.concatenate([key_vectors[0], value_vectors[0]], axis=1)
    pair = shifted(pair_here, "pp", 1)
    cut = heads // 2
    counts = [cut, heads - cut]
    starts = [0, cut]
    crossed = []

    def cross(start, count, after, micros):
        part = call(
            functools.partial(take, start * DH),
            shape((rows, count * DH), BF16),
            (queries, after),
            [WHOLE, OUTSIDE],
            name="take",
            micros=micros,
        )
        crossed.append(shifted(part, "pp", 1))

    mark = call(touch, shape((8, LANES), F32), (pair_here,), [OUTSIDE], name="touch", micros=3)
    cross(starts[0], counts[0], mark, 3)
    triple = call(join, shape((rows, 3 * kv_width), BF16), (pair, pair_here), name="join")
    moved = {d: swapped(triple, "cp", d) for d in reversed(range(1, sources))}
    triples = [triple] + [moved[d] for d in range(1, sources)]
    cross(starts[1], counts[1], triple, 0)
    features = call(
        prepare,
        shape((2, LANES, sources * rows), BF16),
        (block_order, mark),
        [SCALARS, OUTSIDE],
        name="prepare",
        micros=3,
    )
    w = call(
        weigh,
        shape((width, columns), BF16),
        (kv_weight[0], norm_gain, moved[sources - 1]),
        [WHOLE, WHOLE, OUTSIDE],
        name="weigh",
        micros=1,
    )
    kv_local = kv_width // DH
    turned = shape((kv_local, 2, DH + LANES, sources * rows), BF16)
    kt, v_all, own = call(
        arrange,
        (turned, shape((kv_local, sources * rows, 2 * DH), BF16), turned),
        (w, features, *reversed(triples)),
        [OUTSIDE] + [WHOLE] * (1 + sources),
        name="arrange",
        micros=0.2,
    )
    peak = call(maxima, shape((1, heads), F32), (queries, own), limit=32, name="maxima", micros=0.7)
    contexts, after = [], peak
    for start, count, part in zip(starts, counts, crossed):
        context = call(
            functools.partial(attend, start, heads),
            shape((rows, count * DH), BF16),
            (part, kt, v_all, after),
            [WHOLE, WHOLE, WHOLE, OUTSIDE],
            limit=32,
            name="attend",
            micros=count * 0.12,
        )
        contexts.append(context)
        if start == 0:
            total, squares = call(
                project_first,
                (shape((rows, columns), F32), shape((rows, LANES), F32)),
                (context, w),
                name="project_first",
                micros=0.7,
            )
            after = squares
    for step in steps[:-1]:
        peak = call(
            larger,
            shape((1, heads), F32),
            (peak, swapped(peak, "cp", step), squares),
            [WHOLE, WHOLE, OUTSIDE],
            name="larger",
        )
    slab = shape((peers // 2, rows + SQUARE_ROWS, out_cols), BF16)
    give, keep = call(
        project_last,
        (slab, slab),
        (contexts[-1], w, total, squares, peak),
        [WHOLE] * 4 + [OUTSIDE],
        name="project_last",
        micros=0.5,
    )
    got = lax.ppermute(give, "tp", [(i, i ^ 1) for i in range(peers)])
    peak = bind(peak, give)
    slab = (rows + SQUARE_ROWS, out_cols)
    mine, *others = call(
        merge, [shape(slab, F32)] + [shape(slab, BF16)] * (peers // 2 - 1), (keep, got), name="merge"
    )
    others = [
        lax.ppermute(block, "tp", [(i, (i + 2 * (step + 1)) % peers) for i in range(peers)])
        for step, block in enumerate(others)
    ]
    max_logits, kv_next = call(
        functools.partial(finish, width * peers),
        (shape((1, heads), F32), shape((rows, out_cols), BF16)),
        (peak, swapped(peak, "cp", steps[-1]), mine, *others),
        name="finish",
    )
    return (max_logits, kv_next[None])


def solution(mesh):
    return jax.shard_map(
        on_device,
        mesh=mesh,
        in_specs=(
            P("pp", "cp", "tp"),
            P("pp", "cp", "tp"),
            P("pp", "cp", "tp"),
            P(),
            P("pp", "tp"),
            P("pp", "tp", None),
        ),
        out_specs=(P("pp", "tp"), P("pp", "cp", "tp")),
        check_vma=False,
    )
```

```python
import functools
import math

import jax
import jax.numpy as jnp
from jax import lax
from jax.experimental import pallas as pl
from jax.experimental.pallas import tpu as pltpu
from jax.sharding import PartitionSpec as P

DH = 128
LANES = 128
SQUARE_ROWS = 16
MASKED = -(2.0**100)
LOG2E = math.log2(math.e)
F32 = jnp.float32
BF16 = jnp.bfloat16
WHOLE = pl.BlockSpec(memory_space=pltpu.VMEM)
OUTSIDE = pl.BlockSpec(memory_space=pl.ANY)
SCALARS = pl.BlockSpec(memory_space=pltpu.SMEM)


def call(kernel, outs, args, specs=None, scratch=(), limit=16, name=None, aliases=None, micros=0):
    return pl.pallas_call(
        kernel,
        out_shape=outs,
        in_specs=specs or [WHOLE] * len(args),
        out_specs=jax.tree.map(lambda _: WHOLE, outs),
        scratch_shapes=scratch,
        name=name,
        input_output_aliases=aliases or {},
        cost_estimate=pl.CostEstimate(flops=int(micros * 1e9), bytes_accessed=0, transcendentals=0) if micros else None,
        compiler_params=pltpu.CompilerParams(vmem_limit_bytes=limit * 2**20),
    )(*args)


def partner(index, step, size):
    return (index + step) % size if size & (size - 1) else index ^ step


def swapped(block, axis, step):
    size = lax.axis_size(axis)
    return lax.ppermute(block, axis, [(i, partner(i, step, size)) for i in range(size)])


def shifted(block, axis, distance):
    size = lax.axis_size(axis)
    return lax.ppermute(block, axis, [((i - distance) % size, i) for i in range(size)])


def bind_kernel(block_ref, after, out_ref):
    out_ref[...] = block_ref[...]


def bind(block, after):
    return call(
        bind_kernel, jax.ShapeDtypeStruct(block.shape, block.dtype), (block, after), [WHOLE, OUTSIDE], name="bind"
    )


def source_of(d, me, sources):
    return lax.rem(me - d + sources, sources) if sources & (sources - 1) else me ^ d


def take(first, q_ref, after, part_ref):
    part_ref[...] = q_ref[0, :, first:first + part_ref.shape[1]]


def prepare(order_ref, after, feature_ref):
    sources = lax.axis_size("cp")
    me = lax.axis_index("cp")
    rows = feature_ref.shape[2] // sources
    block = rows // 2
    feature = lax.broadcasted_iota(jnp.int32, (LANES, rows), 0)
    key = lax.broadcasted_iota(jnp.int32, (LANES, rows), 1)
    place = lax.rem(key, block)
    for side in range(2):
        mine = order_ref[2 * me + side]
        for d in range(sources):
            source = source_of(d, me, sources)
            other = jnp.where(key < block, order_ref[2 * source], order_ref[2 * source + 1])
            chosen = jnp.where(other == mine, place, jnp.where(other > mine, block, -1))
            feature_ref[side, :, d * rows:(d + 1) * rows] = jnp.where(feature == chosen, 1.0, 0.0).astype(BF16)


def touch(block_ref, out_ref):
    out_ref[...] = jnp.zeros(out_ref.shape, F32)


def join(pair_ref, here_ref, out_ref):
    width = pair_ref.shape[1]
    out_ref[:, :width] = pair_ref[...]
    out_ref[:, width:] = here_ref[:, :width // 2]


def arrange(after, feature_ref, *refs):
    triples, (kt_ref, v_ref, own_ref) = refs[-4::-1], refs[-3:]
    rows = triples[0].shape[0]
    kv_local = v_ref.shape[0]
    for g in range(kv_local):
        v_ref[g, :, DH:] = jnp.ones((v_ref.shape[1], DH), BF16)
        for ref in (kt_ref, own_ref):
            for side in range(2):
                ref[g, side, DH:, :] = feature_ref[side]
        for d, triple in enumerate(triples):
            part = slice(d * rows, (d + 1) * rows)
            for ref, first in ((kt_ref, g * DH), (own_ref, (2 * kv_local + g) * DH)):
                turned = triple[:, first:first + DH].astype(F32).T.astype(BF16)
                for side in range(2):
                    ref[g, side, :DH, part] = turned
            first = (kv_local + g) * DH
            v_ref[g, part, :DH] = triple[:, first:first + DH]


def spans(first_head, count, group, together):
    start = 0
    while start < count:
        g = (first_head + start) // group
        stop = min(start + together, count, (g + 1) * group - first_head)
        yield g, start, stop
        start = stop


def stacked(q_ref, start, stop, side):
    block = q_ref.shape[0] // 2
    shape = ((stop - start) * block, LANES)
    token = lax.rem(lax.broadcasted_iota(jnp.int32, shape, 0), block)
    lane = lax.broadcasted_iota(jnp.int32, shape, 1)
    blocked = jnp.where((lane > token) & (lane <= block), MASKED, 0.0).astype(BF16)
    tokens = slice(side * block, (side + 1) * block)
    q = jnp.concatenate([q_ref[tokens, h * DH:(h + 1) * DH] for h in range(start, stop)], axis=0)
    return jnp.concatenate([q, blocked], axis=1)


def maxima(q_ref, own_ref, peak_ref):
    q_ref = q_ref.at[0]
    block = q_ref.shape[0] // 2
    heads = q_ref.shape[1] // DH
    keys = own_ref.shape[3]
    for g, start, stop in spans(0, heads, heads // own_ref.shape[0], max(1, 8 * 512 // keys)):
        tops = []
        for side in range(2):
            s = jnp.dot(stacked(q_ref, start, stop, side), own_ref[g, side], preferred_element_type=F32)
            top = s[:, :LANES]
            for c in range(LANES, keys, LANES):
                top = jnp.maximum(top, s[:, c:c + LANES])
            tops.append(top)
        top = jnp.maximum(*tops)
        for j in range(stop - start):
            one = jnp.max(top[j * block:(j + 1) * block, :], axis=0, keepdims=True)
            h = start + j
            peak_ref[:, h:h + 1] = jnp.max(one, axis=1, keepdims=True) * (1.0 / math.sqrt(DH))


def attend(first_head, heads, q_ref, kt_ref, v_ref, after, ctx_ref):
    rows, width = q_ref.shape
    keys = v_ref.shape[1]
    block = rows // 2
    count = width // DH
    scale = 1.0 / math.sqrt(DH)
    for g, start, stop in spans(first_head, count, heads // v_ref.shape[0], max(1, 12 * 512 // keys)):
        scores = [
            jnp.dot(stacked(q_ref, start, stop, side), kt_ref[g, side], preferred_element_type=F32) for side in range(2)
        ]
        probs = []
        for s in scores:
            m = jnp.max(s, axis=1, keepdims=True)
            probs.append(jnp.exp2((s - m) * (scale * LOG2E)).astype(BF16))
        for side in range(2):
            o = jnp.dot(probs[side], v_ref[g], preferred_element_type=F32)
            o = (o[:, :DH] * (1.0 / o[:, DH:])).astype(BF16)
            for j in range(stop - start):
                ctx_ref[side * block:(side + 1) * block, (start + j) * DH:(start + j + 1) * DH] = o[
                    j * block:(j + 1) * block, :
                ]


def weigh(w_ref, gain_ref, after, out_ref):
    features, columns = w_ref.shape
    for f in range(0, features, LANES):
        gain = jnp.broadcast_to(gain_ref[:, f:f + LANES].astype(F32), (LANES, LANES)).T
        for c in range(0, columns, LANES):
            out_ref[f:f + LANES, c:c + LANES] = (w_ref[f:f + LANES, c:c + LANES].astype(F32) * gain).astype(BF16)


def square_sums(ctx_ref):
    total = None
    for c in range(0, ctx_ref.shape[1], LANES):
        wide = ctx_ref[:, c:c + LANES].astype(F32)
        total = wide * wide if total is None else total + wide * wide
    return jnp.broadcast_to(jnp.sum(total, axis=1, keepdims=True), total.shape)


def columns_of(y, side, cols):
    return pl.ds(pl.multiple_of((2 * y + side) * cols, cols), cols)


def fill(ref, y, part, squares):
    rows, cols = part.shape
    lanes = squares.T[:SQUARE_ROWS, :]
    first = lanes.astype(BF16)
    rest = (lanes - first.astype(F32)).astype(BF16)
    ref[y, :rows, :] = part.astype(BF16)
    ref[y, rows:, :rows] = first
    ref[y, rows:, rows:2 * rows] = rest
    if cols > 2 * rows:
        ref[y, rows:, 2 * rows:] = jnp.zeros((SQUARE_ROWS, cols - 2 * rows), BF16)


def project_first(ctx_ref, w_ref, sum_ref, square_ref):
    other = 1 - lax.rem(lax.axis_index("tp"), 2)
    square_ref[...] = square_sums(ctx_ref)
    for y in range(sum_ref.shape[0]):
        w = w_ref[:ctx_ref.shape[1], columns_of(y, other, sum_ref.shape[2])]
        sum_ref[y] = jnp.dot(ctx_ref[...], w, preferred_element_type=F32)


def project_give(ctx_ref, w_ref, sum_ref, square_ref, after, give_ref, square_out):
    other = 1 - lax.rem(lax.axis_index("tp"), 2)
    start = w_ref.shape[0] - ctx_ref.shape[1]
    squares = square_ref[...] + square_sums(ctx_ref)
    square_out[...] = squares
    for y in range(give_ref.shape[0]):
        w = w_ref[start:, columns_of(y, other, give_ref.shape[2])]
        fill(give_ref, y, sum_ref[y] + jnp.dot(ctx_ref[...], w, preferred_element_type=F32), squares)


def project_keep(first_ref, last_ref, w_ref, square_ref, keep_ref):
    core = lax.rem(lax.axis_index("tp"), 2)
    cut = first_ref.shape[1]
    for y in range(keep_ref.shape[0]):
        at = columns_of(y, core, keep_ref.shape[2])
        part = jnp.dot(first_ref[...], w_ref[:cut, at], preferred_element_type=F32)
        part += jnp.dot(last_ref[...], w_ref[cut:, at], preferred_element_type=F32)
        fill(keep_ref, y, part, square_ref[...])


def larger(left_ref, right_ref, after, out_ref):
    out_ref[...] = jnp.maximum(left_ref[...], right_ref[...])


def merge(keep_ref, got_ref, *give_refs):
    groups = keep_ref.shape[0]
    mine = lax.axis_index("tp") // 2
    for step, ref in enumerate(give_refs):
        y = lax.rem(mine + step, groups)
        total = keep_ref[y].astype(F32) + got_ref[y].astype(F32)
        ref[...] = total.astype(ref.dtype)


def finish(features, peak_ref, peak_got, keep_ref, *refs):
    peak_out, out_ref = refs[-2:]
    peak_out[...] = jnp.maximum(peak_ref[...], peak_got[...])
    rows = out_ref.shape[0]
    total = keep_ref[...]
    for ref in refs[:-2]:
        total = total + ref[...].astype(F32)
    squares = total[rows:rows + 8, :rows] + total[rows:rows + 8, rows:2 * rows]
    inverse = lax.rsqrt(squares / features + 1e-05)
    column = jnp.broadcast_to(inverse[:1, :], (rows, rows)).T[:, :1]
    out_ref[...] = (total[:rows, :] * column).astype(BF16)


def on_device(queries, key_vectors, value_vectors, block_order, norm_gain, kv_weight):
    rows, width = queries.shape[1:]
    heads = width // DH
    peers = lax.axis_size("tp")
    sources = lax.axis_size("cp")
    kv_width = key_vectors.shape[2]
    columns = kv_weight.shape[2]
    out_cols = columns // peers
    shape = jax.ShapeDtypeStruct
    steps = [2**i for i in range((sources - 1).bit_length())]

    pair_here = jnp.concatenate([key_vectors[0], value_vectors[0]], axis=1)
    pair = shifted(pair_here, "pp", 1)
    cut = heads // 2
    counts = [cut, heads - cut]
    starts = [0, cut]
    crossed = []

    def cross(start, count, after, micros):
        part = call(
            functools.partial(take, start * DH),
            shape((rows, count * DH), BF16),
            (queries, after),
            [WHOLE, OUTSIDE],
            name="take",
            micros=micros,
        )
        crossed.append(shifted(part, "pp", 1))

    mark = call(touch, shape((8, LANES), F32), (pair_here,), [OUTSIDE], name="touch", micros=3)
    cross(starts[0], counts[0], mark, 3)
    triple = call(join, shape((rows, 3 * kv_width), BF16), (pair, pair_here), name="join")
    moved = {d: swapped(triple, "cp", d) for d in reversed(range(1, sources))}
    triples = [triple] + [moved[d] for d in range(1, sources)]
    cross(starts[1], counts[1], triple, 0)
    features = call(
        prepare,
        shape((2, LANES, sources * rows), BF16),
        (block_order, mark),
        [SCALARS, OUTSIDE],
        name="prepare",
        micros=3,
    )
    w = call(
        weigh,
        shape((width, columns), BF16),
        (kv_weight[0], norm_gain, moved[sources - 1]),
        [WHOLE, WHOLE, OUTSIDE],
        name="weigh",
        micros=1,
    )
    kv_local = kv_width // DH
    turned = shape((kv_local, 2, DH + LANES, sources * rows), BF16)
    kt, v_all, own = call(
        arrange,
        (turned, shape((kv_local, sources * rows, 2 * DH), BF16), turned),
        (w, features, *reversed(triples)),
        [OUTSIDE] + [WHOLE] * (1 + sources),
        name="arrange",
        micros=0.2,
    )
    peak = call(maxima, shape((1, heads), F32), (queries, own), limit=32, name="maxima", micros=0.7)
    contexts, after = [], peak
    for start, count, part in zip(starts, counts, crossed):
        context = call(
            functools.partial(attend, start, heads),
            shape((rows, count * DH), BF16),
            (part, kt, v_all, after),
            [WHOLE, WHOLE, WHOLE, OUTSIDE],
            limit=32,
            name="attend",
            micros=count * 0.12,
        )
        contexts.append(context)
        if start == 0:
            total, squares = call(
                project_first,
                (shape((peers // 2, rows, out_cols), F32), shape((rows, LANES), F32)),
                (context, w),
                name="project_first",
                micros=0.7,
            )
            after = squares
    for step in steps[:-1]:
        peak = call(
            larger,
            shape((1, heads), F32),
            (peak, swapped(peak, "cp", step), contexts[-1]),
            [WHOLE, WHOLE, OUTSIDE],
            name="larger",
        )
    slab = shape((peers // 2, rows + SQUARE_ROWS, out_cols), BF16)
    give, squares = call(
        project_give,
        (slab, shape((rows, LANES), F32)),
        (contexts[-1], w, total, squares, peak),
        [WHOLE] * 4 + [OUTSIDE],
        name="project_give",
        micros=0.4,
    )
    keep = call(project_keep, slab, (*contexts, w, squares), name="project_keep", micros=0.6)
    got = lax.ppermute(give, "tp", [(i, i ^ 1) for i in range(peers)])
    peak = bind(peak, give)
    slab = (rows + SQUARE_ROWS, out_cols)
    mine, *others = call(
        merge, [shape(slab, F32)] + [shape(slab, BF16)] * (peers // 2 - 1), (keep, got), name="merge"
    )
    others = [
        lax.ppermute(block, "tp", [(i, (i + 2 * (step + 1)) % peers) for i in range(peers)])
        for step, block in enumerate(others)
    ]
    max_logits, kv_next = call(
        functools.partial(finish, width * peers),
        (shape((1, heads), F32), shape((rows, out_cols), BF16)),
        (peak, swapped(peak, "cp", steps[-1]), mine, *others),
        name="finish",
    )
    return (max_logits, kv_next[None])


def solution(mesh):
    return jax.shard_map(
        on_device,
        mesh=mesh,
        in_specs=(
            P("pp", "cp", "tp"),
            P("pp", "cp", "tp"),
            P("pp", "cp", "tp"),
            P(),
            P("pp", "tp"),
            P("pp", "tp", None),
        ),
        out_specs=(P("pp", "tp"), P("pp", "cp", "tp")),
        check_vma=False,
    )
```

```python
import functools
import math

import jax
import jax.numpy as jnp
from jax import lax
from jax.experimental import pallas as pl
from jax.experimental.pallas import tpu as pltpu
from jax.sharding import PartitionSpec as P

DH = 128
LANES = 128
SQUARE_ROWS = 16
MASKED = -(2.0**100)
LOG2E = math.log2(math.e)
F32 = jnp.float32
BF16 = jnp.bfloat16
WHOLE = pl.BlockSpec(memory_space=pltpu.VMEM)
OUTSIDE = pl.BlockSpec(memory_space=pl.ANY)
SCALARS = pl.BlockSpec(memory_space=pltpu.SMEM)


def call(kernel, outs, args, specs=None, scratch=(), limit=16, name=None, aliases=None, micros=0):
    return pl.pallas_call(
        kernel,
        out_shape=outs,
        in_specs=specs or [WHOLE] * len(args),
        out_specs=jax.tree.map(lambda _: WHOLE, outs),
        scratch_shapes=scratch,
        name=name,
        input_output_aliases=aliases or {},
        cost_estimate=pl.CostEstimate(flops=int(micros * 1e9), bytes_accessed=0, transcendentals=0) if micros else None,
        compiler_params=pltpu.CompilerParams(vmem_limit_bytes=limit * 2**20),
    )(*args)


def partner(index, step, size):
    return (index + step) % size if size & (size - 1) else index ^ step


def swapped(block, axis, step):
    size = lax.axis_size(axis)
    return lax.ppermute(block, axis, [(i, partner(i, step, size)) for i in range(size)])


def shifted(block, axis, distance):
    size = lax.axis_size(axis)
    return lax.ppermute(block, axis, [((i - distance) % size, i) for i in range(size)])


def bind_kernel(block_ref, after, out_ref):
    out_ref[...] = block_ref[...]


def bind(block, after):
    return call(
        bind_kernel, jax.ShapeDtypeStruct(block.shape, block.dtype), (block, after), [WHOLE, OUTSIDE], name="bind"
    )


def source_of(d, me, sources):
    return lax.rem(me - d + sources, sources) if sources & (sources - 1) else me ^ d


def take(first, q_ref, after, part_ref):
    part_ref[...] = q_ref[0, :, first:first + part_ref.shape[1]]


def prepare(order_ref, after, feature_ref):
    sources = lax.axis_size("cp")
    me = lax.axis_index("cp")
    rows = feature_ref.shape[2] // sources
    block = rows // 2
    feature = lax.broadcasted_iota(jnp.int32, (LANES, rows), 0)
    key = lax.broadcasted_iota(jnp.int32, (LANES, rows), 1)
    place = lax.rem(key, block)
    for side in range(2):
        mine = order_ref[2 * me + side]
        for d in range(sources):
            source = source_of(d, me, sources)
            other = jnp.where(key < block, order_ref[2 * source], order_ref[2 * source + 1])
            chosen = jnp.where(other == mine, place, jnp.where(other > mine, block, -1))
            feature_ref[side, :, d * rows:(d + 1) * rows] = jnp.where(feature == chosen, 1.0, 0.0).astype(BF16)


def touch(block_ref, out_ref):
    out_ref[...] = jnp.zeros(out_ref.shape, F32)


def join(pair_ref, here_ref, out_ref):
    width = pair_ref.shape[1]
    out_ref[:, :width] = pair_ref[...]
    out_ref[:, width:] = here_ref[:, :width // 2]


def turn(triple, first, block):
    return triple[:, first:first + block].astype(F32).T.astype(BF16)


def arrange_own(distances, after, feature_ref, *refs):
    triples, own_ref = refs[:-1], refs[-1]
    kv_local, rows = own_ref.shape[0], triples[0].shape[0]
    for g in range(kv_local):
        for n, (d, triple) in enumerate(zip(distances, triples)):
            part = slice(n * rows, (n + 1) * rows)
            turned = turn(triple, (2 * kv_local + g) * DH, DH)
            for side in range(2):
                own_ref[g, side, DH:, part] = feature_ref[side, :, d * rows:(d + 1) * rows]
                own_ref[g, side, :DH, part] = turned


def arrange(distances, after, feature_ref, *refs):
    triples, (kt_ref, v_ref) = refs[:-2], refs[-2:]
    rows = triples[0].shape[0]
    kv_local = v_ref.shape[0]
    for g in range(kv_local):
        v_ref[g, :, DH:] = jnp.ones((v_ref.shape[1], DH), BF16)
        for side in range(2):
            kt_ref[g, side, DH:, :] = feature_ref[side]
        for d, triple in zip(distances, triples):
            part = slice(d * rows, (d + 1) * rows)
            turned = turn(triple, g * DH, DH)
            for side in range(2):
                kt_ref[g, side, :DH, part] = turned
            first = (kv_local + g) * DH
            v_ref[g, part, :DH] = triple[:, first:first + DH]


def spans(first_head, count, group, together):
    start = 0
    while start < count:
        g = (first_head + start) // group
        stop = min(start + together, count, (g + 1) * group - first_head)
        yield g, start, stop
        start = stop


def stacked(q_ref, start, stop, side):
    block = q_ref.shape[0] // 2
    shape = ((stop - start) * block, LANES)
    token = lax.rem(lax.broadcasted_iota(jnp.int32, shape, 0), block)
    lane = lax.broadcasted_iota(jnp.int32, shape, 1)
    blocked = jnp.where((lane > token) & (lane <= block), MASKED, 0.0).astype(BF16)
    tokens = slice(side * block, (side + 1) * block)
    q = jnp.concatenate([q_ref[tokens, h * DH:(h + 1) * DH] for h in range(start, stop)], axis=0)
    return jnp.concatenate([q, blocked], axis=1)


def maxima(q_ref, own_ref, *refs):
    before, peak_ref = refs[:-1], refs[-1]
    q_ref = q_ref.at[0]
    block = q_ref.shape[0] // 2
    heads = q_ref.shape[1] // DH
    keys = own_ref.shape[3]
    for g, start, stop in spans(0, heads, heads // own_ref.shape[0], max(1, 8 * 512 // keys)):
        tops = []
        for side in range(2):
            s = jnp.dot(stacked(q_ref, start, stop, side), own_ref[g, side], preferred_element_type=F32)
            top = s[:, :LANES]
            for c in range(LANES, keys, LANES):
                top = jnp.maximum(top, s[:, c:c + LANES])
            tops.append(top)
        top = jnp.maximum(*tops)
        for j in range(stop - start):
            one = jnp.max(top[j * block:(j + 1) * block, :], axis=0, keepdims=True)
            h = start + j
            one = jnp.max(one, axis=1, keepdims=True) * (1.0 / math.sqrt(DH))
            peak_ref[:, h:h + 1] = jnp.maximum(one, before[0][:, h:h + 1]) if before else one


def attend(first_head, heads, q_ref, kt_ref, v_ref, after, ctx_ref):
    rows, width = q_ref.shape
    keys = v_ref.shape[1]
    block = rows // 2
    count = width // DH
    scale = 1.0 / math.sqrt(DH)
    together = max(1, min(4, 4 * 512 // keys))
    units = [
        (g, start, stop, side)
        for g, start, stop in spans(first_head, count, heads // v_ref.shape[0], together)
        for side in range(2)
    ]

    def scores(g, start, stop, side):
        return jnp.dot(stacked(q_ref, start, stop, side), kt_ref[g, side], preferred_element_type=F32)

    ahead = [scores(*unit) for unit in units[:2]]
    for n, (g, start, stop, side) in enumerate(units):
        s = ahead.pop(0)
        m = jnp.max(s, axis=1, keepdims=True)
        p = jnp.exp2((s - m) * (scale * LOG2E)).astype(BF16)
        if n + 2 < len(units):
            ahead.append(scores(*units[n + 2]))
        o = jnp.dot(p, v_ref[g], preferred_element_type=F32)
        o = (o[:, :DH] * (1.0 / o[:, DH:])).astype(BF16)
        for j in range(stop - start):
            ctx_ref[side * block:(side + 1) * block, (start + j) * DH:(start + j + 1) * DH] = o[
                j * block:(j + 1) * block, :
            ]


def weigh(w_ref, gain_ref, after, out_ref):
    features, columns = w_ref.shape
    for f in range(0, features, LANES):
        gain = jnp.broadcast_to(gain_ref[:, f:f + LANES].astype(F32), (LANES, LANES)).T
        for c in range(0, columns, LANES):
            out_ref[f:f + LANES, c:c + LANES] = (w_ref[f:f + LANES, c:c + LANES].astype(F32) * gain).astype(BF16)


def square_sums(ctx_ref):
    total = None
    for c in range(0, ctx_ref.shape[1], LANES):
        wide = ctx_ref[:, c:c + LANES].astype(F32)
        total = wide * wide if total is None else total + wide * wide
    return jnp.broadcast_to(jnp.sum(total, axis=1, keepdims=True), total.shape)


def columns_of(y, side, cols):
    return pl.ds(pl.multiple_of((2 * y + side) * cols, cols), cols)


def product(first_ref, last_ref, w_ref, at):
    cut = first_ref.shape[1]
    part = jnp.dot(first_ref[...], w_ref[:cut, at], preferred_element_type=F32)
    return part + jnp.dot(last_ref[...], w_ref[cut:, at], preferred_element_type=F32)


def fill(ref, y, part, squares):
    rows, cols = part.shape
    lanes = squares.T[:SQUARE_ROWS, :]
    first = lanes.astype(BF16)
    rest = (lanes - first.astype(F32)).astype(BF16)
    ref[y, :rows, :] = part.astype(BF16)
    ref[y, rows:, :rows] = first
    ref[y, rows:, rows:2 * rows] = rest
    if cols > 2 * rows:
        ref[y, rows:, 2 * rows:] = jnp.zeros((SQUARE_ROWS, cols - 2 * rows), BF16)


def project_give(first_ref, last_ref, w_ref, after, give_ref, square_ref):
    other = 1 - lax.rem(lax.axis_index("tp"), 2)
    squares = square_sums(first_ref) + square_sums(last_ref)
    square_ref[...] = squares
    for y in range(give_ref.shape[0]):
        fill(give_ref, y, product(first_ref, last_ref, w_ref, columns_of(y, other, give_ref.shape[2])), squares)


def project_keep(first_ref, last_ref, w_ref, square_ref, keep_ref):
    core = lax.rem(lax.axis_index("tp"), 2)
    for y in range(keep_ref.shape[0]):
        at = columns_of(y, core, keep_ref.shape[2])
        fill(keep_ref, y, product(first_ref, last_ref, w_ref, at), square_ref[...])


def larger(left_ref, right_ref, after, out_ref):
    out_ref[...] = jnp.maximum(left_ref[...], right_ref[...])


def merge(keep_ref, got_ref, *give_refs):
    groups = keep_ref.shape[0]
    mine = lax.axis_index("tp") // 2
    for step, ref in enumerate(give_refs):
        y = lax.rem(mine + step, groups)
        total = keep_ref[y].astype(F32) + got_ref[y].astype(F32)
        ref[...] = total.astype(ref.dtype)


def finish(features, peak_ref, peak_got, keep_ref, *refs):
    peak_out, out_ref = refs[-2:]
    peak_out[...] = jnp.maximum(peak_ref[...], peak_got[...])
    rows = out_ref.shape[0]
    total = keep_ref[...]
    for ref in refs[:-2]:
        total = total + ref[...].astype(F32)
    squares = total[rows:rows + 8, :rows] + total[rows:rows + 8, rows:2 * rows]
    inverse = lax.rsqrt(squares / features + 1e-05)
    column = jnp.broadcast_to(inverse[:1, :], (rows, rows)).T[:, :1]
    out_ref[...] = (total[:rows, :] * column).astype(BF16)


def on_device(queries, key_vectors, value_vectors, block_order, norm_gain, kv_weight):
    rows, width = queries.shape[1:]
    heads = width // DH
    peers = lax.axis_size("tp")
    sources = lax.axis_size("cp")
    kv_width = key_vectors.shape[2]
    columns = kv_weight.shape[2]
    out_cols = columns // peers
    shape = jax.ShapeDtypeStruct
    steps = [2**i for i in range((sources - 1).bit_length())]

    pair_here = jnp.concatenate([key_vectors[0], value_vectors[0]], axis=1)
    pair = shifted(pair_here, "pp", 1)
    cut = heads // 2
    counts = [cut, heads - cut]
    starts = [0, cut]
    crossed = []

    def cross(start, count, after, micros):
        part = call(
            functools.partial(take, start * DH),
            shape((rows, count * DH), BF16),
            (queries, after),
            [WHOLE, OUTSIDE],
            name="take",
            micros=micros,
        )
        crossed.append(shifted(part, "pp", 1))

    mark = call(touch, shape((8, LANES), F32), (pair_here,), [OUTSIDE], name="touch", micros=3)
    cross(starts[0], counts[0], mark, 3)
    triple = call(join, shape((rows, 3 * kv_width), BF16), (pair, pair_here), name="join")
    moved = {d: swapped(triple, "cp", d) for d in reversed(range(1, sources))}
    triples = [triple] + [moved[d] for d in range(1, sources)]
    cross(starts[1], counts[1], triple, 0)
    features = call(
        prepare,
        shape((2, LANES, sources * rows), BF16),
        (block_order, mark),
        [SCALARS, OUTSIDE],
        name="prepare",
        micros=0.5,
    )
    w = call(
        weigh,
        shape((width, columns), BF16),
        (kv_weight[0], norm_gain, features),
        [WHOLE, WHOLE, OUTSIDE],
        name="weigh",
        micros=1,
    )
    kv_local = kv_width // DH
    near = sorted({0, sources - 1})
    far = list(reversed(range(1, sources - 1)))
    peaks, after = [], w
    for distances in [near, far] if far else [near]:
        own = call(
            functools.partial(arrange_own, distances),
            shape((kv_local, 2, DH + LANES, len(distances) * rows), BF16),
            (after, features, *[triples[d] for d in distances]),
            [OUTSIDE] + [WHOLE] * (1 + len(distances)),
            name="arrange_own",
            micros=0.2,
        )
        peaks.append(
            call(
                maxima,
                shape((1, heads), F32),
                (queries, own, *peaks[-1:]),
                limit=32,
                name="maxima",
                micros=0.5,
            )
        )
        after = peaks[-1]
    peak = peaks[-1]
    distances = list(reversed(range(sources)))
    kt, v_all = call(
        functools.partial(arrange, distances),
        (
            shape((kv_local, 2, DH + LANES, sources * rows), BF16),
            shape((kv_local, sources * rows, 2 * DH), BF16),
        ),
        (w, features, *[triples[d] for d in distances]),
        [OUTSIDE] + [WHOLE] * (1 + sources),
        name="arrange",
        micros=0.2,
    )
    contexts, after = [], peak
    for start, count, part in zip(starts, counts, crossed):
        context = call(
            functools.partial(attend, start, heads),
            shape((rows, count * DH), BF16),
            (part, kt, v_all, after),
            [WHOLE, WHOLE, WHOLE, OUTSIDE],
            limit=32,
            name="attend",
            micros=count * 0.12,
        )
        contexts.append(context)
        after = context
    for step in steps[:-1]:
        peak = call(
            larger,
            shape((1, heads), F32),
            (peak, swapped(peak, "cp", step), contexts[-1]),
            [WHOLE, WHOLE, OUTSIDE],
            name="larger",
        )
    slab = shape((peers // 2, rows + SQUARE_ROWS, out_cols), BF16)
    give, squares = call(
        project_give,
        (slab, shape((rows, LANES), F32)),
        (*contexts, w, peak),
        [WHOLE] * 3 + [OUTSIDE],
        name="project_give",
        micros=0.4,
    )
    keep = call(project_keep, slab, (*contexts, w, squares), name="project_keep", micros=0.6)
    got = lax.ppermute(give, "tp", [(i, i ^ 1) for i in range(peers)])
    peak = bind(peak, give)
    slab = (rows + SQUARE_ROWS, out_cols)
    mine, *others = call(
        merge, [shape(slab, F32)] + [shape(slab, BF16)] * (peers // 2 - 1), (keep, got), name="merge"
    )
    others = [
        lax.ppermute(block, "tp", [(i, (i + 2 * (step + 1)) % peers) for i in range(peers)])
        for step, block in enumerate(others)
    ]
    max_logits, kv_next = call(
        functools.partial(finish, width * peers),
        (shape((1, heads), F32), shape((rows, out_cols), BF16)),
        (peak, swapped(peak, "cp", steps[-1]), mine, *others),
        name="finish",
    )
    return (max_logits, kv_next[None])


def solution(mesh):
    return jax.shard_map(
        on_device,
        mesh=mesh,
        in_specs=(
            P("pp", "cp", "tp"),
            P("pp", "cp", "tp"),
            P("pp", "cp", "tp"),
            P(),
            P("pp", "tp"),
            P("pp", "tp", None),
        ),
        out_specs=(P("pp", "tp"), P("pp", "cp", "tp")),
        check_vma=False,
    )
```

```python
import functools
import math

import jax
import jax.numpy as jnp
from jax import lax
from jax.experimental import pallas as pl
from jax.experimental.pallas import tpu as pltpu
from jax.sharding import PartitionSpec as P

DH = 128
LANES = 128
SQUARE_ROWS = 16
MASKED = -(2.0**100)
LOG2E = math.log2(math.e)
F32 = jnp.float32
BF16 = jnp.bfloat16
WHOLE = pl.BlockSpec(memory_space=pltpu.VMEM)
OUTSIDE = pl.BlockSpec(memory_space=pl.ANY)
SCALARS = pl.BlockSpec(memory_space=pltpu.SMEM)


def call(kernel, outs, args, specs=None, scratch=(), limit=16, name=None, aliases=None, micros=0):
    return pl.pallas_call(
        kernel,
        out_shape=outs,
        in_specs=specs or [WHOLE] * len(args),
        out_specs=jax.tree.map(lambda _: WHOLE, outs),
        scratch_shapes=scratch,
        name=name,
        input_output_aliases=aliases or {},
        cost_estimate=pl.CostEstimate(flops=int(micros * 1e9), bytes_accessed=0, transcendentals=0) if micros else None,
        compiler_params=pltpu.CompilerParams(vmem_limit_bytes=limit * 2**20),
    )(*args)


def partner(index, step, size):
    return (index + step) % size if size & (size - 1) else index ^ step


def swapped(block, axis, step):
    size = lax.axis_size(axis)
    return lax.ppermute(block, axis, [(i, partner(i, step, size)) for i in range(size)])


def shifted(block, axis, distance):
    size = lax.axis_size(axis)
    return lax.ppermute(block, axis, [((i - distance) % size, i) for i in range(size)])


def bind_kernel(block_ref, after, out_ref):
    out_ref[...] = block_ref[...]


def bind(block, after):
    return call(
        bind_kernel, jax.ShapeDtypeStruct(block.shape, block.dtype), (block, after), [WHOLE, OUTSIDE], name="bind"
    )


def source_of(d, me, sources):
    return lax.rem(me - d + sources, sources) if sources & (sources - 1) else me ^ d


def take(first, q_ref, after, part_ref):
    part_ref[...] = q_ref[0, :, first:first + part_ref.shape[1]]


def prepare(order_ref, after, feature_ref):
    sources = lax.axis_size("cp")
    me = lax.axis_index("cp")
    rows = feature_ref.shape[2] // sources
    block = rows // 2
    feature = lax.broadcasted_iota(jnp.int32, (LANES, rows), 0)
    key = lax.broadcasted_iota(jnp.int32, (LANES, rows), 1)
    place = lax.rem(key, block)
    for side in range(2):
        mine = order_ref[2 * me + side]
        for d in range(sources):
            source = source_of(d, me, sources)
            other = jnp.where(key < block, order_ref[2 * source], order_ref[2 * source + 1])
            chosen = jnp.where(other == mine, place, jnp.where(other > mine, block, -1))
            feature_ref[side, :, d * rows:(d + 1) * rows] = jnp.where(feature == chosen, 1.0, 0.0).astype(BF16)


def touch(block_ref, out_ref):
    out_ref[...] = jnp.zeros(out_ref.shape, F32)


def join(pair_ref, here_ref, out_ref):
    width = pair_ref.shape[1]
    out_ref[:, :width] = pair_ref[...]
    out_ref[:, width:] = here_ref[:, :width // 2]


def arrange(after, feature_ref, *refs):
    triples, (kt_ref, v_ref, own_ref) = refs[-4::-1], refs[-3:]
    rows = triples[0].shape[0]
    kv_local = v_ref.shape[0]
    for g in range(kv_local):
        v_ref[g, :, DH:] = jnp.ones((v_ref.shape[1], DH), BF16)
        for ref in (kt_ref, own_ref):
            for side in range(2):
                ref[g, side, DH:, :] = feature_ref[side]
        for d, triple in enumerate(triples):
            part = slice(d * rows, (d + 1) * rows)
            for ref, first in ((kt_ref, g * DH), (own_ref, (2 * kv_local + g) * DH)):
                turned = triple[:, first:first + DH].astype(F32).T.astype(BF16)
                for side in range(2):
                    ref[g, side, :DH, part] = turned
            first = (kv_local + g) * DH
            v_ref[g, part, :DH] = triple[:, first:first + DH]


def spans(first_head, count, group, together):
    start = 0
    while start < count:
        g = (first_head + start) // group
        stop = min(start + together, count, (g + 1) * group - first_head)
        yield g, start, stop
        start = stop


def stacked(q_ref, start, stop, side):
    block = q_ref.shape[0] // 2
    shape = ((stop - start) * block, LANES)
    token = lax.rem(lax.broadcasted_iota(jnp.int32, shape, 0), block)
    lane = lax.broadcasted_iota(jnp.int32, shape, 1)
    blocked = jnp.where((lane > token) & (lane <= block), MASKED, 0.0).astype(BF16)
    tokens = slice(side * block, (side + 1) * block)
    q = jnp.concatenate([q_ref[tokens, h * DH:(h + 1) * DH] for h in range(start, stop)], axis=0)
    return jnp.concatenate([q, blocked], axis=1)


def maxima(q_ref, own_ref, peak_ref):
    q_ref = q_ref.at[0]
    block = q_ref.shape[0] // 2
    heads = q_ref.shape[1] // DH
    keys = own_ref.shape[3]
    for g, start, stop in spans(0, heads, heads // own_ref.shape[0], max(1, 8 * 512 // keys)):
        tops = []
        for side in range(2):
            s = jnp.dot(stacked(q_ref, start, stop, side), own_ref[g, side], preferred_element_type=F32)
            top = s[:, :LANES]
            for c in range(LANES, keys, LANES):
                top = jnp.maximum(top, s[:, c:c + LANES])
            tops.append(top)
        top = jnp.maximum(*tops)
        for j in range(stop - start):
            one = jnp.max(top[j * block:(j + 1) * block, :], axis=0, keepdims=True)
            h = start + j
            peak_ref[:, h:h + 1] = jnp.max(one, axis=1, keepdims=True) * (1.0 / math.sqrt(DH))


def attend(first_head, heads, q_ref, kt_ref, v_ref, after, ctx_ref):
    rows, width = q_ref.shape
    keys = v_ref.shape[1]
    block = rows // 2
    count = width // DH
    scale = 1.0 / math.sqrt(DH)
    for g, start, stop in spans(first_head, count, heads // v_ref.shape[0], max(1, 12 * 512 // keys)):
        scores = [
            jnp.dot(stacked(q_ref, start, stop, side), kt_ref[g, side], preferred_element_type=F32) for side in range(2)
        ]
        probs = []
        for s in scores:
            m = jnp.max(s, axis=1, keepdims=True)
            probs.append(jnp.exp2((s - m) * (scale * LOG2E)).astype(BF16))
        for side in range(2):
            o = jnp.dot(probs[side], v_ref[g], preferred_element_type=F32)
            o = (o[:, :DH] * (1.0 / o[:, DH:])).astype(BF16)
            for j in range(stop - start):
                ctx_ref[side * block:(side + 1) * block, (start + j) * DH:(start + j + 1) * DH] = o[
                    j * block:(j + 1) * block, :
                ]


def weigh(w_ref, gain_ref, after, out_ref):
    features, columns = w_ref.shape
    for f in range(0, features, LANES):
        gain = jnp.broadcast_to(gain_ref[:, f:f + LANES].astype(F32), (LANES, LANES)).T
        for c in range(0, columns, LANES):
            out_ref[f:f + LANES, c:c + LANES] = (w_ref[f:f + LANES, c:c + LANES].astype(F32) * gain).astype(BF16)


def square_sums(ctx_ref):
    total = None
    for c in range(0, ctx_ref.shape[1], LANES):
        wide = ctx_ref[:, c:c + LANES].astype(F32)
        total = wide * wide if total is None else total + wide * wide
    return jnp.broadcast_to(jnp.sum(total, axis=1, keepdims=True), total.shape)


def columns_of(y, side, cols):
    return pl.ds(pl.multiple_of((2 * y + side) * cols, cols), cols)


def fill(ref, y, part, squares):
    rows, cols = part.shape
    lanes = squares.T[:SQUARE_ROWS, :]
    first = lanes.astype(BF16)
    rest = (lanes - first.astype(F32)).astype(BF16)
    ref[y, :rows, :] = part.astype(BF16)
    ref[y, rows:, :rows] = first
    ref[y, rows:, rows:2 * rows] = rest
    if cols > 2 * rows:
        ref[y, rows:, 2 * rows:] = jnp.zeros((SQUARE_ROWS, cols - 2 * rows), BF16)


def product(first_ref, last_ref, w_ref, at):
    cut = first_ref.shape[1]
    part = jnp.dot(first_ref[...], w_ref[:cut, at], preferred_element_type=F32)
    return part + jnp.dot(last_ref[...], w_ref[cut:, at], preferred_element_type=F32)


def project_give(first_ref, last_ref, w_ref, give_ref, square_ref):
    other = 1 - lax.rem(lax.axis_index("tp"), 2)
    squares = square_sums(first_ref) + square_sums(last_ref)
    square_ref[...] = squares
    for y in range(give_ref.shape[0]):
        fill(give_ref, y, product(first_ref, last_ref, w_ref, columns_of(y, other, give_ref.shape[2])), squares)


def project_keep(first_ref, last_ref, w_ref, square_ref, keep_ref):
    core = lax.rem(lax.axis_index("tp"), 2)
    for y in range(keep_ref.shape[0]):
        at = columns_of(y, core, keep_ref.shape[2])
        fill(keep_ref, y, product(first_ref, last_ref, w_ref, at), square_ref[...])


def larger(left_ref, right_ref, out_ref):
    out_ref[...] = jnp.maximum(left_ref[...], right_ref[...])


def merge(keep_ref, got_ref, *give_refs):
    groups = keep_ref.shape[0]
    mine = lax.axis_index("tp") // 2
    for step, ref in enumerate(give_refs):
        y = lax.rem(mine + step, groups)
        total = keep_ref[y].astype(F32) + got_ref[y].astype(F32)
        ref[...] = total.astype(ref.dtype)


def finish(features, peak_ref, peak_got, keep_ref, *refs):
    peak_out, out_ref = refs[-2:]
    peak_out[...] = jnp.maximum(peak_ref[...], peak_got[...])
    rows = out_ref.shape[0]
    total = keep_ref[...]
    for ref in refs[:-2]:
        total = total + ref[...].astype(F32)
    squares = total[rows:rows + 8, :rows] + total[rows:rows + 8, rows:2 * rows]
    inverse = lax.rsqrt(squares / features + 1e-05)
    column = jnp.broadcast_to(inverse[:1, :], (rows, rows)).T[:, :1]
    out_ref[...] = (total[:rows, :] * column).astype(BF16)


def on_device(queries, key_vectors, value_vectors, block_order, norm_gain, kv_weight):
    rows, width = queries.shape[1:]
    heads = width // DH
    peers = lax.axis_size("tp")
    sources = lax.axis_size("cp")
    kv_width = key_vectors.shape[2]
    columns = kv_weight.shape[2]
    out_cols = columns // peers
    shape = jax.ShapeDtypeStruct
    steps = [2**i for i in range((sources - 1).bit_length())]

    pair_here = jnp.concatenate([key_vectors[0], value_vectors[0]], axis=1)
    pair = shifted(pair_here, "pp", 1)
    cut = heads // 2
    counts = [cut, heads - cut]
    starts = [0, cut]
    crossed = []

    def cross(start, count, after, micros):
        part = call(
            functools.partial(take, start * DH),
            shape((rows, count * DH), BF16),
            (queries, after),
            [WHOLE, OUTSIDE],
            name="take",
            micros=micros,
        )
        crossed.append(shifted(part, "pp", 1))

    mark = call(touch, shape((8, LANES), F32), (pair_here,), [OUTSIDE], name="touch", micros=3)
    cross(starts[0], counts[0], mark, 3)
    triple = call(join, shape((rows, 3 * kv_width), BF16), (pair, pair_here), name="join")
    moved = {d: swapped(triple, "cp", d) for d in reversed(range(1, sources))}
    triples = [triple] + [moved[d] for d in range(1, sources)]
    cross(starts[1], counts[1], triple, 0)
    features = call(
        prepare,
        shape((2, LANES, sources * rows), BF16),
        (block_order, mark),
        [SCALARS, OUTSIDE],
        name="prepare",
        micros=3,
    )
    w = call(
        weigh,
        shape((width, columns), BF16),
        (kv_weight[0], norm_gain, moved[sources - 1]),
        [WHOLE, WHOLE, OUTSIDE],
        name="weigh",
        micros=1,
    )
    kv_local = kv_width // DH
    turned = shape((kv_local, 2, DH + LANES, sources * rows), BF16)
    kt, v_all, own = call(
        arrange,
        (turned, shape((kv_local, sources * rows, 2 * DH), BF16), turned),
        (w, features, *reversed(triples)),
        [OUTSIDE] + [WHOLE] * (1 + sources),
        name="arrange",
        micros=0.2,
    )
    peak = call(maxima, shape((1, heads), F32), (queries, own), limit=32, name="maxima", micros=0.7)
    contexts, after = [], peak
    for start, count, part in zip(starts, counts, crossed):
        context = call(
            functools.partial(attend, start, heads),
            shape((rows, count * DH), BF16),
            (part, kt, v_all, after),
            [WHOLE, WHOLE, WHOLE, OUTSIDE],
            limit=32,
            name="attend",
            micros=count * 0.12,
        )
        contexts.append(context)
        after = context
    slab = shape((peers // 2, rows + SQUARE_ROWS, out_cols), BF16)
    give, squares = call(
        project_give,
        (slab, shape((rows, LANES), F32)),
        (*contexts, w),
        name="project_give",
        micros=0.4,
    )
    keep = call(project_keep, slab, (*contexts, w, squares), name="project_keep", micros=0.6)
    got = lax.ppermute(give, "tp", [(i, i ^ 1) for i in range(peers)])
    peak = bind(peak, give)
    for step in reversed(steps[1:]):
        peak = call(
            larger,
            shape((1, heads), F32),
            (peak, swapped(peak, "cp", step)),
            name="larger",
            micros=5,
        )
    slab = (rows + SQUARE_ROWS, out_cols)
    mine, *others = call(
        merge, [shape(slab, F32)] + [shape(slab, BF16)] * (peers // 2 - 1), (keep, got), name="merge"
    )
    others = [
        lax.ppermute(block, "tp", [(i, (i + 2 * (step + 1)) % peers) for i in range(peers)])
        for step, block in enumerate(others)
    ]
    max_logits, kv_next = call(
        functools.partial(finish, width * peers),
        (shape((1, heads), F32), shape((rows, out_cols), BF16)),
        (peak, swapped(peak, "cp", steps[0]), mine, *others),
        name="finish",
    )
    return (max_logits, kv_next[None])


def solution(mesh):
    return jax.shard_map(
        on_device,
        mesh=mesh,
        in_specs=(
            P("pp", "cp", "tp"),
            P("pp", "cp", "tp"),
            P("pp", "cp", "tp"),
            P(),
            P("pp", "tp"),
            P("pp", "tp", None),
        ),
        out_specs=(P("pp", "tp"), P("pp", "cp", "tp")),
        check_vma=False,
    )
```

```python
import functools
import math

import jax
import jax.numpy as jnp
from jax import lax
from jax.experimental import pallas as pl
from jax.experimental.pallas import tpu as pltpu
from jax.sharding import PartitionSpec as P

DH = 128
LANES = 128
SQUARE_ROWS = 16
MASKED = -(2.0**100)
LOG2E = math.log2(math.e)
F32 = jnp.float32
BF16 = jnp.bfloat16
WHOLE = pl.BlockSpec(memory_space=pltpu.VMEM)
OUTSIDE = pl.BlockSpec(memory_space=pl.ANY)
SCALARS = pl.BlockSpec(memory_space=pltpu.SMEM)


def call(kernel, outs, args, specs=None, scratch=(), limit=16, name=None, aliases=None, micros=0):
    return pl.pallas_call(
        kernel,
        out_shape=outs,
        in_specs=specs or [WHOLE] * len(args),
        out_specs=jax.tree.map(lambda _: WHOLE, outs),
        scratch_shapes=scratch,
        name=name,
        input_output_aliases=aliases or {},
        cost_estimate=pl.CostEstimate(flops=int(micros * 1e9), bytes_accessed=0, transcendentals=0) if micros else None,
        compiler_params=pltpu.CompilerParams(vmem_limit_bytes=limit * 2**20),
    )(*args)


def partner(index, step, size):
    return (index + step) % size if size & (size - 1) else index ^ step


def swapped(block, axis, step):
    size = lax.axis_size(axis)
    return lax.ppermute(block, axis, [(i, partner(i, step, size)) for i in range(size)])


def shifted(block, axis, distance):
    size = lax.axis_size(axis)
    return lax.ppermute(block, axis, [((i - distance) % size, i) for i in range(size)])


def bind_kernel(block_ref, after, out_ref):
    out_ref[...] = block_ref[...]


def bind(block, after):
    return call(
        bind_kernel, jax.ShapeDtypeStruct(block.shape, block.dtype), (block, after), [WHOLE, OUTSIDE], name="bind"
    )


def source_of(d, me, sources):
    return lax.rem(me - d + sources, sources) if sources & (sources - 1) else me ^ d


def take(first, q_ref, after, part_ref):
    part_ref[...] = q_ref[0, :, first:first + part_ref.shape[1]]


def prepare(order_ref, after, feature_ref):
    sources = lax.axis_size("cp")
    me = lax.axis_index("cp")
    rows = feature_ref.shape[2] // sources
    block = rows // 2
    feature = lax.broadcasted_iota(jnp.int32, (LANES, rows), 0)
    key = lax.broadcasted_iota(jnp.int32, (LANES, rows), 1)
    place = lax.rem(key, block)
    for side in range(2):
        mine = order_ref[2 * me + side]
        for d in range(sources):
            source = source_of(d, me, sources)
            other = jnp.where(key < block, order_ref[2 * source], order_ref[2 * source + 1])
            chosen = jnp.where(other == mine, place, jnp.where(other > mine, block, -1))
            feature_ref[side, :, d * rows:(d + 1) * rows] = jnp.where(feature == chosen, 1.0, 0.0).astype(BF16)


def touch(block_ref, out_ref):
    out_ref[...] = jnp.zeros(out_ref.shape, F32)


def join(pair_ref, here_ref, out_ref):
    width = pair_ref.shape[1]
    out_ref[:, :width] = pair_ref[...]
    out_ref[:, width:] = here_ref[:, :width // 2]


def arrange(after, feature_ref, *refs):
    triples, (kt_ref, v_ref, own_ref) = refs[-4::-1], refs[-3:]
    rows = triples[0].shape[0]
    kv_local = v_ref.shape[0]
    for g in range(kv_local):
        v_ref[g, :, DH:] = jnp.ones((v_ref.shape[1], DH), BF16)
        for ref in (kt_ref, own_ref):
            for side in range(2):
                ref[g, side, DH:, :] = feature_ref[side]
        for d, triple in enumerate(triples):
            part = slice(d * rows, (d + 1) * rows)
            for ref, first in ((kt_ref, g * DH), (own_ref, (2 * kv_local + g) * DH)):
                turned = triple[:, first:first + DH].astype(F32).T.astype(BF16)
                for side in range(2):
                    ref[g, side, :DH, part] = turned
            first = (kv_local + g) * DH
            v_ref[g, part, :DH] = triple[:, first:first + DH]


def spans(first_head, count, group, together):
    start = 0
    while start < count:
        g = (first_head + start) // group
        stop = min(start + together, count, (g + 1) * group - first_head)
        yield g, start, stop
        start = stop


def stacked(q_ref, start, stop, side):
    block = q_ref.shape[0] // 2
    shape = ((stop - start) * block, LANES)
    token = lax.rem(lax.broadcasted_iota(jnp.int32, shape, 0), block)
    lane = lax.broadcasted_iota(jnp.int32, shape, 1)
    blocked = jnp.where((lane > token) & (lane <= block), MASKED, 0.0).astype(BF16)
    tokens = slice(side * block, (side + 1) * block)
    q = jnp.concatenate([q_ref[tokens, h * DH:(h + 1) * DH] for h in range(start, stop)], axis=0)
    return jnp.concatenate([q, blocked], axis=1)


def maxima(q_ref, own_ref, peak_ref):
    q_ref = q_ref.at[0]
    block = q_ref.shape[0] // 2
    heads = q_ref.shape[1] // DH
    keys = own_ref.shape[3]
    for g, start, stop in spans(0, heads, heads // own_ref.shape[0], max(1, 8 * 512 // keys)):
        tops = []
        for side in range(2):
            s = jnp.dot(stacked(q_ref, start, stop, side), own_ref[g, side], preferred_element_type=F32)
            top = s[:, :LANES]
            for c in range(LANES, keys, LANES):
                top = jnp.maximum(top, s[:, c:c + LANES])
            tops.append(top)
        top = jnp.maximum(*tops)
        for j in range(stop - start):
            one = jnp.max(top[j * block:(j + 1) * block, :], axis=0, keepdims=True)
            h = start + j
            peak_ref[:, h:h + 1] = jnp.max(one, axis=1, keepdims=True) * (1.0 / math.sqrt(DH))


def attend(first_head, heads, q_ref, kt_ref, v_ref, after, ctx_ref):
    rows, width = q_ref.shape
    keys = v_ref.shape[1]
    block = rows // 2
    count = width // DH
    scale = 1.0 / math.sqrt(DH)
    for g, start, stop in spans(first_head, count, heads // v_ref.shape[0], max(1, 12 * 512 // keys)):
        scores = [
            jnp.dot(stacked(q_ref, start, stop, side), kt_ref[g, side], preferred_element_type=F32) for side in range(2)
        ]
        probs = []
        for s in scores:
            m = jnp.max(s, axis=1, keepdims=True)
            probs.append(jnp.exp2((s - m) * (scale * LOG2E)).astype(BF16))
        for side in range(2):
            o = jnp.dot(probs[side], v_ref[g], preferred_element_type=F32)
            o = (o[:, :DH] * (1.0 / o[:, DH:])).astype(BF16)
            for j in range(stop - start):
                ctx_ref[side * block:(side + 1) * block, (start + j) * DH:(start + j + 1) * DH] = o[
                    j * block:(j + 1) * block, :
                ]


def weigh(w_ref, gain_ref, after, out_ref):
    features, columns = w_ref.shape
    for f in range(0, features, LANES):
        gain = jnp.broadcast_to(gain_ref[:, f:f + LANES].astype(F32), (LANES, LANES)).T
        for c in range(0, columns, LANES):
            out_ref[f:f + LANES, c:c + LANES] = (w_ref[f:f + LANES, c:c + LANES].astype(F32) * gain).astype(BF16)


def square_sums(ctx_ref):
    total = None
    for c in range(0, ctx_ref.shape[1], LANES):
        wide = ctx_ref[:, c:c + LANES].astype(F32)
        total = wide * wide if total is None else total + wide * wide
    return jnp.broadcast_to(jnp.sum(total, axis=1, keepdims=True), total.shape)


def columns_of(y, side, cols):
    return pl.ds(pl.multiple_of((2 * y + side) * cols, cols), cols)


def fill(ref, y, part, squares):
    rows, cols = part.shape
    lanes = squares.T[:SQUARE_ROWS, :]
    first = lanes.astype(BF16)
    rest = (lanes - first.astype(F32)).astype(BF16)
    ref[y, :rows, :] = part.astype(BF16)
    ref[y, rows:, :rows] = first
    ref[y, rows:, rows:2 * rows] = rest
    if cols > 2 * rows:
        ref[y, rows:, 2 * rows:] = jnp.zeros((SQUARE_ROWS, cols - 2 * rows), BF16)


def product(first_ref, last_ref, w_ref, at):
    cut = first_ref.shape[1]
    part = jnp.dot(first_ref[...], w_ref[:cut, at], preferred_element_type=F32)
    return part + jnp.dot(last_ref[...], w_ref[cut:, at], preferred_element_type=F32)


def project_give(first_ref, last_ref, w_ref, give_ref, square_ref):
    other = 1 - lax.rem(lax.axis_index("tp"), 2)
    squares = square_sums(first_ref) + square_sums(last_ref)
    square_ref[...] = squares
    for y in range(give_ref.shape[0]):
        fill(give_ref, y, product(first_ref, last_ref, w_ref, columns_of(y, other, give_ref.shape[2])), squares)


def project_keep(first_ref, last_ref, w_ref, square_ref, keep_ref):
    core = lax.rem(lax.axis_index("tp"), 2)
    for y in range(keep_ref.shape[0]):
        at = columns_of(y, core, keep_ref.shape[2])
        fill(keep_ref, y, product(first_ref, last_ref, w_ref, at), square_ref[...])


def larger(left_ref, right_ref, out_ref):
    out_ref[...] = jnp.maximum(left_ref[...], right_ref[...])


def merge(keep_ref, got_ref, *give_refs):
    groups = keep_ref.shape[0]
    mine = lax.axis_index("tp") // 2
    for step, ref in enumerate(give_refs):
        y = lax.rem(mine + step, groups)
        total = keep_ref[y].astype(F32) + got_ref[y].astype(F32)
        ref[...] = total.astype(ref.dtype)


def finish(features, peak_ref, peak_got, keep_ref, *refs):
    peak_out, out_ref = refs[-2:]
    peak_out[...] = jnp.maximum(peak_ref[...], peak_got[...])
    rows = out_ref.shape[0]
    total = keep_ref[...]
    for ref in refs[:-2]:
        total = total + ref[...].astype(F32)
    squares = total[rows:rows + 8, :rows] + total[rows:rows + 8, rows:2 * rows]
    inverse = lax.rsqrt(squares / features + 1e-05)
    column = jnp.broadcast_to(inverse[:1, :], (rows, rows)).T[:, :1]
    out_ref[...] = (total[:rows, :] * column).astype(BF16)


def on_device(queries, key_vectors, value_vectors, block_order, norm_gain, kv_weight):
    rows, width = queries.shape[1:]
    heads = width // DH
    peers = lax.axis_size("tp")
    sources = lax.axis_size("cp")
    kv_width = key_vectors.shape[2]
    columns = kv_weight.shape[2]
    out_cols = columns // peers
    shape = jax.ShapeDtypeStruct
    steps = [2**i for i in range((sources - 1).bit_length())]

    pair_here = jnp.concatenate([key_vectors[0], value_vectors[0]], axis=1)
    pair = shifted(pair_here, "pp", 1)
    cut = heads // 2
    counts = [cut, heads - cut]
    starts = [0, cut]
    crossed = []

    def cross(start, count, after, micros):
        part = call(
            functools.partial(take, start * DH),
            shape((rows, count * DH), BF16),
            (queries, after),
            [WHOLE, OUTSIDE],
            name="take",
            micros=micros,
        )
        crossed.append(shifted(part, "pp", 1))

    mark = call(touch, shape((8, LANES), F32), (pair_here,), [OUTSIDE], name="touch", micros=3)
    cross(starts[0], counts[0], mark, 3)
    triple = call(join, shape((rows, 3 * kv_width), BF16), (pair, pair_here), name="join")
    moved = {d: swapped(triple, "cp", d) for d in reversed(range(1, sources))}
    triples = [triple] + [moved[d] for d in range(1, sources)]
    cross(starts[1], counts[1], triple, 0)
    features = call(
        prepare,
        shape((2, LANES, sources * rows), BF16),
        (block_order, mark),
        [SCALARS, OUTSIDE],
        name="prepare",
        micros=3,
    )
    w = call(
        weigh,
        shape((width, columns), BF16),
        (kv_weight[0], norm_gain, moved[sources - 1]),
        [WHOLE, WHOLE, OUTSIDE],
        name="weigh",
        micros=1,
    )
    kv_local = kv_width // DH
    turned = shape((kv_local, 2, DH + LANES, sources * rows), BF16)
    kt, v_all, own = call(
        arrange,
        (turned, shape((kv_local, sources * rows, 2 * DH), BF16), turned),
        (w, features, *reversed(triples)),
        [OUTSIDE] + [WHOLE] * (1 + sources),
        name="arrange",
        micros=0.2,
    )
    peak = call(maxima, shape((1, heads), F32), (queries, own), limit=32, name="maxima", micros=0.7)
    contexts, after = [], peak
    for start, count, part in zip(starts, counts, crossed):
        context = call(
            functools.partial(attend, start, heads),
            shape((rows, count * DH), BF16),
            (part, kt, v_all, after),
            [WHOLE, WHOLE, WHOLE, OUTSIDE],
            limit=32,
            name="attend",
            micros=count * 0.12,
        )
        contexts.append(context)
        after = context
    slab = shape((peers // 2, rows + SQUARE_ROWS, out_cols), BF16)
    give, squares = call(
        project_give,
        (slab, shape((rows, LANES), F32)),
        (*contexts, w),
        name="project_give",
        micros=0.4,
    )
    keep = call(project_keep, slab, (*contexts, w, squares), name="project_keep", micros=3)
    got = lax.ppermute(give, "tp", [(i, i ^ 1) for i in range(peers)])
    peak = bind(peak, contexts[0])
    for step in reversed(steps[1:]):
        peak = call(
            larger,
            shape((1, heads), F32),
            (peak, swapped(peak, "cp", step)),
            name="larger",
            micros=5,
        )
    slab = (rows + SQUARE_ROWS, out_cols)
    mine, *others = call(
        merge, [shape(slab, F32)] + [shape(slab, BF16)] * (peers // 2 - 1), (keep, got), name="merge"
    )
    others = [
        lax.ppermute(block, "tp", [(i, (i + 2 * (step + 1)) % peers) for i in range(peers)])
        for step, block in enumerate(others)
    ]
    max_logits, kv_next = call(
        functools.partial(finish, width * peers),
        (shape((1, heads), F32), shape((rows, out_cols), BF16)),
        (peak, swapped(peak, "cp", steps[0]), mine, *others),
        name="finish",
    )
    return (max_logits, kv_next[None])


def solution(mesh):
    return jax.shard_map(
        on_device,
        mesh=mesh,
        in_specs=(
            P("pp", "cp", "tp"),
            P("pp", "cp", "tp"),
            P("pp", "cp", "tp"),
            P(),
            P("pp", "tp"),
            P("pp", "tp", None),
        ),
        out_specs=(P("pp", "tp"), P("pp", "cp", "tp")),
        check_vma=False,
    )
```

```python
import functools
import math

import jax
import jax.numpy as jnp
from jax import lax
from jax.experimental import pallas as pl
from jax.experimental.pallas import tpu as pltpu
from jax.sharding import PartitionSpec as P

DH = 128
LANES = 128
SQUARE_ROWS = 16
MASKED = -(2.0**100)
LOG2E = math.log2(math.e)
F32 = jnp.float32
BF16 = jnp.bfloat16
WHOLE = pl.BlockSpec(memory_space=pltpu.VMEM)
OUTSIDE = pl.BlockSpec(memory_space=pl.ANY)
SCALARS = pl.BlockSpec(memory_space=pltpu.SMEM)


def call(kernel, outs, args, specs=None, scratch=(), limit=16, name=None, aliases=None, micros=0):
    return pl.pallas_call(
        kernel,
        out_shape=outs,
        in_specs=specs or [WHOLE] * len(args),
        out_specs=jax.tree.map(lambda _: WHOLE, outs),
        scratch_shapes=scratch,
        name=name,
        input_output_aliases=aliases or {},
        cost_estimate=pl.CostEstimate(flops=int(micros * 1e9), bytes_accessed=0, transcendentals=0) if micros else None,
        compiler_params=pltpu.CompilerParams(vmem_limit_bytes=limit * 2**20),
    )(*args)


def partner(index, step, size):
    return (index + step) % size if size & (size - 1) else index ^ step


def swapped(block, axis, step):
    size = lax.axis_size(axis)
    return lax.ppermute(block, axis, [(i, partner(i, step, size)) for i in range(size)])


def shifted(block, axis, distance):
    size = lax.axis_size(axis)
    return lax.ppermute(block, axis, [((i - distance) % size, i) for i in range(size)])


def partner(index, step, size):
    return (index + step) % size if size & (size - 1) else index ^ step


def swapped(block, axis, step):
    size = lax.axis_size(axis)
    return lax.ppermute(block, axis, [(i, partner(i, step, size)) for i in range(size)])


def shifted(block, axis, distance):
    size = lax.axis_size(axis)
    return lax.ppermute(block, axis, [((i - distance) % size, i) for i in range(size)])


def bind_kernel(block_ref, after, out_ref):
    out_ref[...] = block_ref[...]


def bind(block, after):
    return call(
        bind_kernel, jax.ShapeDtypeStruct(block.shape, block.dtype), (block, after), [WHOLE, OUTSIDE], name="bind"
    )


def source_of(d, me, sources):
    return lax.rem(me - d + sources, sources) if sources & (sources - 1) else me ^ d


def take(first, q_ref, after, part_ref):
    part_ref[...] = q_ref[0, :, first:first + part_ref.shape[1]]


def prepare(order_ref, after, feature_ref):
    sources = lax.axis_size("cp")
    me = lax.axis_index("cp")
    rows = feature_ref.shape[2] // sources
    block = rows // 2
    feature = lax.broadcasted_iota(jnp.int32, (LANES, rows), 0)
    key = lax.broadcasted_iota(jnp.int32, (LANES, rows), 1)
    place = lax.rem(key, block)
    for side in range(2):
        mine = order_ref[2 * me + side]
        for d in range(sources):
            source = source_of(d, me, sources)
            other = jnp.where(key < block, order_ref[2 * source], order_ref[2 * source + 1])
            chosen = jnp.where(other == mine, place, jnp.where(other > mine, block, -1))
            feature_ref[side, :, d * rows:(d + 1) * rows] = jnp.where(feature == chosen, 1.0, 0.0).astype(BF16)


def touch(block_ref, out_ref):
    out_ref[...] = jnp.zeros(out_ref.shape, F32)


def join(pair_ref, here_ref, out_ref):
    width = pair_ref.shape[1]
    out_ref[:, :width] = pair_ref[...]
    out_ref[:, width:] = here_ref[:, :width // 2]


def arrange(after, feature_ref, *refs):
    triples, (kt_ref, v_ref, own_ref) = refs[-4::-1], refs[-3:]
    rows = triples[0].shape[0]
    kv_local = v_ref.shape[0]
    for g in range(kv_local):
        v_ref[g, :, DH:] = jnp.ones((v_ref.shape[1], DH), BF16)
        for ref in (kt_ref, own_ref):
            for side in range(2):
                ref[g, side, DH:, :] = feature_ref[side]
        for d, triple in enumerate(triples):
            part = slice(d * rows, (d + 1) * rows)
            for ref, first in ((kt_ref, g * DH), (own_ref, (2 * kv_local + g) * DH)):
                turned = triple[:, first:first + DH].astype(F32).T.astype(BF16)
                for side in range(2):
                    ref[g, side, :DH, part] = turned
            first = (kv_local + g) * DH
            v_ref[g, part, :DH] = triple[:, first:first + DH]


def spans(first_head, count, group, together):
    start = 0
    while start < count:
        g = (first_head + start) // group
        stop = min(start + together, count, (g + 1) * group - first_head)
        yield g, start, stop
        start = stop


def stacked(q_ref, start, stop, side):
    block = q_ref.shape[0] // 2
    shape = ((stop - start) * block, LANES)
    token = lax.rem(lax.broadcasted_iota(jnp.int32, shape, 0), block)
    lane = lax.broadcasted_iota(jnp.int32, shape, 1)
    blocked = jnp.where((lane > token) & (lane <= block), MASKED, 0.0).astype(BF16)
    tokens = slice(side * block, (side + 1) * block)
    q = jnp.concatenate([q_ref[tokens, h * DH:(h + 1) * DH] for h in range(start, stop)], axis=0)
    return jnp.concatenate([q, blocked], axis=1)


def attention_units(first_head, heads, q_ref, kt_ref, v_ref, ctx_ref):
    rows, width = q_ref.shape
    keys = v_ref.shape[1]
    block = rows // 2
    factor = LOG2E / math.sqrt(DH)
    units = [
        (g, start, stop, side)
        for g, start, stop in spans(first_head, width // DH, heads // v_ref.shape[0], max(1, 12 * 512 // keys))
        for side in range(2)
    ]

    def scores(unit):
        g, start, stop, side = unit
        return jnp.dot(stacked(q_ref, start, stop, side), kt_ref[g, side], preferred_element_type=F32)

    def finish_unit(unit, s):
        g, start, stop, side = unit
        m = jnp.max(s, axis=1, keepdims=True)
        p = jnp.exp2((s - m) * factor).astype(BF16)
        yield
        o = jnp.dot(p, v_ref[g], preferred_element_type=F32)
        o = (o[:, :DH] * (1.0 / o[:, DH:])).astype(BF16)
        for j in range(stop - start):
            ctx_ref[side * block:(side + 1) * block, (start + j) * DH:(start + j + 1) * DH] = o[
                j * block:(j + 1) * block, :
            ]

    ahead = [scores(unit) for unit in units[:2]]
    for n, unit in enumerate(units):
        yield from finish_unit(unit, ahead.pop(0))
        if n + 2 < len(units):
            ahead.append(scores(units[n + 2]))


def maxima_units(q_ref, own_ref, peak_ref):
    block = q_ref.shape[0] // 2
    heads = q_ref.shape[1] // DH
    keys = own_ref.shape[3]
    for g, start, stop in spans(0, heads, heads // own_ref.shape[0], max(1, 8 * 512 // keys)):
        tops = []
        for side in range(2):
            s = jnp.dot(stacked(q_ref, start, stop, side), own_ref[g, side], preferred_element_type=F32)
            yield
            top = s[:, :LANES]
            for c in range(LANES, keys, LANES):
                top = jnp.maximum(top, s[:, c:c + LANES])
            tops.append(top)
        top = jnp.maximum(*tops)
        for j in range(stop - start):
            one = jnp.max(top[j * block:(j + 1) * block, :], axis=0, keepdims=True)
            h = start + j
            peak_ref[:, h:h + 1] = jnp.max(one, axis=1, keepdims=True) * (1.0 / math.sqrt(DH))


def interleave(*streams):
    streams = list(streams)
    while streams:
        for stream in list(streams):
            if next(stream, stream) is stream:
                streams.remove(stream)


def attend_first(heads, w_ref, feature_ref, *refs):
    triples, refs = refs[:-7], refs[-7:]
    mine_ref, q_ref, kt_ref, v_ref, ctx_ref, peak_ref, own_ref = refs
    arrange(None, feature_ref, *triples, kt_ref, v_ref, own_ref)
    interleave(
        attention_units(0, heads, q_ref, kt_ref, v_ref, ctx_ref), maxima_units(mine_ref.at[0], own_ref, peak_ref)
    )


def attend_last(first_head, heads, q_ref, kt_ref, v_ref, first_ref, w_ref, ctx_ref, give_ref, square_ref):
    interleave(attention_units(first_head, heads, q_ref, kt_ref, v_ref, ctx_ref))
    project_give(first_ref, ctx_ref, w_ref, give_ref, square_ref)


def weigh(w_ref, gain_ref, after, out_ref):
    features, columns = w_ref.shape
    for f in range(0, features, LANES):
        gain = jnp.broadcast_to(gain_ref[:, f:f + LANES].astype(F32), (LANES, LANES)).T
        for c in range(0, columns, LANES):
            out_ref[f:f + LANES, c:c + LANES] = (w_ref[f:f + LANES, c:c + LANES].astype(F32) * gain).astype(BF16)


def square_sums(ctx_ref):
    total = None
    for c in range(0, ctx_ref.shape[1], LANES):
        wide = ctx_ref[:, c:c + LANES].astype(F32)
        total = wide * wide if total is None else total + wide * wide
    return jnp.broadcast_to(jnp.sum(total, axis=1, keepdims=True), total.shape)


def columns_of(y, side, cols):
    return pl.ds(pl.multiple_of((2 * y + side) * cols, cols), cols)


def fill(ref, y, part, squares):
    rows, cols = part.shape
    lanes = squares.T[:SQUARE_ROWS, :]
    first = lanes.astype(BF16)
    rest = (lanes - first.astype(F32)).astype(BF16)
    ref[y, :rows, :] = part.astype(BF16)
    ref[y, rows:, :rows] = first
    ref[y, rows:, rows:2 * rows] = rest
    if cols > 2 * rows:
        ref[y, rows:, 2 * rows:] = jnp.zeros((SQUARE_ROWS, cols - 2 * rows), BF16)


def product(first_ref, last_ref, w_ref, at):
    cut = first_ref.shape[1]
    part = jnp.dot(first_ref[...], w_ref[:cut, at], preferred_element_type=F32)
    return part + jnp.dot(last_ref[...], w_ref[cut:, at], preferred_element_type=F32)


def project_give(first_ref, last_ref, w_ref, give_ref, square_ref):
    other = 1 - lax.rem(lax.axis_index("tp"), 2)
    squares = square_sums(first_ref) + square_sums(last_ref)
    square_ref[...] = squares
    for y in range(give_ref.shape[0]):
        fill(give_ref, y, product(first_ref, last_ref, w_ref, columns_of(y, other, give_ref.shape[2])), squares)


def project_keep(first_ref, last_ref, w_ref, square_ref, keep_ref):
    core = lax.rem(lax.axis_index("tp"), 2)
    for y in range(keep_ref.shape[0]):
        at = columns_of(y, core, keep_ref.shape[2])
        fill(keep_ref, y, product(first_ref, last_ref, w_ref, at), square_ref[...])


def larger(left_ref, right_ref, out_ref):
    out_ref[...] = jnp.maximum(left_ref[...], right_ref[...])


def merge(keep_ref, got_ref, *give_refs):
    groups = keep_ref.shape[0]
    mine = lax.axis_index("tp") // 2
    for step, ref in enumerate(give_refs):
        y = lax.rem(mine + step, groups)
        total = keep_ref[y].astype(F32) + got_ref[y].astype(F32)
        ref[...] = total.astype(ref.dtype)


def finish(features, peak_ref, peak_got, keep_ref, *refs):
    peak_out, out_ref = refs[-2:]
    peak_out[...] = jnp.maximum(peak_ref[...], peak_got[...])
    rows = out_ref.shape[0]
    total = keep_ref[...]
    for ref in refs[:-2]:
        total = total + ref[...].astype(F32)
    squares = total[rows:rows + 8, :rows] + total[rows:rows + 8, rows:2 * rows]
    inverse = lax.rsqrt(squares / features + 1e-05)
    column = jnp.broadcast_to(inverse[:1, :], (rows, rows)).T[:, :1]
    out_ref[...] = (total[:rows, :] * column).astype(BF16)


def on_device(queries, key_vectors, value_vectors, block_order, norm_gain, kv_weight):
    rows, width = queries.shape[1:]
    heads = width // DH
    peers = lax.axis_size("tp")
    sources = lax.axis_size("cp")
    kv_width = key_vectors.shape[2]
    columns = kv_weight.shape[2]
    out_cols = columns // peers
    shape = jax.ShapeDtypeStruct
    steps = [2**i for i in range((sources - 1).bit_length())]

    pair_here = jnp.concatenate([key_vectors[0], value_vectors[0]], axis=1)
    pair = shifted(pair_here, "pp", 1)
    cut = heads // 2
    counts = [cut, heads - cut]
    starts = [0, cut]
    crossed = []

    def cross(start, count, after, micros):
        part = call(
            functools.partial(take, start * DH),
            shape((rows, count * DH), BF16),
            (queries, after),
            [WHOLE, OUTSIDE],
            name="take",
            micros=micros,
        )
        crossed.append(shifted(part, "pp", 1))

    mark = call(touch, shape((8, LANES), F32), (pair_here,), [OUTSIDE], name="touch", micros=3)
    cross(starts[0], counts[0], mark, 3)
    triple = call(join, shape((rows, 3 * kv_width), BF16), (pair, pair_here), name="join")
    moved = {d: swapped(triple, "cp", d) for d in reversed(range(1, sources))}
    triples = [triple] + [moved[d] for d in range(1, sources)]
    cross(starts[1], counts[1], triple, 0)
    features = call(
        prepare,
        shape((2, LANES, sources * rows), BF16),
        (block_order, mark),
        [SCALARS, OUTSIDE],
        name="prepare",
        micros=3,
    )
    w = call(
        weigh,
        shape((width, columns), BF16),
        (kv_weight[0], norm_gain, moved[sources - 1]),
        [WHOLE, WHOLE, OUTSIDE],
        name="weigh",
        micros=1,
    )
    kv_local = kv_width // DH
    turned = shape((kv_local, 2, DH + LANES, sources * rows), BF16)
    kt, v_all, first_context, peak = call(
        functools.partial(attend_first, heads),
        (
            turned,
            shape((kv_local, sources * rows, 2 * DH), BF16),
            shape((rows, counts[0] * DH), BF16),
            shape((1, heads), F32),
        ),
        (w, features, *reversed(triples), queries, crossed[0]),
        [OUTSIDE] + [WHOLE] * (3 + sources),
        scratch=[pltpu.VMEM(turned.shape, BF16)],
        limit=36,
        name="attend_first",
        micros=2,
    )
    slab = shape((peers // 2, rows + SQUARE_ROWS, out_cols), BF16)
    last_context, give, squares = call(
        functools.partial(attend_last, starts[1], heads),
        (shape((rows, counts[1] * DH), BF16), slab, shape((rows, LANES), F32)),
        (crossed[1], kt, v_all, first_context, w),
        limit=32,
        name="attend_last",
        micros=1.5,
    )
    contexts = [first_context, last_context]
    keep = call(project_keep, slab, (*contexts, w, squares), name="project_keep", micros=3)
    got = lax.ppermute(give, "tp", [(i, i ^ 1) for i in range(peers)])
    for step in reversed(steps[1:]):
        peak = call(
            larger,
            shape((1, heads), F32),
            (peak, swapped(peak, "cp", step)),
            name="larger",
            micros=5,
        )
    slab = (rows + SQUARE_ROWS, out_cols)
    mine, *others = call(
        merge, [shape(slab, F32)] + [shape(slab, BF16)] * (peers // 2 - 1), (keep, got), name="merge"
    )
    others = [
        lax.ppermute(block, "tp", [(i, (i + 2 * (step + 1)) % peers) for i in range(peers)])
        for step, block in enumerate(others)
    ]
    max_logits, kv_next = call(
        functools.partial(finish, width * peers),
        (shape((1, heads), F32), shape((rows, out_cols), BF16)),
        (peak, swapped(peak, "cp", steps[0]), mine, *others),
        name="finish",
    )
    return (max_logits, kv_next[None])


def solution(mesh):
    return jax.shard_map(
        on_device,
        mesh=mesh,
        in_specs=(
            P("pp", "cp", "tp"),
            P("pp", "cp", "tp"),
            P("pp", "cp", "tp"),
            P(),
            P("pp", "tp"),
            P("pp", "tp", None),
        ),
        out_specs=(P("pp", "tp"), P("pp", "cp", "tp")),
        check_vma=False,
    )
```

```python
import functools
import math

import jax
import jax.numpy as jnp
from jax import lax
from jax.experimental import pallas as pl
from jax.experimental.pallas import tpu as pltpu
from jax.sharding import PartitionSpec as P

DH = 128
LANES = 128
SQUARE_ROWS = 16
MASKED = -(2.0**100)
LOG2E = math.log2(math.e)
F32 = jnp.float32
BF16 = jnp.bfloat16
WHOLE = pl.BlockSpec(memory_space=pltpu.VMEM)
OUTSIDE = pl.BlockSpec(memory_space=pl.ANY)
SCALARS = pl.BlockSpec(memory_space=pltpu.SMEM)


def call(kernel, outs, args, specs=None, scratch=(), limit=16, name=None, aliases=None, micros=0):
    return pl.pallas_call(
        kernel,
        out_shape=outs,
        in_specs=specs or [WHOLE] * len(args),
        out_specs=jax.tree.map(lambda _: WHOLE, outs),
        scratch_shapes=scratch,
        name=name,
        input_output_aliases=aliases or {},
        cost_estimate=pl.CostEstimate(flops=int(micros * 1e9), bytes_accessed=0, transcendentals=0) if micros else None,
        compiler_params=pltpu.CompilerParams(vmem_limit_bytes=limit * 2**20),
    )(*args)


def partner(index, step, size):
    return (index + step) % size if size & (size - 1) else index ^ step


def swapped(block, axis, step):
    size = lax.axis_size(axis)
    return lax.ppermute(block, axis, [(i, partner(i, step, size)) for i in range(size)])


def shifted(block, axis, distance):
    size = lax.axis_size(axis)
    return lax.ppermute(block, axis, [((i - distance) % size, i) for i in range(size)])


def partner(index, step, size):
    return (index + step) % size if size & (size - 1) else index ^ step


def swapped(block, axis, step):
    size = lax.axis_size(axis)
    return lax.ppermute(block, axis, [(i, partner(i, step, size)) for i in range(size)])


def shifted(block, axis, distance):
    size = lax.axis_size(axis)
    return lax.ppermute(block, axis, [((i - distance) % size, i) for i in range(size)])


def bind_kernel(block_ref, after, out_ref):
    out_ref[...] = block_ref[...]


def bind(block, after):
    return call(
        bind_kernel, jax.ShapeDtypeStruct(block.shape, block.dtype), (block, after), [WHOLE, OUTSIDE], name="bind"
    )


def source_of(d, me, sources):
    return lax.rem(me - d + sources, sources) if sources & (sources - 1) else me ^ d


def take(first, q_ref, after, part_ref):
    part_ref[...] = q_ref[0, :, first:first + part_ref.shape[1]]


def prepare(order_ref, after, feature_ref):
    sources = lax.axis_size("cp")
    me = lax.axis_index("cp")
    rows = feature_ref.shape[2] // sources
    block = rows // 2
    feature = lax.broadcasted_iota(jnp.int32, (LANES, rows), 0)
    key = lax.broadcasted_iota(jnp.int32, (LANES, rows), 1)
    place = lax.rem(key, block)
    for side in range(2):
        mine = order_ref[2 * me + side]
        for d in range(sources):
            source = source_of(d, me, sources)
            other = jnp.where(key < block, order_ref[2 * source], order_ref[2 * source + 1])
            chosen = jnp.where(other == mine, place, jnp.where(other > mine, block, -1))
            feature_ref[side, :, d * rows:(d + 1) * rows] = jnp.where(feature == chosen, 1.0, 0.0).astype(BF16)


def touch(block_ref, out_ref):
    out_ref[...] = jnp.zeros(out_ref.shape, F32)


def join(pair_ref, here_ref, out_ref):
    width = pair_ref.shape[1]
    out_ref[:, :width] = pair_ref[...]
    out_ref[:, width:] = here_ref[:, :width // 2]


def arrange(after, feature_ref, *refs):
    triples, (kt_ref, v_ref, own_ref) = refs[-4::-1], refs[-3:]
    rows = triples[0].shape[0]
    kv_local = v_ref.shape[0]
    for g in range(kv_local):
        v_ref[g, :, DH:] = jnp.ones((v_ref.shape[1], DH), BF16)
        for ref in (kt_ref, own_ref):
            for side in range(2):
                ref[g, side, DH:, :] = feature_ref[side]
        for d, triple in enumerate(triples):
            part = slice(d * rows, (d + 1) * rows)
            for ref, first in ((kt_ref, g * DH), (own_ref, (2 * kv_local + g) * DH)):
                turned = triple[:, first:first + DH].astype(F32).T.astype(BF16)
                for side in range(2):
                    ref[g, side, :DH, part] = turned
            first = (kv_local + g) * DH
            v_ref[g, part, :DH] = triple[:, first:first + DH]


def spans(first_head, count, group, together):
    start = 0
    while start < count:
        g = (first_head + start) // group
        stop = min(start + together, count, (g + 1) * group - first_head)
        yield g, start, stop
        start = stop


def stacked(q_ref, start, stop, side):
    block = q_ref.shape[0] // 2
    shape = ((stop - start) * block, LANES)
    token = lax.rem(lax.broadcasted_iota(jnp.int32, shape, 0), block)
    lane = lax.broadcasted_iota(jnp.int32, shape, 1)
    blocked = jnp.where((lane > token) & (lane <= block), MASKED, 0.0).astype(BF16)
    tokens = slice(side * block, (side + 1) * block)
    q = jnp.concatenate([q_ref[tokens, h * DH:(h + 1) * DH] for h in range(start, stop)], axis=0)
    return jnp.concatenate([q, blocked], axis=1)


def attention_units(first_head, heads, q_ref, kt_ref, v_ref, ctx_ref):
    rows, width = q_ref.shape
    keys = v_ref.shape[1]
    block = rows // 2
    factor = LOG2E / math.sqrt(DH)
    units = [
        (g, start, stop, side)
        for g, start, stop in spans(first_head, width // DH, heads // v_ref.shape[0], max(1, 12 * 512 // keys))
        for side in range(2)
    ]

    def scores(unit):
        g, start, stop, side = unit
        return jnp.dot(stacked(q_ref, start, stop, side), kt_ref[g, side], preferred_element_type=F32)

    def finish_unit(unit, s):
        g, start, stop, side = unit
        m = jnp.max(s, axis=1, keepdims=True)
        p = jnp.exp2((s - m) * factor).astype(BF16)
        yield
        o = jnp.dot(p, v_ref[g], preferred_element_type=F32)
        o = (o[:, :DH] * (1.0 / o[:, DH:])).astype(BF16)
        for j in range(stop - start):
            ctx_ref[side * block:(side + 1) * block, (start + j) * DH:(start + j + 1) * DH] = o[
                j * block:(j + 1) * block, :
            ]

    ahead = [scores(unit) for unit in units[:2]]
    for n, unit in enumerate(units):
        yield from finish_unit(unit, ahead.pop(0))
        if n + 2 < len(units):
            ahead.append(scores(units[n + 2]))


def maxima_units(q_ref, own_ref, peak_ref):
    block = q_ref.shape[0] // 2
    heads = q_ref.shape[1] // DH
    keys = own_ref.shape[3]
    for g, start, stop in spans(0, heads, heads // own_ref.shape[0], max(1, 8 * 512 // keys)):
        tops = []
        for side in range(2):
            s = jnp.dot(stacked(q_ref, start, stop, side), own_ref[g, side], preferred_element_type=F32)
            yield
            top = s[:, :LANES]
            for c in range(LANES, keys, LANES):
                top = jnp.maximum(top, s[:, c:c + LANES])
            tops.append(top)
        top = jnp.maximum(*tops)
        for j in range(stop - start):
            one = jnp.max(top[j * block:(j + 1) * block, :], axis=0, keepdims=True)
            h = start + j
            peak_ref[:, h:h + 1] = jnp.max(one, axis=1, keepdims=True) * (1.0 / math.sqrt(DH))


def interleave(*streams):
    streams = list(streams)
    while streams:
        for stream in list(streams):
            if next(stream, stream) is stream:
                streams.remove(stream)


def attend_first(heads, w_ref, feature_ref, *refs):
    triples, refs = refs[:-7], refs[-7:]
    mine_ref, q_ref, kt_ref, v_ref, ctx_ref, peak_ref, own_ref = refs
    arrange(None, feature_ref, *triples, kt_ref, v_ref, own_ref)
    interleave(
        attention_units(0, heads, q_ref, kt_ref, v_ref, ctx_ref), maxima_units(mine_ref.at[0], own_ref, peak_ref)
    )


def product_units(ctx_ref, w_ref, sums):
    other = 1 - lax.rem(lax.axis_index("tp"), 2)
    for y in range(sums.shape[0]):
        w = w_ref[:ctx_ref.shape[1], columns_of(y, other, sums.shape[2])]
        sums[y] = jnp.dot(ctx_ref[...], w, preferred_element_type=F32)
        yield


def attend_last(first_head, heads, q_ref, kt_ref, v_ref, first_ref, w_ref, ctx_ref, give_ref, square_ref, sums):
    interleave(
        attention_units(first_head, heads, q_ref, kt_ref, v_ref, ctx_ref), product_units(first_ref, w_ref, sums)
    )
    other = 1 - lax.rem(lax.axis_index("tp"), 2)
    squares = square_sums(first_ref) + square_sums(ctx_ref)
    square_ref[...] = squares
    for y in range(give_ref.shape[0]):
        w = w_ref[first_ref.shape[1]:, columns_of(y, other, give_ref.shape[2])]
        fill(give_ref, y, sums[y] + jnp.dot(ctx_ref[...], w, preferred_element_type=F32), squares)


def weigh(w_ref, gain_ref, after, out_ref):
    features, columns = w_ref.shape
    for f in range(0, features, LANES):
        gain = jnp.broadcast_to(gain_ref[:, f:f + LANES].astype(F32), (LANES, LANES)).T
        for c in range(0, columns, LANES):
            out_ref[f:f + LANES, c:c + LANES] = (w_ref[f:f + LANES, c:c + LANES].astype(F32) * gain).astype(BF16)


def square_sums(ctx_ref):
    total = None
    for c in range(0, ctx_ref.shape[1], LANES):
        wide = ctx_ref[:, c:c + LANES].astype(F32)
        total = wide * wide if total is None else total + wide * wide
    return jnp.broadcast_to(jnp.sum(total, axis=1, keepdims=True), total.shape)


def columns_of(y, side, cols):
    return pl.ds(pl.multiple_of((2 * y + side) * cols, cols), cols)


def fill(ref, y, part, squares):
    rows, cols = part.shape
    lanes = squares.T[:SQUARE_ROWS, :]
    first = lanes.astype(BF16)
    rest = (lanes - first.astype(F32)).astype(BF16)
    ref[y, :rows, :] = part.astype(BF16)
    ref[y, rows:, :rows] = first
    ref[y, rows:, rows:2 * rows] = rest
    if cols > 2 * rows:
        ref[y, rows:, 2 * rows:] = jnp.zeros((SQUARE_ROWS, cols - 2 * rows), BF16)


def product(first_ref, last_ref, w_ref, at):
    cut = first_ref.shape[1]
    part = jnp.dot(first_ref[...], w_ref[:cut, at], preferred_element_type=F32)
    return part + jnp.dot(last_ref[...], w_ref[cut:, at], preferred_element_type=F32)


def project_keep(first_ref, last_ref, w_ref, square_ref, keep_ref):
    core = lax.rem(lax.axis_index("tp"), 2)
    for y in range(keep_ref.shape[0]):
        at = columns_of(y, core, keep_ref.shape[2])
        fill(keep_ref, y, product(first_ref, last_ref, w_ref, at), square_ref[...])


def larger(left_ref, right_ref, out_ref):
    out_ref[...] = jnp.maximum(left_ref[...], right_ref[...])


def merge(keep_ref, got_ref, *give_refs):
    groups = keep_ref.shape[0]
    mine = lax.axis_index("tp") // 2
    for step, ref in enumerate(give_refs):
        y = lax.rem(mine + step, groups)
        total = keep_ref[y].astype(F32) + got_ref[y].astype(F32)
        ref[...] = total.astype(ref.dtype)


def finish(features, peak_ref, peak_got, keep_ref, *refs):
    peak_out, out_ref = refs[-2:]
    peak_out[...] = jnp.maximum(peak_ref[...], peak_got[...])
    rows = out_ref.shape[0]
    total = keep_ref[...]
    for ref in refs[:-2]:
        total = total + ref[...].astype(F32)
    squares = total[rows:rows + 8, :rows] + total[rows:rows + 8, rows:2 * rows]
    inverse = lax.rsqrt(squares / features + 1e-05)
    column = jnp.broadcast_to(inverse[:1, :], (rows, rows)).T[:, :1]
    out_ref[...] = (total[:rows, :] * column).astype(BF16)


def on_device(queries, key_vectors, value_vectors, block_order, norm_gain, kv_weight):
    rows, width = queries.shape[1:]
    heads = width // DH
    peers = lax.axis_size("tp")
    sources = lax.axis_size("cp")
    kv_width = key_vectors.shape[2]
    columns = kv_weight.shape[2]
    out_cols = columns // peers
    shape = jax.ShapeDtypeStruct
    steps = [2**i for i in range((sources - 1).bit_length())]

    pair_here = jnp.concatenate([key_vectors[0], value_vectors[0]], axis=1)
    pair = shifted(pair_here, "pp", 1)
    cut = heads // 2
    counts = [cut, heads - cut]
    starts = [0, cut]
    crossed = []

    def cross(start, count, after, micros):
        part = call(
            functools.partial(take, start * DH),
            shape((rows, count * DH), BF16),
            (queries, after),
            [WHOLE, OUTSIDE],
            name="take",
            micros=micros,
        )
        crossed.append(shifted(part, "pp", 1))

    mark = call(touch, shape((8, LANES), F32), (pair_here,), [OUTSIDE], name="touch", micros=3)
    cross(starts[0], counts[0], mark, 3)
    triple = call(join, shape((rows, 3 * kv_width), BF16), (pair, pair_here), name="join")
    moved = {d: swapped(triple, "cp", d) for d in reversed(range(1, sources))}
    triples = [triple] + [moved[d] for d in range(1, sources)]
    cross(starts[1], counts[1], triple, 0)
    features = call(
        prepare,
        shape((2, LANES, sources * rows), BF16),
        (block_order, mark),
        [SCALARS, OUTSIDE],
        name="prepare",
        micros=3,
    )
    w = call(
        weigh,
        shape((width, columns), BF16),
        (kv_weight[0], norm_gain, moved[sources - 1]),
        [WHOLE, WHOLE, OUTSIDE],
        name="weigh",
        micros=1,
    )
    kv_local = kv_width // DH
    turned = shape((kv_local, 2, DH + LANES, sources * rows), BF16)
    kt, v_all, first_context, peak = call(
        functools.partial(attend_first, heads),
        (
            turned,
            shape((kv_local, sources * rows, 2 * DH), BF16),
            shape((rows, counts[0] * DH), BF16),
            shape((1, heads), F32),
        ),
        (w, features, *reversed(triples), queries, crossed[0]),
        [OUTSIDE] + [WHOLE] * (3 + sources),
        scratch=[pltpu.VMEM(turned.shape, BF16)],
        limit=36,
        name="attend_first",
        micros=2,
    )
    slab = shape((peers // 2, rows + SQUARE_ROWS, out_cols), BF16)
    last_context, give, squares = call(
        functools.partial(attend_last, starts[1], heads),
        (shape((rows, counts[1] * DH), BF16), slab, shape((rows, LANES), F32)),
        (crossed[1], kt, v_all, first_context, w),
        scratch=[pltpu.VMEM((peers // 2, rows, out_cols), F32)],
        limit=32,
        name="attend_last",
        micros=1.5,
    )
    contexts = [first_context, last_context]
    keep = call(project_keep, slab, (*contexts, w, squares), name="project_keep", micros=3)
    got = lax.ppermute(give, "tp", [(i, i ^ 1) for i in range(peers)])
    for step in steps[:-1]:
        peak = call(
            larger,
            shape((1, heads), F32),
            (peak, swapped(peak, "cp", step)),
            name="larger",
            micros=5,
        )
    slab = (rows + SQUARE_ROWS, out_cols)
    mine, *others = call(
        merge, [shape(slab, F32)] + [shape(slab, BF16)] * (peers // 2 - 1), (keep, got), name="merge"
    )
    others = [
        lax.ppermute(block, "tp", [(i, (i + 2 * (step + 1)) % peers) for i in range(peers)])
        for step, block in enumerate(others)
    ]
    max_logits, kv_next = call(
        functools.partial(finish, width * peers),
        (shape((1, heads), F32), shape((rows, out_cols), BF16)),
        (peak, swapped(peak, "cp", steps[-1]), mine, *others),
        name="finish",
    )
    return (max_logits, kv_next[None])


def solution(mesh):
    return jax.shard_map(
        on_device,
        mesh=mesh,
        in_specs=(
            P("pp", "cp", "tp"),
            P("pp", "cp", "tp"),
            P("pp", "cp", "tp"),
            P(),
            P("pp", "tp"),
            P("pp", "tp", None),
        ),
        out_specs=(P("pp", "tp"), P("pp", "cp", "tp")),
        check_vma=False,
    )
```

```python
import functools
import math

import jax
import jax.numpy as jnp
from jax import lax
from jax.experimental import pallas as pl
from jax.experimental.pallas import tpu as pltpu
from jax.sharding import PartitionSpec as P

DH = 128
LANES = 128
SQUARE_ROWS = 16
MASKED = -(2.0**100)
LOG2E = math.log2(math.e)
F32 = jnp.float32
BF16 = jnp.bfloat16
WHOLE = pl.BlockSpec(memory_space=pltpu.VMEM)
OUTSIDE = pl.BlockSpec(memory_space=pl.ANY)
SCALARS = pl.BlockSpec(memory_space=pltpu.SMEM)


def call(kernel, outs, args, specs=None, scratch=(), limit=16, name=None, aliases=None, micros=0):
    return pl.pallas_call(
        kernel,
        out_shape=outs,
        in_specs=specs or [WHOLE] * len(args),
        out_specs=jax.tree.map(lambda _: WHOLE, outs),
        scratch_shapes=scratch,
        name=name,
        input_output_aliases=aliases or {},
        cost_estimate=pl.CostEstimate(flops=int(micros * 1e9), bytes_accessed=0, transcendentals=0) if micros else None,
        compiler_params=pltpu.CompilerParams(vmem_limit_bytes=limit * 2**20),
    )(*args)


def partner(index, step, size):
    return (index + step) % size if size & (size - 1) else index ^ step


def swapped(block, axis, step):
    size = lax.axis_size(axis)
    return lax.ppermute(block, axis, [(i, partner(i, step, size)) for i in range(size)])


def shifted(block, axis, distance):
    size = lax.axis_size(axis)
    return lax.ppermute(block, axis, [((i - distance) % size, i) for i in range(size)])


def partner(index, step, size):
    return (index + step) % size if size & (size - 1) else index ^ step


def swapped(block, axis, step):
    size = lax.axis_size(axis)
    return lax.ppermute(block, axis, [(i, partner(i, step, size)) for i in range(size)])


def shifted(block, axis, distance):
    size = lax.axis_size(axis)
    return lax.ppermute(block, axis, [((i - distance) % size, i) for i in range(size)])


def bind_kernel(block_ref, after, out_ref):
    out_ref[...] = block_ref[...]


def bind(block, after):
    return call(
        bind_kernel, jax.ShapeDtypeStruct(block.shape, block.dtype), (block, after), [WHOLE, OUTSIDE], name="bind"
    )


def source_of(d, me, sources):
    return lax.rem(me - d + sources, sources) if sources & (sources - 1) else me ^ d


def take(first, q_ref, after, part_ref):
    part_ref[...] = q_ref[0, :, first:first + part_ref.shape[1]]


def prepare(order_ref, after, feature_ref):
    sources = lax.axis_size("cp")
    me = lax.axis_index("cp")
    rows = feature_ref.shape[2] // sources
    block = rows // 2
    feature = lax.broadcasted_iota(jnp.int32, (LANES, rows), 0)
    key = lax.broadcasted_iota(jnp.int32, (LANES, rows), 1)
    place = lax.rem(key, block)
    for side in range(2):
        mine = order_ref[2 * me + side]
        for d in range(sources):
            source = source_of(d, me, sources)
            other = jnp.where(key < block, order_ref[2 * source], order_ref[2 * source + 1])
            chosen = jnp.where(other == mine, place, jnp.where(other > mine, block, -1))
            feature_ref[side, :, d * rows:(d + 1) * rows] = jnp.where(feature == chosen, 1.0, 0.0).astype(BF16)


def touch(block_ref, out_ref):
    out_ref[...] = jnp.zeros(out_ref.shape, F32)


def join(pair_ref, here_ref, out_ref):
    width = pair_ref.shape[1]
    out_ref[:, :width] = pair_ref[...]
    out_ref[:, width:] = here_ref[:, :width // 2]


def arrange(after, feature_ref, *refs):
    triples, (kt_ref, v_ref, own_ref) = refs[-4::-1], refs[-3:]
    rows = triples[0].shape[0]
    kv_local = v_ref.shape[0]
    for g in range(kv_local):
        v_ref[g, :, DH:] = jnp.ones((v_ref.shape[1], DH), BF16)
        for ref in (kt_ref, own_ref):
            for side in range(2):
                ref[g, side, DH:, :] = feature_ref[side]
        for d, triple in enumerate(triples):
            part = slice(d * rows, (d + 1) * rows)
            for ref, first in ((kt_ref, g * DH), (own_ref, (2 * kv_local + g) * DH)):
                turned = triple[:, first:first + DH].astype(F32).T.astype(BF16)
                for side in range(2):
                    ref[g, side, :DH, part] = turned
            first = (kv_local + g) * DH
            v_ref[g, part, :DH] = triple[:, first:first + DH]


def spans(first_head, count, group, together):
    start = 0
    while start < count:
        g = (first_head + start) // group
        stop = min(start + together, count, (g + 1) * group - first_head)
        yield g, start, stop
        start = stop


def stacked(q_ref, start, stop, side):
    block = q_ref.shape[0] // 2
    shape = ((stop - start) * block, LANES)
    token = lax.rem(lax.broadcasted_iota(jnp.int32, shape, 0), block)
    lane = lax.broadcasted_iota(jnp.int32, shape, 1)
    blocked = jnp.where((lane > token) & (lane <= block), MASKED, 0.0).astype(BF16)
    tokens = slice(side * block, (side + 1) * block)
    q = jnp.concatenate([q_ref[tokens, h * DH:(h + 1) * DH] for h in range(start, stop)], axis=0)
    return jnp.concatenate([q, blocked], axis=1)


def attention_units(first_head, heads, q_ref, kt_ref, v_ref, ctx_ref):
    rows, width = q_ref.shape
    keys = v_ref.shape[1]
    block = rows // 2
    factor = LOG2E / math.sqrt(DH)
    units = [
        (g, start, stop, side)
        for g, start, stop in spans(first_head, width // DH, heads // v_ref.shape[0], max(1, 12 * 512 // keys))
        for side in range(2)
    ]

    def scores(unit):
        g, start, stop, side = unit
        return jnp.dot(stacked(q_ref, start, stop, side), kt_ref[g, side], preferred_element_type=F32)

    def finish_unit(unit, s):
        g, start, stop, side = unit
        m = jnp.max(s, axis=1, keepdims=True)
        p = jnp.exp2((s - m) * factor).astype(BF16)
        yield
        o = jnp.dot(p, v_ref[g], preferred_element_type=F32)
        o = (o[:, :DH] * (1.0 / o[:, DH:])).astype(BF16)
        for j in range(stop - start):
            ctx_ref[side * block:(side + 1) * block, (start + j) * DH:(start + j + 1) * DH] = o[
                j * block:(j + 1) * block, :
            ]

    ahead = [scores(unit) for unit in units[:2]]
    for n, unit in enumerate(units):
        yield from finish_unit(unit, ahead.pop(0))
        if n + 2 < len(units):
            ahead.append(scores(units[n + 2]))


def maxima_units(q_ref, own_ref, peak_ref):
    block = q_ref.shape[0] // 2
    heads = q_ref.shape[1] // DH
    keys = own_ref.shape[3]
    for g, start, stop in spans(0, heads, heads // own_ref.shape[0], max(1, 8 * 512 // keys)):
        tops = []
        for side in range(2):
            s = jnp.dot(stacked(q_ref, start, stop, side), own_ref[g, side], preferred_element_type=F32)
            yield
            top = s[:, :LANES]
            for c in range(LANES, keys, LANES):
                top = jnp.maximum(top, s[:, c:c + LANES])
            tops.append(top)
        top = jnp.maximum(*tops)
        for j in range(stop - start):
            one = jnp.max(top[j * block:(j + 1) * block, :], axis=0, keepdims=True)
            h = start + j
            peak_ref[:, h:h + 1] = jnp.max(one, axis=1, keepdims=True) * (1.0 / math.sqrt(DH))


def interleave(*streams):
    streams = list(streams)
    while streams:
        for stream in list(streams):
            if next(stream, stream) is stream:
                streams.remove(stream)


def attend_first(heads, w_ref, feature_ref, *refs):
    triples, refs = refs[:-7], refs[-7:]
    mine_ref, q_ref, kt_ref, v_ref, ctx_ref, peak_ref, own_ref = refs
    arrange(None, feature_ref, *triples, kt_ref, v_ref, own_ref)
    interleave(
        attention_units(0, heads, q_ref, kt_ref, v_ref, ctx_ref), maxima_units(mine_ref.at[0], own_ref, peak_ref)
    )


def attend_last(
    first_head, heads, q_ref, kt_ref, v_ref, first_ref, w_ref, ctx_ref, far_ref, near_ref, square_ref
):
    interleave(attention_units(first_head, heads, q_ref, kt_ref, v_ref, ctx_ref))
    squares = square_sums(first_ref) + square_sums(ctx_ref)
    square_ref[...] = squares
    other = 1 - lax.rem(lax.axis_index("tp"), 2)
    project(first_ref, ctx_ref, w_ref, other, 1, squares, far_ref)
    project(first_ref, ctx_ref, w_ref, other, 0, squares, near_ref)


def weigh(w_ref, gain_ref, after, out_ref):
    features, columns = w_ref.shape
    for f in range(0, features, LANES):
        gain = jnp.broadcast_to(gain_ref[:, f:f + LANES].astype(F32), (LANES, LANES)).T
        for c in range(0, columns, LANES):
            out_ref[f:f + LANES, c:c + LANES] = (w_ref[f:f + LANES, c:c + LANES].astype(F32) * gain).astype(BF16)


def square_sums(ctx_ref):
    total = None
    for c in range(0, ctx_ref.shape[1], LANES):
        wide = ctx_ref[:, c:c + LANES].astype(F32)
        total = wide * wide if total is None else total + wide * wide
    return jnp.broadcast_to(jnp.sum(total, axis=1, keepdims=True), total.shape)


def columns_of(y, side, cols):
    return pl.ds(pl.multiple_of((2 * y + side) * cols, cols), cols)


def fill(ref, y, part, squares):
    rows, cols = part.shape
    lanes = squares.T[:SQUARE_ROWS, :]
    first = lanes.astype(BF16)
    rest = (lanes - first.astype(F32)).astype(BF16)
    ref[y, :rows, :] = part.astype(BF16)
    ref[y, rows:, :rows] = first
    ref[y, rows:, rows:2 * rows] = rest
    if cols > 2 * rows:
        ref[y, rows:, 2 * rows:] = jnp.zeros((SQUARE_ROWS, cols - 2 * rows), BF16)


def product(first_ref, last_ref, w_ref, at):
    cut = first_ref.shape[1]
    part = jnp.dot(first_ref[...], w_ref[:cut, at], preferred_element_type=F32)
    return part + jnp.dot(last_ref[...], w_ref[cut:, at], preferred_element_type=F32)


def project(first_ref, last_ref, w_ref, side, step, squares, out_ref):
    groups = w_ref.shape[1] // (2 * out_ref.shape[2])
    mine = lax.axis_index("tp") // 2
    for n in range(out_ref.shape[0]):
        at = columns_of(lax.rem(mine + step + n, groups), side, out_ref.shape[2])
        fill(out_ref, n, product(first_ref, last_ref, w_ref, at), squares)


def project_keep(step, first_ref, last_ref, w_ref, square_ref, out_ref):
    project(first_ref, last_ref, w_ref, lax.rem(lax.axis_index("tp"), 2), step, square_ref[...], out_ref)


def larger(left_ref, right_ref, after, out_ref):
    out_ref[...] = jnp.maximum(left_ref[...], right_ref[...])


def merge(keep_ref, got_ref, *give_refs):
    for n, ref in enumerate(give_refs):
        ref[...] = (keep_ref[n].astype(F32) + got_ref[n].astype(F32)).astype(ref.dtype)


def finish(features, peak_ref, peak_got, keep_ref, got_ref, *refs):
    peak_out, out_ref = refs[-2:]
    peak_out[...] = jnp.maximum(peak_ref[...], peak_got[...])
    rows = out_ref.shape[0]
    total = keep_ref[0].astype(F32) + got_ref[0].astype(F32)
    for ref in refs[:-2]:
        total = total + ref[...].astype(F32)
    squares = total[rows:rows + 8, :rows] + total[rows:rows + 8, rows:2 * rows]
    inverse = lax.rsqrt(squares / features + 1e-05)
    column = jnp.broadcast_to(inverse[:1, :], (rows, rows)).T[:, :1]
    out_ref[...] = (total[:rows, :] * column).astype(BF16)


def on_device(queries, key_vectors, value_vectors, block_order, norm_gain, kv_weight):
    rows, width = queries.shape[1:]
    heads = width // DH
    peers = lax.axis_size("tp")
    sources = lax.axis_size("cp")
    kv_width = key_vectors.shape[2]
    columns = kv_weight.shape[2]
    out_cols = columns // peers
    shape = jax.ShapeDtypeStruct
    steps = [2**i for i in range((sources - 1).bit_length())]

    pair_here = jnp.concatenate([key_vectors[0], value_vectors[0]], axis=1)
    pair = shifted(pair_here, "pp", 1)
    cut = heads // 2
    counts = [cut, heads - cut]
    starts = [0, cut]
    crossed = []

    def cross(start, count, after, micros):
        part = call(
            functools.partial(take, start * DH),
            shape((rows, count * DH), BF16),
            (queries, after),
            [WHOLE, OUTSIDE],
            name="take",
            micros=micros,
        )
        crossed.append(shifted(part, "pp", 1))

    mark = call(touch, shape((8, LANES), F32), (pair_here,), [OUTSIDE], name="touch", micros=3)
    cross(starts[0], counts[0], mark, 3)
    triple = call(join, shape((rows, 3 * kv_width), BF16), (pair, pair_here), name="join")
    moved = {d: swapped(triple, "cp", d) for d in reversed(range(1, sources))}
    triples = [triple] + [moved[d] for d in range(1, sources)]
    cross(starts[1], counts[1], triple, 0)
    features = call(
        prepare,
        shape((2, LANES, sources * rows), BF16),
        (block_order, mark),
        [SCALARS, OUTSIDE],
        name="prepare",
        micros=3,
    )
    w = call(
        weigh,
        shape((width, columns), BF16),
        (kv_weight[0], norm_gain, moved[sources - 1]),
        [WHOLE, WHOLE, OUTSIDE],
        name="weigh",
        micros=1,
    )
    kv_local = kv_width // DH
    turned = shape((kv_local, 2, DH + LANES, sources * rows), BF16)
    kt, v_all, first_context, peak = call(
        functools.partial(attend_first, heads),
        (
            turned,
            shape((kv_local, sources * rows, 2 * DH), BF16),
            shape((rows, counts[0] * DH), BF16),
            shape((1, heads), F32),
        ),
        (w, features, *reversed(triples), queries, crossed[0]),
        [OUTSIDE] + [WHOLE] * (3 + sources),
        scratch=[pltpu.VMEM(turned.shape, BF16)],
        limit=36,
        name="attend_first",
        micros=2,
    )
    def slabs(count):
        return shape((count, rows + SQUARE_ROWS, out_cols), BF16)

    def to_other_core(block):
        return lax.ppermute(block, "tp", [(i, i ^ 1) for i in range(peers)])

    last_context, give_far, give_near, squares = call(
        functools.partial(attend_last, starts[1], heads),
        (shape((rows, counts[1] * DH), BF16), slabs(peers // 2 - 1), slabs(1), shape((rows, LANES), F32)),
        (crossed[1], kt, v_all, first_context, w),
        limit=32,
        name="attend_last",
        micros=1.5,
    )
    keep_far, keep_near = [
        call(
            functools.partial(project_keep, step),
            slabs(count),
            (first_context, last_context, w, squares),
            name="project_keep",
            micros=3 if step else 0,
        )
        for step, count in ((1, peers // 2 - 1), (0, 1))
    ]
    got_far, got_near = to_other_core(give_far), to_other_core(give_near)
    for step in steps[:-1]:
        peak = call(
            larger,
            shape((1, heads), F32),
            (peak, swapped(peak, "cp", step), give_far),
            [WHOLE, WHOLE, OUTSIDE],
            name="larger",
            micros=5,
        )
    others = call(
        merge,
        [shape((rows + SQUARE_ROWS, out_cols), BF16)] * (peers // 2 - 1),
        (keep_far, got_far),
        name="merge",
    )
    others = [
        lax.ppermute(block, "tp", [(i, (i + 2 * (step + 1)) % peers) for i in range(peers)])
        for step, block in enumerate(others)
    ]
    max_logits, kv_next = call(
        functools.partial(finish, width * peers),
        (shape((1, heads), F32), shape((rows, out_cols), BF16)),
        (peak, swapped(peak, "cp", steps[-1]), keep_near, got_near, *others),
        name="finish",
    )
    return (max_logits, kv_next[None])


def solution(mesh):
    return jax.shard_map(
        on_device,
        mesh=mesh,
        in_specs=(
            P("pp", "cp", "tp"),
            P("pp", "cp", "tp"),
            P("pp", "cp", "tp"),
            P(),
            P("pp", "tp"),
            P("pp", "tp", None),
        ),
        out_specs=(P("pp", "tp"), P("pp", "cp", "tp")),
        check_vma=False,
    )
```

```python
import functools
import math

import jax
import jax.numpy as jnp
from jax import lax
from jax.experimental import pallas as pl
from jax.experimental.pallas import tpu as pltpu
from jax.sharding import PartitionSpec as P

DH = 128
LANES = 128
SQUARE_ROWS = 16
MASKED = -(2.0**100)
LOG2E = math.log2(math.e)
F32 = jnp.float32
BF16 = jnp.bfloat16
WHOLE = pl.BlockSpec(memory_space=pltpu.VMEM)
OUTSIDE = pl.BlockSpec(memory_space=pl.ANY)
SCALARS = pl.BlockSpec(memory_space=pltpu.SMEM)


def call(kernel, outs, args, specs=None, scratch=(), limit=16, name=None, aliases=None, micros=0):
    return pl.pallas_call(
        kernel,
        out_shape=outs,
        in_specs=specs or [WHOLE] * len(args),
        out_specs=jax.tree.map(lambda _: WHOLE, outs),
        scratch_shapes=scratch,
        name=name,
        input_output_aliases=aliases or {},
        cost_estimate=pl.CostEstimate(flops=int(micros * 1e9), bytes_accessed=0, transcendentals=0) if micros else None,
        compiler_params=pltpu.CompilerParams(vmem_limit_bytes=limit * 2**20),
    )(*args)


def partner(index, step, size):
    return (index + step) % size if size & (size - 1) else index ^ step


def swapped(block, axis, step):
    size = lax.axis_size(axis)
    return lax.ppermute(block, axis, [(i, partner(i, step, size)) for i in range(size)])


def shifted(block, axis, distance):
    size = lax.axis_size(axis)
    return lax.ppermute(block, axis, [((i - distance) % size, i) for i in range(size)])


def partner(index, step, size):
    return (index + step) % size if size & (size - 1) else index ^ step


def swapped(block, axis, step):
    size = lax.axis_size(axis)
    return lax.ppermute(block, axis, [(i, partner(i, step, size)) for i in range(size)])


def shifted(block, axis, distance):
    size = lax.axis_size(axis)
    return lax.ppermute(block, axis, [((i - distance) % size, i) for i in range(size)])


def bind_kernel(block_ref, after, out_ref):
    out_ref[...] = block_ref[...]


def bind(block, after):
    return call(
        bind_kernel, jax.ShapeDtypeStruct(block.shape, block.dtype), (block, after), [WHOLE, OUTSIDE], name="bind"
    )


def source_of(d, me, sources):
    return lax.rem(me - d + sources, sources) if sources & (sources - 1) else me ^ d


def take(first, q_ref, after, part_ref):
    part_ref[...] = q_ref[0, :, first:first + part_ref.shape[1]]


def prepare(order_ref, after, feature_ref):
    sources = lax.axis_size("cp")
    me = lax.axis_index("cp")
    rows = feature_ref.shape[2] // sources
    block = rows // 2
    feature = lax.broadcasted_iota(jnp.int32, (LANES, rows), 0)
    key = lax.broadcasted_iota(jnp.int32, (LANES, rows), 1)
    place = lax.rem(key, block)
    for side in range(2):
        mine = order_ref[2 * me + side]
        for d in range(sources):
            source = source_of(d, me, sources)
            other = jnp.where(key < block, order_ref[2 * source], order_ref[2 * source + 1])
            chosen = jnp.where(other == mine, place, jnp.where(other > mine, block, -1))
            feature_ref[side, :, d * rows:(d + 1) * rows] = jnp.where(feature == chosen, 1.0, 0.0).astype(BF16)


def touch(block_ref, out_ref):
    out_ref[...] = jnp.zeros(out_ref.shape, F32)


def join(pair_ref, here_ref, out_ref):
    width = pair_ref.shape[1]
    out_ref[:, :width] = pair_ref[...]
    out_ref[:, width:] = here_ref[:, :width // 2]


def arrange(after, feature_ref, *refs):
    triples, (kt_ref, v_ref, own_ref) = refs[-4::-1], refs[-3:]
    rows = triples[0].shape[0]
    kv_local = v_ref.shape[0]
    for g in range(kv_local):
        v_ref[g, :, DH:] = jnp.ones((v_ref.shape[1], DH), BF16)
        for ref in (kt_ref, own_ref):
            for side in range(2):
                ref[g, side, DH:, :] = feature_ref[side]
        for d, triple in enumerate(triples):
            part = slice(d * rows, (d + 1) * rows)
            for ref, first in ((kt_ref, g * DH), (own_ref, (2 * kv_local + g) * DH)):
                turned = triple[:, first:first + DH].astype(F32).T.astype(BF16)
                for side in range(2):
                    ref[g, side, :DH, part] = turned
            first = (kv_local + g) * DH
            v_ref[g, part, :DH] = triple[:, first:first + DH]


def spans(first_head, count, group, together):
    start = 0
    while start < count:
        g = (first_head + start) // group
        stop = min(start + together, count, (g + 1) * group - first_head)
        yield g, start, stop
        start = stop


def stacked(q_ref, start, stop, side):
    block = q_ref.shape[0] // 2
    shape = ((stop - start) * block, LANES)
    token = lax.rem(lax.broadcasted_iota(jnp.int32, shape, 0), block)
    lane = lax.broadcasted_iota(jnp.int32, shape, 1)
    blocked = jnp.where((lane > token) & (lane <= block), MASKED, 0.0).astype(BF16)
    tokens = slice(side * block, (side + 1) * block)
    q = jnp.concatenate([q_ref[tokens, h * DH:(h + 1) * DH] for h in range(start, stop)], axis=0)
    return jnp.concatenate([q, blocked], axis=1)


def attention_units(first_head, heads, q_ref, kt_ref, v_ref, ctx_ref):
    rows, width = q_ref.shape
    keys = v_ref.shape[1]
    block = rows // 2
    factor = LOG2E / math.sqrt(DH)
    units = [
        (g, start, stop, side)
        for g, start, stop in spans(first_head, width // DH, heads // v_ref.shape[0], max(1, 12 * 512 // keys))
        for side in range(2)
    ]

    def scores(unit):
        g, start, stop, side = unit
        return jnp.dot(stacked(q_ref, start, stop, side), kt_ref[g, side], preferred_element_type=F32)

    def finish_unit(unit, s):
        g, start, stop, side = unit
        m = jnp.max(s, axis=1, keepdims=True)
        p = jnp.exp2((s - m) * factor).astype(BF16)
        yield
        o = jnp.dot(p, v_ref[g], preferred_element_type=F32)
        o = (o[:, :DH] * (1.0 / o[:, DH:])).astype(BF16)
        for j in range(stop - start):
            ctx_ref[side * block:(side + 1) * block, (start + j) * DH:(start + j + 1) * DH] = o[
                j * block:(j + 1) * block, :
            ]

    ahead = [scores(unit) for unit in units[:2]]
    for n, unit in enumerate(units):
        yield from finish_unit(unit, ahead.pop(0))
        if n + 2 < len(units):
            ahead.append(scores(units[n + 2]))


def maxima_units(q_ref, own_ref, peak_ref):
    block = q_ref.shape[0] // 2
    heads = q_ref.shape[1] // DH
    keys = own_ref.shape[3]
    for g, start, stop in spans(0, heads, heads // own_ref.shape[0], max(1, 8 * 512 // keys)):
        tops = []
        for side in range(2):
            s = jnp.dot(stacked(q_ref, start, stop, side), own_ref[g, side], preferred_element_type=F32)
            yield
            top = s[:, :LANES]
            for c in range(LANES, keys, LANES):
                top = jnp.maximum(top, s[:, c:c + LANES])
            tops.append(top)
        top = jnp.maximum(*tops)
        for j in range(stop - start):
            one = jnp.max(top[j * block:(j + 1) * block, :], axis=0, keepdims=True)
            h = start + j
            peak_ref[:, h:h + 1] = jnp.max(one, axis=1, keepdims=True) * (1.0 / math.sqrt(DH))


def interleave(*streams):
    streams = list(streams)
    while streams:
        for stream in list(streams):
            if next(stream, stream) is stream:
                streams.remove(stream)


def attend_first(heads, w_ref, feature_ref, *refs):
    triples, refs = refs[:-7], refs[-7:]
    mine_ref, q_ref, kt_ref, v_ref, ctx_ref, peak_ref, own_ref = refs
    arrange(None, feature_ref, *triples, kt_ref, v_ref, own_ref)
    interleave(
        attention_units(0, heads, q_ref, kt_ref, v_ref, ctx_ref), maxima_units(mine_ref.at[0], own_ref, peak_ref)
    )


def attend_last(
    first_head, heads, q_ref, kt_ref, v_ref, first_ref, w_ref, ctx_ref, far_ref, near_ref, square_ref
):
    interleave(attention_units(first_head, heads, q_ref, kt_ref, v_ref, ctx_ref))
    squares = square_sums(first_ref) + square_sums(ctx_ref)
    square_ref[...] = squares
    other = 1 - lax.rem(lax.axis_index("tp"), 2)
    project(first_ref, ctx_ref, w_ref, other, 1, squares, far_ref)
    project(first_ref, ctx_ref, w_ref, other, 0, squares, near_ref)


def weigh(w_ref, gain_ref, after, out_ref):
    features, columns = w_ref.shape
    for f in range(0, features, LANES):
        gain = jnp.broadcast_to(gain_ref[:, f:f + LANES].astype(F32), (LANES, LANES)).T
        for c in range(0, columns, LANES):
            out_ref[f:f + LANES, c:c + LANES] = (w_ref[f:f + LANES, c:c + LANES].astype(F32) * gain).astype(BF16)


def square_sums(ctx_ref):
    total = None
    for c in range(0, ctx_ref.shape[1], LANES):
        wide = ctx_ref[:, c:c + LANES].astype(F32)
        total = wide * wide if total is None else total + wide * wide
    return jnp.broadcast_to(jnp.sum(total, axis=1, keepdims=True), total.shape)


def columns_of(y, side, cols):
    return pl.ds(pl.multiple_of((2 * y + side) * cols, cols), cols)


def fill(ref, y, part, squares):
    rows, cols = part.shape
    lanes = squares.T[:SQUARE_ROWS, :]
    first = lanes.astype(BF16)
    rest = (lanes - first.astype(F32)).astype(BF16)
    ref[y, :rows, :] = part.astype(BF16)
    ref[y, rows:, :rows] = first
    ref[y, rows:, rows:2 * rows] = rest
    if cols > 2 * rows:
        ref[y, rows:, 2 * rows:] = jnp.zeros((SQUARE_ROWS, cols - 2 * rows), BF16)


def product(first_ref, last_ref, w_ref, at):
    cut = first_ref.shape[1]
    part = jnp.dot(first_ref[...], w_ref[:cut, at], preferred_element_type=F32)
    return part + jnp.dot(last_ref[...], w_ref[cut:, at], preferred_element_type=F32)


def project(first_ref, last_ref, w_ref, side, step, squares, out_ref):
    groups = w_ref.shape[1] // (2 * out_ref.shape[2])
    mine = lax.axis_index("tp") // 2
    for n in range(out_ref.shape[0]):
        at = columns_of(lax.rem(mine + step + n, groups), side, out_ref.shape[2])
        fill(out_ref, n, product(first_ref, last_ref, w_ref, at), squares)


def project_keep(step, first_ref, last_ref, w_ref, square_ref, out_ref):
    project(first_ref, last_ref, w_ref, lax.rem(lax.axis_index("tp"), 2), step, square_ref[...], out_ref)


def larger(left_ref, right_ref, after, out_ref):
    out_ref[...] = jnp.maximum(left_ref[...], right_ref[...])


def merge(keep_ref, got_ref, *give_refs):
    for n, ref in enumerate(give_refs):
        ref[...] = (keep_ref[n].astype(F32) + got_ref[n].astype(F32)).astype(ref.dtype)


def finish(features, peak_ref, peak_got, keep_ref, got_ref, *refs):
    peak_out, out_ref = refs[-2:]
    peak_out[...] = jnp.maximum(peak_ref[...], peak_got[...])
    rows = out_ref.shape[0]
    total = keep_ref[0].astype(F32) + got_ref[0].astype(F32)
    for ref in refs[:-2]:
        total = total + ref[...].astype(F32)
    squares = total[rows:rows + 8, :rows] + total[rows:rows + 8, rows:2 * rows]
    inverse = lax.rsqrt(squares / features + 1e-05)
    column = jnp.broadcast_to(inverse[:1, :], (rows, rows)).T[:, :1]
    out_ref[...] = (total[:rows, :] * column).astype(BF16)


def on_device(queries, key_vectors, value_vectors, block_order, norm_gain, kv_weight):
    rows, width = queries.shape[1:]
    heads = width // DH
    peers = lax.axis_size("tp")
    sources = lax.axis_size("cp")
    kv_width = key_vectors.shape[2]
    columns = kv_weight.shape[2]
    out_cols = columns // peers
    shape = jax.ShapeDtypeStruct
    steps = [2**i for i in range((sources - 1).bit_length())]

    pair_here = jnp.concatenate([key_vectors[0], value_vectors[0]], axis=1)
    pair = shifted(pair_here, "pp", 1)
    cut = heads * 3 // 8
    counts = [cut, heads - cut]
    starts = [0, cut]
    crossed = []

    def cross(start, count, after, micros):
        part = call(
            functools.partial(take, start * DH),
            shape((rows, count * DH), BF16),
            (queries, after),
            [WHOLE, OUTSIDE],
            name="take",
            micros=micros,
        )
        crossed.append(shifted(part, "pp", 1))

    mark = call(touch, shape((8, LANES), F32), (pair_here,), [OUTSIDE], name="touch", micros=3)
    cross(starts[0], counts[0], mark, 3)
    triple = call(join, shape((rows, 3 * kv_width), BF16), (pair, pair_here), name="join")
    moved = {d: swapped(triple, "cp", d) for d in reversed(range(1, sources))}
    triples = [triple] + [moved[d] for d in range(1, sources)]
    cross(starts[1], counts[1], triple, 0)
    features = call(
        prepare,
        shape((2, LANES, sources * rows), BF16),
        (block_order, mark),
        [SCALARS, OUTSIDE],
        name="prepare",
        micros=3,
    )
    w = call(
        weigh,
        shape((width, columns), BF16),
        (kv_weight[0], norm_gain, moved[sources - 1]),
        [WHOLE, WHOLE, OUTSIDE],
        name="weigh",
        micros=1,
    )
    kv_local = kv_width // DH
    turned = shape((kv_local, 2, DH + LANES, sources * rows), BF16)
    kt, v_all, first_context, peak = call(
        functools.partial(attend_first, heads),
        (
            turned,
            shape((kv_local, sources * rows, 2 * DH), BF16),
            shape((rows, counts[0] * DH), BF16),
            shape((1, heads), F32),
        ),
        (w, features, *reversed(triples), queries, crossed[0]),
        [OUTSIDE] + [WHOLE] * (3 + sources),
        scratch=[pltpu.VMEM(turned.shape, BF16)],
        limit=36,
        name="attend_first",
        micros=2,
    )
    def slabs(count):
        return shape((count, rows + SQUARE_ROWS, out_cols), BF16)

    def to_other_core(block):
        return lax.ppermute(block, "tp", [(i, i ^ 1) for i in range(peers)])

    last_context, give_far, give_near, squares = call(
        functools.partial(attend_last, starts[1], heads),
        (shape((rows, counts[1] * DH), BF16), slabs(peers // 2 - 1), slabs(1), shape((rows, LANES), F32)),
        (crossed[1], kt, v_all, first_context, w),
        limit=32,
        name="attend_last",
        micros=1.5,
    )
    keep_far, keep_near = [
        call(
            functools.partial(project_keep, step),
            slabs(count),
            (first_context, last_context, w, squares),
            name="project_keep",
            micros=3 if step else 0,
        )
        for step, count in ((1, peers // 2 - 1), (0, 1))
    ]
    got_far, got_near = to_other_core(give_far), to_other_core(give_near)
    for step in steps[:-1]:
        peak = call(
            larger,
            shape((1, heads), F32),
            (peak, swapped(peak, "cp", step), give_far),
            [WHOLE, WHOLE, OUTSIDE],
            name="larger",
            micros=5,
        )
    others = call(
        merge,
        [shape((rows + SQUARE_ROWS, out_cols), BF16)] * (peers // 2 - 1),
        (keep_far, got_far),
        name="merge",
    )
    others = [
        lax.ppermute(block, "tp", [(i, (i + 2 * (step + 1)) % peers) for i in range(peers)])
        for step, block in enumerate(others)
    ]
    max_logits, kv_next = call(
        functools.partial(finish, width * peers),
        (shape((1, heads), F32), shape((rows, out_cols), BF16)),
        (peak, swapped(peak, "cp", steps[-1]), keep_near, got_near, *others),
        name="finish",
    )
    return (max_logits, kv_next[None])


def solution(mesh):
    return jax.shard_map(
        on_device,
        mesh=mesh,
        in_specs=(
            P("pp", "cp", "tp"),
            P("pp", "cp", "tp"),
            P("pp", "cp", "tp"),
            P(),
            P("pp", "tp"),
            P("pp", "tp", None),
        ),
        out_specs=(P("pp", "tp"), P("pp", "cp", "tp")),
        check_vma=False,
    )
```

```python
import functools
import math

import jax
import jax.numpy as jnp
from jax import lax
from jax.experimental import pallas as pl
from jax.experimental.pallas import tpu as pltpu
from jax.sharding import PartitionSpec as P

DH = 128
LANES = 128
SQUARE_ROWS = 16
MASKED = -(2.0**100)
LOG2E = math.log2(math.e)
F32 = jnp.float32
BF16 = jnp.bfloat16
WHOLE = pl.BlockSpec(memory_space=pltpu.VMEM)
OUTSIDE = pl.BlockSpec(memory_space=pl.ANY)
SCALARS = pl.BlockSpec(memory_space=pltpu.SMEM)


def call(kernel, outs, args, specs=None, scratch=(), limit=16, name=None, aliases=None, micros=0):
    return pl.pallas_call(
        kernel,
        out_shape=outs,
        in_specs=specs or [WHOLE] * len(args),
        out_specs=jax.tree.map(lambda _: WHOLE, outs),
        scratch_shapes=scratch,
        name=name,
        input_output_aliases=aliases or {},
        cost_estimate=pl.CostEstimate(flops=int(micros * 1e9), bytes_accessed=0, transcendentals=0) if micros else None,
        compiler_params=pltpu.CompilerParams(vmem_limit_bytes=limit * 2**20),
    )(*args)


def partner(index, step, size):
    return (index + step) % size if size & (size - 1) else index ^ step


def swapped(block, axis, step):
    size = lax.axis_size(axis)
    return lax.ppermute(block, axis, [(i, partner(i, step, size)) for i in range(size)])


def shifted(block, axis, distance):
    size = lax.axis_size(axis)
    return lax.ppermute(block, axis, [((i - distance) % size, i) for i in range(size)])


def partner(index, step, size):
    return (index + step) % size if size & (size - 1) else index ^ step


def swapped(block, axis, step):
    size = lax.axis_size(axis)
    return lax.ppermute(block, axis, [(i, partner(i, step, size)) for i in range(size)])


def shifted(block, axis, distance):
    size = lax.axis_size(axis)
    return lax.ppermute(block, axis, [((i - distance) % size, i) for i in range(size)])


def bind_kernel(block_ref, after, out_ref):
    out_ref[...] = block_ref[...]


def bind(block, after):
    return call(
        bind_kernel, jax.ShapeDtypeStruct(block.shape, block.dtype), (block, after), [WHOLE, OUTSIDE], name="bind"
    )


def source_of(d, me, sources):
    return lax.rem(me - d + sources, sources) if sources & (sources - 1) else me ^ d


def take(first, q_ref, after, part_ref):
    part_ref[...] = q_ref[0, :, first:first + part_ref.shape[1]]


def prepare(order_ref, after, feature_ref):
    sources = lax.axis_size("cp")
    me = lax.axis_index("cp")
    rows = feature_ref.shape[2] // sources
    block = rows // 2
    feature = lax.broadcasted_iota(jnp.int32, (LANES, rows), 0)
    key = lax.broadcasted_iota(jnp.int32, (LANES, rows), 1)
    place = lax.rem(key, block)
    for side in range(2):
        mine = order_ref[2 * me + side]
        for d in range(sources):
            source = source_of(d, me, sources)
            other = jnp.where(key < block, order_ref[2 * source], order_ref[2 * source + 1])
            chosen = jnp.where(other == mine, place, jnp.where(other > mine, block, -1))
            feature_ref[side, :, d * rows:(d + 1) * rows] = jnp.where(feature == chosen, 1.0, 0.0).astype(BF16)


def touch(block_ref, out_ref):
    out_ref[...] = jnp.zeros(out_ref.shape, F32)


def join(pair_ref, here_ref, out_ref):
    width = pair_ref.shape[1]
    out_ref[:, :width] = pair_ref[...]
    out_ref[:, width:] = here_ref[:, :width // 2]


def arrange(after, feature_ref, *refs):
    triples, (kt_ref, v_ref, own_ref) = refs[-4::-1], refs[-3:]
    rows = triples[0].shape[0]
    kv_local = v_ref.shape[0]
    for g in range(kv_local):
        v_ref[g, :, DH:] = jnp.ones((v_ref.shape[1], DH), BF16)
        for ref in (kt_ref, own_ref):
            for side in range(2):
                ref[g, side, DH:, :] = feature_ref[side]
        for d, triple in enumerate(triples):
            part = slice(d * rows, (d + 1) * rows)
            for ref, first in ((kt_ref, g * DH), (own_ref, (2 * kv_local + g) * DH)):
                turned = triple[:, first:first + DH].astype(F32).T.astype(BF16)
                for side in range(2):
                    ref[g, side, :DH, part] = turned
            first = (kv_local + g) * DH
            v_ref[g, part, :DH] = triple[:, first:first + DH]


def spans(first_head, count, group, together):
    start = 0
    while start < count:
        g = (first_head + start) // group
        stop = min(start + together, count, (g + 1) * group - first_head)
        yield g, start, stop
        start = stop


def stacked(q_ref, start, stop, side):
    block = q_ref.shape[0] // 2
    shape = ((stop - start) * block, LANES)
    token = lax.rem(lax.broadcasted_iota(jnp.int32, shape, 0), block)
    lane = lax.broadcasted_iota(jnp.int32, shape, 1)
    blocked = jnp.where((lane > token) & (lane <= block), MASKED, 0.0).astype(BF16)
    tokens = slice(side * block, (side + 1) * block)
    q = jnp.concatenate([q_ref[tokens, h * DH:(h + 1) * DH] for h in range(start, stop)], axis=0)
    return jnp.concatenate([q, blocked], axis=1)


def attention_units(first_head, heads, q_ref, kt_ref, v_ref, ctx_ref):
    rows, width = q_ref.shape
    keys = v_ref.shape[1]
    block = rows // 2
    factor = LOG2E / math.sqrt(DH)
    units = [
        (g, start, stop, side)
        for g, start, stop in spans(first_head, width // DH, heads // v_ref.shape[0], max(1, 12 * 512 // keys))
        for side in range(2)
    ]

    def scores(unit):
        g, start, stop, side = unit
        return jnp.dot(stacked(q_ref, start, stop, side), kt_ref[g, side], preferred_element_type=F32)

    def finish_unit(unit, s):
        g, start, stop, side = unit
        m = jnp.max(s, axis=1, keepdims=True)
        p = jnp.exp2((s - m) * factor).astype(BF16)
        yield
        o = jnp.dot(p, v_ref[g], preferred_element_type=F32)
        o = (o[:, :DH] * (1.0 / o[:, DH:])).astype(BF16)
        for j in range(stop - start):
            ctx_ref[side * block:(side + 1) * block, (start + j) * DH:(start + j + 1) * DH] = o[
                j * block:(j + 1) * block, :
            ]

    ahead = [scores(unit) for unit in units[:2]]
    for n, unit in enumerate(units):
        yield from finish_unit(unit, ahead.pop(0))
        if n + 2 < len(units):
            ahead.append(scores(units[n + 2]))


def maxima_units(q_ref, own_ref, peak_ref):
    block = q_ref.shape[0] // 2
    heads = q_ref.shape[1] // DH
    keys = own_ref.shape[3]
    for g, start, stop in spans(0, heads, heads // own_ref.shape[0], max(1, 8 * 512 // keys)):
        tops = []
        for side in range(2):
            s = jnp.dot(stacked(q_ref, start, stop, side), own_ref[g, side], preferred_element_type=F32)
            yield
            top = s[:, :LANES]
            for c in range(LANES, keys, LANES):
                top = jnp.maximum(top, s[:, c:c + LANES])
            tops.append(top)
        top = jnp.maximum(*tops)
        for j in range(stop - start):
            one = jnp.max(top[j * block:(j + 1) * block, :], axis=0, keepdims=True)
            h = start + j
            peak_ref[:, h:h + 1] = jnp.max(one, axis=1, keepdims=True) * (1.0 / math.sqrt(DH))


def interleave(*streams):
    streams = list(streams)
    while streams:
        for stream in list(streams):
            if next(stream, stream) is stream:
                streams.remove(stream)


def attend_first(heads, w_ref, feature_ref, *refs):
    triples, refs = refs[:-7], refs[-7:]
    mine_ref, q_ref, kt_ref, v_ref, ctx_ref, peak_ref, own_ref = refs
    arrange(None, feature_ref, *triples, kt_ref, v_ref, own_ref)
    interleave(
        attention_units(0, heads, q_ref, kt_ref, v_ref, ctx_ref), maxima_units(mine_ref.at[0], own_ref, peak_ref)
    )


def attend_last(
    first_head, heads, q_ref, kt_ref, v_ref, first_ref, w_ref, ctx_ref, far_ref, square_ref
):
    interleave(attention_units(first_head, heads, q_ref, kt_ref, v_ref, ctx_ref))
    squares = square_sums(first_ref) + square_sums(ctx_ref)
    square_ref[...] = squares
    other = 1 - lax.rem(lax.axis_index("tp"), 2)
    project(first_ref, ctx_ref, w_ref, other, 1, squares, far_ref)


def weigh(w_ref, gain_ref, after, out_ref):
    features, columns = w_ref.shape
    for f in range(0, features, LANES):
        gain = jnp.broadcast_to(gain_ref[:, f:f + LANES].astype(F32), (LANES, LANES)).T
        for c in range(0, columns, LANES):
            out_ref[f:f + LANES, c:c + LANES] = (w_ref[f:f + LANES, c:c + LANES].astype(F32) * gain).astype(BF16)


def square_sums(ctx_ref):
    total = None
    for c in range(0, ctx_ref.shape[1], LANES):
        wide = ctx_ref[:, c:c + LANES].astype(F32)
        total = wide * wide if total is None else total + wide * wide
    return jnp.broadcast_to(jnp.sum(total, axis=1, keepdims=True), total.shape)


def columns_of(y, side, cols):
    return pl.ds(pl.multiple_of((2 * y + side) * cols, cols), cols)


def fill(ref, y, part, squares):
    rows, cols = part.shape
    lanes = squares.T[:SQUARE_ROWS, :]
    first = lanes.astype(BF16)
    rest = (lanes - first.astype(F32)).astype(BF16)
    ref[y, :rows, :] = part.astype(BF16)
    ref[y, rows:, :rows] = first
    ref[y, rows:, rows:2 * rows] = rest
    if cols > 2 * rows:
        ref[y, rows:, 2 * rows:] = jnp.zeros((SQUARE_ROWS, cols - 2 * rows), BF16)


def product(first_ref, last_ref, w_ref, at):
    cut = first_ref.shape[1]
    part = jnp.dot(first_ref[...], w_ref[:cut, at], preferred_element_type=F32)
    return part + jnp.dot(last_ref[...], w_ref[cut:, at], preferred_element_type=F32)


def project(first_ref, last_ref, w_ref, side, step, squares, out_ref):
    groups = w_ref.shape[1] // (2 * out_ref.shape[2])
    mine = lax.axis_index("tp") // 2
    for n in range(out_ref.shape[0]):
        at = columns_of(lax.rem(mine + step + n, groups), side, out_ref.shape[2])
        fill(out_ref, n, product(first_ref, last_ref, w_ref, at), squares)


def project_more(shift, step, first_ref, last_ref, w_ref, square_ref, out_ref):
    side = lax.rem(lax.axis_index("tp") + shift, 2)
    project(first_ref, last_ref, w_ref, side, step, square_ref[...], out_ref)


def larger(left_ref, right_ref, after, out_ref):
    out_ref[...] = jnp.maximum(left_ref[...], right_ref[...])


def merge(keep_ref, got_ref, *give_refs):
    for n, ref in enumerate(give_refs):
        ref[...] = (keep_ref[n].astype(F32) + got_ref[n].astype(F32)).astype(ref.dtype)


def finish(features, peak_ref, peak_got, keep_ref, got_ref, *refs):
    peak_out, out_ref = refs[-2:]
    peak_out[...] = jnp.maximum(peak_ref[...], peak_got[...])
    rows = out_ref.shape[0]
    total = keep_ref[0].astype(F32) + got_ref[0].astype(F32)
    for ref in refs[:-2]:
        total = total + ref[...].astype(F32)
    squares = total[rows:rows + 8, :rows] + total[rows:rows + 8, rows:2 * rows]
    inverse = lax.rsqrt(squares / features + 1e-05)
    column = jnp.broadcast_to(inverse[:1, :], (rows, rows)).T[:, :1]
    out_ref[...] = (total[:rows, :] * column).astype(BF16)


def on_device(queries, key_vectors, value_vectors, block_order, norm_gain, kv_weight):
    rows, width = queries.shape[1:]
    heads = width // DH
    peers = lax.axis_size("tp")
    sources = lax.axis_size("cp")
    kv_width = key_vectors.shape[2]
    columns = kv_weight.shape[2]
    out_cols = columns // peers
    shape = jax.ShapeDtypeStruct
    steps = [2**i for i in range((sources - 1).bit_length())]

    pair_here = jnp.concatenate([key_vectors[0], value_vectors[0]], axis=1)
    pair = shifted(pair_here, "pp", 1)
    cut = heads * 3 // 8
    counts = [cut, heads - cut]
    starts = [0, cut]
    crossed = []

    def cross(start, count, after, micros):
        part = call(
            functools.partial(take, start * DH),
            shape((rows, count * DH), BF16),
            (queries, after),
            [WHOLE, OUTSIDE],
            name="take",
            micros=micros,
        )
        crossed.append(shifted(part, "pp", 1))

    mark = call(touch, shape((8, LANES), F32), (pair_here,), [OUTSIDE], name="touch", micros=3)
    cross(starts[0], counts[0], mark, 3)
    triple = call(join, shape((rows, 3 * kv_width), BF16), (pair, pair_here), name="join")
    moved = {d: swapped(triple, "cp", d) for d in reversed(range(1, sources))}
    triples = [triple] + [moved[d] for d in range(1, sources)]
    cross(starts[1], counts[1], triple, 0)
    features = call(
        prepare,
        shape((2, LANES, sources * rows), BF16),
        (block_order, mark),
        [SCALARS, OUTSIDE],
        name="prepare",
        micros=3,
    )
    w = call(
        weigh,
        shape((width, columns), BF16),
        (kv_weight[0], norm_gain, moved[sources - 1]),
        [WHOLE, WHOLE, OUTSIDE],
        name="weigh",
        micros=1,
    )
    kv_local = kv_width // DH
    turned = shape((kv_local, 2, DH + LANES, sources * rows), BF16)
    kt, v_all, first_context, peak = call(
        functools.partial(attend_first, heads),
        (
            turned,
            shape((kv_local, sources * rows, 2 * DH), BF16),
            shape((rows, counts[0] * DH), BF16),
            shape((1, heads), F32),
        ),
        (w, features, *reversed(triples), queries, crossed[0]),
        [OUTSIDE] + [WHOLE] * (3 + sources),
        scratch=[pltpu.VMEM(turned.shape, BF16)],
        limit=36,
        name="attend_first",
        micros=2,
    )
    def slabs(count):
        return shape((count, rows + SQUARE_ROWS, out_cols), BF16)

    def to_other_core(block):
        return lax.ppermute(block, "tp", [(i, i ^ 1) for i in range(peers)])

    last_context, give_far, squares = call(
        functools.partial(attend_last, starts[1], heads),
        (shape((rows, counts[1] * DH), BF16), slabs(peers // 2 - 1), shape((rows, LANES), F32)),
        (crossed[1], kt, v_all, first_context, w),
        limit=32,
        name="attend_last",
        micros=1.5,
    )
    give_near, keep_far, keep_near = [
        call(
            functools.partial(project_more, shift, step),
            slabs(count),
            (first_context, last_context, w, squares),
            name="project_more",
            micros=micros,
        )
        for shift, step, count, micros in ((1, 0, 1, 0.3), (0, 1, peers // 2 - 1, 3), (0, 0, 1, 0))
    ]
    got_far, got_near = to_other_core(give_far), to_other_core(give_near)
    for step in steps[:-1]:
        peak = call(
            larger,
            shape((1, heads), F32),
            (peak, swapped(peak, "cp", step), give_far),
            [WHOLE, WHOLE, OUTSIDE],
            name="larger",
            micros=5,
        )
    others = call(
        merge,
        [shape((rows + SQUARE_ROWS, out_cols), BF16)] * (peers // 2 - 1),
        (keep_far, got_far),
        name="merge",
    )
    others = [
        lax.ppermute(block, "tp", [(i, (i + 2 * (step + 1)) % peers) for i in range(peers)])
        for step, block in enumerate(others)
    ]
    max_logits, kv_next = call(
        functools.partial(finish, width * peers),
        (shape((1, heads), F32), shape((rows, out_cols), BF16)),
        (peak, swapped(peak, "cp", steps[-1]), keep_near, got_near, *others),
        name="finish",
    )
    return (max_logits, kv_next[None])


def solution(mesh):
    return jax.shard_map(
        on_device,
        mesh=mesh,
        in_specs=(
            P("pp", "cp", "tp"),
            P("pp", "cp", "tp"),
            P("pp", "cp", "tp"),
            P(),
            P("pp", "tp"),
            P("pp", "tp", None),
        ),
        out_specs=(P("pp", "tp"), P("pp", "cp", "tp")),
        check_vma=False,
    )
```

```python
import functools
import math

import jax
import jax.numpy as jnp
from jax import lax
from jax.experimental import pallas as pl
from jax.experimental.pallas import tpu as pltpu
from jax.sharding import PartitionSpec as P

DH = 128
LANES = 128
SQUARE_ROWS = 16
MASKED = -(2.0**100)
LOG2E = math.log2(math.e)
F32 = jnp.float32
BF16 = jnp.bfloat16
WHOLE = pl.BlockSpec(memory_space=pltpu.VMEM)
OUTSIDE = pl.BlockSpec(memory_space=pl.ANY)
SCALARS = pl.BlockSpec(memory_space=pltpu.SMEM)


def call(kernel, outs, args, specs=None, scratch=(), limit=16, name=None, aliases=None, micros=0):
    return pl.pallas_call(
        kernel,
        out_shape=outs,
        in_specs=specs or [WHOLE] * len(args),
        out_specs=jax.tree.map(lambda _: WHOLE, outs),
        scratch_shapes=scratch,
        name=name,
        input_output_aliases=aliases or {},
        cost_estimate=pl.CostEstimate(flops=int(micros * 1e9), bytes_accessed=0, transcendentals=0) if micros else None,
        compiler_params=pltpu.CompilerParams(vmem_limit_bytes=limit * 2**20),
    )(*args)


def partner(index, step, size):
    return (index + step) % size if size & (size - 1) else index ^ step


def swapped(block, axis, step):
    size = lax.axis_size(axis)
    return lax.ppermute(block, axis, [(i, partner(i, step, size)) for i in range(size)])


def shifted(block, axis, distance):
    size = lax.axis_size(axis)
    return lax.ppermute(block, axis, [((i - distance) % size, i) for i in range(size)])


def partner(index, step, size):
    return (index + step) % size if size & (size - 1) else index ^ step


def swapped(block, axis, step):
    size = lax.axis_size(axis)
    return lax.ppermute(block, axis, [(i, partner(i, step, size)) for i in range(size)])


def shifted(block, axis, distance):
    size = lax.axis_size(axis)
    return lax.ppermute(block, axis, [((i - distance) % size, i) for i in range(size)])


def bind_kernel(block_ref, after, out_ref):
    out_ref[...] = block_ref[...]


def bind(block, after):
    return call(
        bind_kernel, jax.ShapeDtypeStruct(block.shape, block.dtype), (block, after), [WHOLE, OUTSIDE], name="bind"
    )


def source_of(d, me, sources):
    return lax.rem(me - d + sources, sources) if sources & (sources - 1) else me ^ d


def take(first, q_ref, after, part_ref):
    part_ref[...] = q_ref[0, :, first:first + part_ref.shape[1]]


def prepare(order_ref, after, feature_ref):
    sources = lax.axis_size("cp")
    me = lax.axis_index("cp")
    rows = feature_ref.shape[2] // sources
    block = rows // 2
    feature = lax.broadcasted_iota(jnp.int32, (LANES, rows), 0)
    key = lax.broadcasted_iota(jnp.int32, (LANES, rows), 1)
    place = lax.rem(key, block)
    for side in range(2):
        mine = order_ref[2 * me + side]
        for d in range(sources):
            source = source_of(d, me, sources)
            other = jnp.where(key < block, order_ref[2 * source], order_ref[2 * source + 1])
            chosen = jnp.where(other == mine, place, jnp.where(other > mine, block, -1))
            feature_ref[side, :, d * rows:(d + 1) * rows] = jnp.where(feature == chosen, 1.0, 0.0).astype(BF16)


def touch(block_ref, out_ref):
    out_ref[...] = jnp.zeros(out_ref.shape, F32)


def join(pair_ref, here_ref, out_ref):
    width = pair_ref.shape[1]
    out_ref[:, :width] = pair_ref[...]
    out_ref[:, width:] = here_ref[:, :width // 2]


def arrange(after, feature_ref, *refs):
    triples, (kt_ref, v_ref, own_ref) = refs[-4::-1], refs[-3:]
    rows = triples[0].shape[0]
    kv_local = v_ref.shape[0]
    for g in range(kv_local):
        v_ref[g, :, DH:] = jnp.ones((v_ref.shape[1], DH), BF16)
        for ref in (kt_ref, own_ref):
            for side in range(2):
                ref[g, side, DH:, :] = feature_ref[side]
        for d, triple in enumerate(triples):
            part = slice(d * rows, (d + 1) * rows)
            for ref, first in ((kt_ref, g * DH), (own_ref, (2 * kv_local + g) * DH)):
                turned = triple[:, first:first + DH].astype(F32).T.astype(BF16)
                for side in range(2):
                    ref[g, side, :DH, part] = turned
            first = (kv_local + g) * DH
            v_ref[g, part, :DH] = triple[:, first:first + DH]


def spans(first_head, count, group, together):
    start = 0
    while start < count:
        g = (first_head + start) // group
        stop = min(start + together, count, (g + 1) * group - first_head)
        yield g, start, stop
        start = stop


def stacked(q_ref, start, stop, side):
    block = q_ref.shape[0] // 2
    shape = ((stop - start) * block, LANES)
    token = lax.rem(lax.broadcasted_iota(jnp.int32, shape, 0), block)
    lane = lax.broadcasted_iota(jnp.int32, shape, 1)
    blocked = jnp.where((lane > token) & (lane <= block), MASKED, 0.0).astype(BF16)
    tokens = slice(side * block, (side + 1) * block)
    q = jnp.concatenate([q_ref[tokens, h * DH:(h + 1) * DH] for h in range(start, stop)], axis=0)
    return jnp.concatenate([q, blocked], axis=1)


def attention_units(first_head, heads, q_ref, kt_ref, v_ref, ctx_ref):
    rows, width = q_ref.shape
    keys = v_ref.shape[1]
    block = rows // 2
    factor = LOG2E / math.sqrt(DH)
    units = [
        (g, start, stop, side)
        for g, start, stop in spans(first_head, width // DH, heads // v_ref.shape[0], max(1, 12 * 512 // keys))
        for side in range(2)
    ]

    def scores(unit):
        g, start, stop, side = unit
        return jnp.dot(stacked(q_ref, start, stop, side), kt_ref[g, side], preferred_element_type=F32)

    def finish_unit(unit, s):
        g, start, stop, side = unit
        m = jnp.max(s, axis=1, keepdims=True)
        p = jnp.exp2((s - m) * factor).astype(BF16)
        yield
        o = jnp.dot(p, v_ref[g], preferred_element_type=F32)
        o = (o[:, :DH] * (1.0 / o[:, DH:])).astype(BF16)
        for j in range(stop - start):
            ctx_ref[side * block:(side + 1) * block, (start + j) * DH:(start + j + 1) * DH] = o[
                j * block:(j + 1) * block, :
            ]

    ahead = [scores(unit) for unit in units[:2]]
    for n, unit in enumerate(units):
        yield from finish_unit(unit, ahead.pop(0))
        if n + 2 < len(units):
            ahead.append(scores(units[n + 2]))


def maxima_units(q_ref, own_ref, peak_ref):
    block = q_ref.shape[0] // 2
    heads = q_ref.shape[1] // DH
    keys = own_ref.shape[3]
    for g, start, stop in spans(0, heads, heads // own_ref.shape[0], max(1, 8 * 512 // keys)):
        tops = []
        for side in range(2):
            s = jnp.dot(stacked(q_ref, start, stop, side), own_ref[g, side], preferred_element_type=F32)
            yield
            top = s[:, :LANES]
            for c in range(LANES, keys, LANES):
                top = jnp.maximum(top, s[:, c:c + LANES])
            tops.append(top)
        top = jnp.maximum(*tops)
        for j in range(stop - start):
            one = jnp.max(top[j * block:(j + 1) * block, :], axis=0, keepdims=True)
            h = start + j
            peak_ref[:, h:h + 1] = jnp.max(one, axis=1, keepdims=True) * (1.0 / math.sqrt(DH))


def interleave(*streams):
    streams = list(streams)
    while streams:
        for stream in list(streams):
            if next(stream, stream) is stream:
                streams.remove(stream)


def attend_first(heads, w_ref, feature_ref, *refs):
    triples, refs = refs[:-7], refs[-7:]
    mine_ref, q_ref, kt_ref, v_ref, ctx_ref, peak_ref, own_ref = refs
    arrange(None, feature_ref, *triples, kt_ref, v_ref, own_ref)
    interleave(
        attention_units(0, heads, q_ref, kt_ref, v_ref, ctx_ref), maxima_units(mine_ref.at[0], own_ref, peak_ref)
    )


def attend_last(
    first_head, heads, q_ref, kt_ref, v_ref, first_ref, w_ref, ctx_ref, far_ref, near_ref, square_ref
):
    interleave(attention_units(first_head, heads, q_ref, kt_ref, v_ref, ctx_ref))
    squares = square_sums(first_ref) + square_sums(ctx_ref)
    square_ref[...] = squares
    other = 1 - lax.rem(lax.axis_index("tp"), 2)
    project(first_ref, ctx_ref, w_ref, other, 1, squares, far_ref)
    project(first_ref, ctx_ref, w_ref, other, 0, squares, near_ref)


def weigh(w_ref, gain_ref, after, out_ref):
    features, columns = w_ref.shape
    for f in range(0, features, LANES):
        gain = jnp.broadcast_to(gain_ref[:, f:f + LANES].astype(F32), (LANES, LANES)).T
        for c in range(0, columns, LANES):
            out_ref[f:f + LANES, c:c + LANES] = (w_ref[f:f + LANES, c:c + LANES].astype(F32) * gain).astype(BF16)


def square_sums(ctx_ref):
    total = None
    for c in range(0, ctx_ref.shape[1], LANES):
        wide = ctx_ref[:, c:c + LANES].astype(F32)
        total = wide * wide if total is None else total + wide * wide
    return jnp.broadcast_to(jnp.sum(total, axis=1, keepdims=True), total.shape)


def columns_of(y, side, cols):
    return pl.ds(pl.multiple_of((2 * y + side) * cols, cols), cols)


def fill(ref, y, part, squares):
    rows, cols = part.shape
    lanes = squares.T[:SQUARE_ROWS, :]
    first = lanes.astype(BF16)
    rest = (lanes - first.astype(F32)).astype(BF16)
    ref[y, :rows, :] = part.astype(BF16)
    ref[y, rows:, :rows] = first
    ref[y, rows:, rows:2 * rows] = rest
    if cols > 2 * rows:
        ref[y, rows:, 2 * rows:] = jnp.zeros((SQUARE_ROWS, cols - 2 * rows), BF16)


def product(first_ref, last_ref, w_ref, at):
    cut = first_ref.shape[1]
    part = jnp.dot(first_ref[...], w_ref[:cut, at], preferred_element_type=F32)
    return part + jnp.dot(last_ref[...], w_ref[cut:, at], preferred_element_type=F32)


def project(first_ref, last_ref, w_ref, side, step, squares, out_ref):
    groups = w_ref.shape[1] // (2 * out_ref.shape[2])
    mine = lax.axis_index("tp") // 2
    for n in range(out_ref.shape[0]):
        at = columns_of(lax.rem(mine + step + n, groups), side, out_ref.shape[2])
        fill(out_ref, n, product(first_ref, last_ref, w_ref, at), squares)


def project_keep(step, first_ref, last_ref, w_ref, square_ref, out_ref):
    project(first_ref, last_ref, w_ref, lax.rem(lax.axis_index("tp"), 2), step, square_ref[...], out_ref)


def larger(left_ref, right_ref, after, out_ref):
    out_ref[...] = jnp.maximum(left_ref[...], right_ref[...])


def merge(keep_ref, got_ref, *give_refs):
    for n, ref in enumerate(give_refs):
        ref[...] = (keep_ref[n].astype(F32) + got_ref[n].astype(F32)).astype(ref.dtype)


def finish(features, peak_ref, peak_got, keep_ref, got_ref, *refs):
    peak_out, out_ref = refs[-2:]
    peak_out[...] = jnp.maximum(peak_ref[...], peak_got[...])
    rows = out_ref.shape[0]
    total = keep_ref[0].astype(F32) + got_ref[0].astype(F32)
    for ref in refs[:-2]:
        total = total + ref[...].astype(F32)
    squares = total[rows:rows + 8, :rows] + total[rows:rows + 8, rows:2 * rows]
    inverse = lax.rsqrt(squares / features + 1e-05)
    column = jnp.broadcast_to(inverse[:1, :], (rows, rows)).T[:, :1]
    out_ref[...] = (total[:rows, :] * column).astype(BF16)


def on_device(queries, key_vectors, value_vectors, block_order, norm_gain, kv_weight):
    rows, width = queries.shape[1:]
    heads = width // DH
    peers = lax.axis_size("tp")
    sources = lax.axis_size("cp")
    kv_width = key_vectors.shape[2]
    columns = kv_weight.shape[2]
    out_cols = columns // peers
    shape = jax.ShapeDtypeStruct
    steps = [2**i for i in range((sources - 1).bit_length())]

    pair_here = jnp.concatenate([key_vectors[0], value_vectors[0]], axis=1)
    pair = shifted(pair_here, "pp", 1)
    cut = heads // 4
    counts = [cut, heads - cut]
    starts = [0, cut]
    crossed = []

    def cross(start, count, after, micros):
        part = call(
            functools.partial(take, start * DH),
            shape((rows, count * DH), BF16),
            (queries, after),
            [WHOLE, OUTSIDE],
            name="take",
            micros=micros,
        )
        crossed.append(shifted(part, "pp", 1))

    mark = call(touch, shape((8, LANES), F32), (pair_here,), [OUTSIDE], name="touch", micros=3)
    cross(starts[0], counts[0], mark, 3)
    triple = call(join, shape((rows, 3 * kv_width), BF16), (pair, pair_here), name="join")
    moved = {d: swapped(triple, "cp", d) for d in reversed(range(1, sources))}
    triples = [triple] + [moved[d] for d in range(1, sources)]
    cross(starts[1], counts[1], triple, 0)
    features = call(
        prepare,
        shape((2, LANES, sources * rows), BF16),
        (block_order, mark),
        [SCALARS, OUTSIDE],
        name="prepare",
        micros=3,
    )
    w = call(
        weigh,
        shape((width, columns), BF16),
        (kv_weight[0], norm_gain, moved[sources - 1]),
        [WHOLE, WHOLE, OUTSIDE],
        name="weigh",
        micros=1,
    )
    kv_local = kv_width // DH
    turned = shape((kv_local, 2, DH + LANES, sources * rows), BF16)
    kt, v_all, first_context, peak = call(
        functools.partial(attend_first, heads),
        (
            turned,
            shape((kv_local, sources * rows, 2 * DH), BF16),
            shape((rows, counts[0] * DH), BF16),
            shape((1, heads), F32),
        ),
        (w, features, *reversed(triples), queries, crossed[0]),
        [OUTSIDE] + [WHOLE] * (3 + sources),
        scratch=[pltpu.VMEM(turned.shape, BF16)],
        limit=36,
        name="attend_first",
        micros=2,
    )
    def slabs(count):
        return shape((count, rows + SQUARE_ROWS, out_cols), BF16)

    def to_other_core(block):
        return lax.ppermute(block, "tp", [(i, i ^ 1) for i in range(peers)])

    last_context, give_far, give_near, squares = call(
        functools.partial(attend_last, starts[1], heads),
        (shape((rows, counts[1] * DH), BF16), slabs(peers // 2 - 1), slabs(1), shape((rows, LANES), F32)),
        (crossed[1], kt, v_all, first_context, w),
        limit=32,
        name="attend_last",
        micros=1.5,
    )
    keep_far, keep_near = [
        call(
            functools.partial(project_keep, step),
            slabs(count),
            (first_context, last_context, w, squares),
            name="project_keep",
            micros=3 if step else 0,
        )
        for step, count in ((1, peers // 2 - 1), (0, 1))
    ]
    got_far, got_near = to_other_core(give_far), to_other_core(give_near)
    for step in steps[:-1]:
        peak = call(
            larger,
            shape((1, heads), F32),
            (peak, swapped(peak, "cp", step), give_far),
            [WHOLE, WHOLE, OUTSIDE],
            name="larger",
            micros=5,
        )
    others = call(
        merge,
        [shape((rows + SQUARE_ROWS, out_cols), BF16)] * (peers // 2 - 1),
        (keep_far, got_far),
        name="merge",
    )
    others = [
        lax.ppermute(block, "tp", [(i, (i + 2 * (step + 1)) % peers) for i in range(peers)])
        for step, block in enumerate(others)
    ]
    max_logits, kv_next = call(
        functools.partial(finish, width * peers),
        (shape((1, heads), F32), shape((rows, out_cols), BF16)),
        (peak, swapped(peak, "cp", steps[-1]), keep_near, got_near, *others),
        name="finish",
    )
    return (max_logits, kv_next[None])


def solution(mesh):
    return jax.shard_map(
        on_device,
        mesh=mesh,
        in_specs=(
            P("pp", "cp", "tp"),
            P("pp", "cp", "tp"),
            P("pp", "cp", "tp"),
            P(),
            P("pp", "tp"),
            P("pp", "tp", None),
        ),
        out_specs=(P("pp", "tp"), P("pp", "cp", "tp")),
        check_vma=False,
    )
```

```python
import functools
import math

import jax
import jax.numpy as jnp
from jax import lax
from jax.experimental import pallas as pl
from jax.experimental.pallas import tpu as pltpu
from jax.sharding import PartitionSpec as P

DH = 128
LANES = 128
SQUARE_ROWS = 16
MASKED = -(2.0**100)
LOG2E = math.log2(math.e)
F32 = jnp.float32
BF16 = jnp.bfloat16
WHOLE = pl.BlockSpec(memory_space=pltpu.VMEM)
OUTSIDE = pl.BlockSpec(memory_space=pl.ANY)
SCALARS = pl.BlockSpec(memory_space=pltpu.SMEM)


def call(kernel, outs, args, specs=None, scratch=(), limit=16, name=None, aliases=None, micros=0):
    return pl.pallas_call(
        kernel,
        out_shape=outs,
        in_specs=specs or [WHOLE] * len(args),
        out_specs=jax.tree.map(lambda _: WHOLE, outs),
        scratch_shapes=scratch,
        name=name,
        input_output_aliases=aliases or {},
        cost_estimate=pl.CostEstimate(flops=int(micros * 1e9), bytes_accessed=0, transcendentals=0) if micros else None,
        compiler_params=pltpu.CompilerParams(vmem_limit_bytes=limit * 2**20),
    )(*args)


def partner(index, step, size):
    return (index + step) % size if size & (size - 1) else index ^ step


def swapped(block, axis, step):
    size = lax.axis_size(axis)
    return lax.ppermute(block, axis, [(i, partner(i, step, size)) for i in range(size)])


def shifted(block, axis, distance):
    size = lax.axis_size(axis)
    return lax.ppermute(block, axis, [((i - distance) % size, i) for i in range(size)])


def partner(index, step, size):
    return (index + step) % size if size & (size - 1) else index ^ step


def swapped(block, axis, step):
    size = lax.axis_size(axis)
    return lax.ppermute(block, axis, [(i, partner(i, step, size)) for i in range(size)])


def shifted(block, axis, distance):
    size = lax.axis_size(axis)
    return lax.ppermute(block, axis, [((i - distance) % size, i) for i in range(size)])


def bind_kernel(block_ref, after, out_ref):
    out_ref[...] = block_ref[...]


def bind(block, after):
    return call(
        bind_kernel, jax.ShapeDtypeStruct(block.shape, block.dtype), (block, after), [WHOLE, OUTSIDE], name="bind"
    )


def source_of(d, me, sources):
    return lax.rem(me - d + sources, sources) if sources & (sources - 1) else me ^ d


def take(first, q_ref, after, part_ref):
    part_ref[...] = q_ref[0, :, first:first + part_ref.shape[1]]


def prepare(order_ref, after, feature_ref):
    sources = lax.axis_size("cp")
    me = lax.axis_index("cp")
    rows = feature_ref.shape[2] // sources
    block = rows // 2
    feature = lax.broadcasted_iota(jnp.int32, (LANES, rows), 0)
    key = lax.broadcasted_iota(jnp.int32, (LANES, rows), 1)
    place = lax.rem(key, block)
    for side in range(2):
        mine = order_ref[2 * me + side]
        for d in range(sources):
            source = source_of(d, me, sources)
            other = jnp.where(key < block, order_ref[2 * source], order_ref[2 * source + 1])
            chosen = jnp.where(other == mine, place, jnp.where(other > mine, block, -1))
            feature_ref[side, :, d * rows:(d + 1) * rows] = jnp.where(feature == chosen, 1.0, 0.0).astype(BF16)


def touch(block_ref, out_ref):
    out_ref[...] = jnp.zeros(out_ref.shape, F32)


def join(pair_ref, here_ref, out_ref):
    width = pair_ref.shape[1]
    out_ref[:, :width] = pair_ref[...]
    out_ref[:, width:] = here_ref[:, :width // 2]


def arrange(after, feature_ref, *refs):
    triples, (kt_ref, v_ref, own_ref) = refs[-4::-1], refs[-3:]
    rows = triples[0].shape[0]
    kv_local = v_ref.shape[0]
    for g in range(kv_local):
        v_ref[g, :, DH:] = jnp.ones((v_ref.shape[1], DH), BF16)
        for ref in (kt_ref, own_ref):
            for side in range(2):
                ref[g, side, DH:, :] = feature_ref[side]
        for d, triple in enumerate(triples):
            part = slice(d * rows, (d + 1) * rows)
            for ref, first in ((kt_ref, g * DH), (own_ref, (2 * kv_local + g) * DH)):
                turned = triple[:, first:first + DH].astype(F32).T.astype(BF16)
                for side in range(2):
                    ref[g, side, :DH, part] = turned
            first = (kv_local + g) * DH
            v_ref[g, part, :DH] = triple[:, first:first + DH]


def spans(first_head, count, group, together):
    start = 0
    while start < count:
        g = (first_head + start) // group
        stop = min(start + together, count, (g + 1) * group - first_head)
        yield g, start, stop
        start = stop


def stacked(q_ref, start, stop, side):
    block = q_ref.shape[0] // 2
    shape = ((stop - start) * block, LANES)
    token = lax.rem(lax.broadcasted_iota(jnp.int32, shape, 0), block)
    lane = lax.broadcasted_iota(jnp.int32, shape, 1)
    blocked = jnp.where((lane > token) & (lane <= block), MASKED, 0.0).astype(BF16)
    tokens = slice(side * block, (side + 1) * block)
    q = jnp.concatenate([q_ref[tokens, h * DH:(h + 1) * DH] for h in range(start, stop)], axis=0)
    return jnp.concatenate([q, blocked], axis=1)


def attention_units(first_head, heads, q_ref, kt_ref, v_ref, ctx_ref):
    rows, width = q_ref.shape
    keys = v_ref.shape[1]
    block = rows // 2
    factor = LOG2E / math.sqrt(DH)
    units = [
        (g, start, stop, side)
        for g, start, stop in spans(first_head, width // DH, heads // v_ref.shape[0], max(1, 12 * 512 // keys))
        for side in range(2)
    ]

    def scores(unit):
        g, start, stop, side = unit
        return jnp.dot(stacked(q_ref, start, stop, side), kt_ref[g, side], preferred_element_type=F32)

    def finish_unit(unit, s):
        g, start, stop, side = unit
        m = jnp.max(s, axis=1, keepdims=True)
        p = jnp.exp2((s - m) * factor).astype(BF16)
        yield
        o = jnp.dot(p, v_ref[g], preferred_element_type=F32)
        o = (o[:, :DH] * (1.0 / o[:, DH:])).astype(BF16)
        for j in range(stop - start):
            ctx_ref[side * block:(side + 1) * block, (start + j) * DH:(start + j + 1) * DH] = o[
                j * block:(j + 1) * block, :
            ]

    ahead = [scores(unit) for unit in units[:2]]
    for n, unit in enumerate(units):
        yield from finish_unit(unit, ahead.pop(0))
        if n + 2 < len(units):
            ahead.append(scores(units[n + 2]))


def maxima_units(q_ref, own_ref, peak_ref):
    block = q_ref.shape[0] // 2
    heads = q_ref.shape[1] // DH
    keys = own_ref.shape[3]
    for g, start, stop in spans(0, heads, heads // own_ref.shape[0], max(1, 16 * 512 // keys)):
        tops = []
        for side in range(2):
            s = jnp.dot(stacked(q_ref, start, stop, side), own_ref[g, side], preferred_element_type=F32)
            yield
            top = s[:, :LANES]
            for c in range(LANES, keys, LANES):
                top = jnp.maximum(top, s[:, c:c + LANES])
            tops.append(top)
        top = jnp.maximum(*tops)
        for j in range(stop - start):
            one = jnp.max(top[j * block:(j + 1) * block, :], axis=0, keepdims=True)
            h = start + j
            peak_ref[:, h:h + 1] = jnp.max(one, axis=1, keepdims=True) * (1.0 / math.sqrt(DH))


def interleave(*streams):
    streams = list(streams)
    while streams:
        for stream in list(streams):
            if next(stream, stream) is stream:
                streams.remove(stream)


def attend_first(heads, w_ref, feature_ref, *refs):
    triples, refs = refs[:-7], refs[-7:]
    mine_ref, q_ref, kt_ref, v_ref, ctx_ref, peak_ref, own_ref = refs
    arrange(None, feature_ref, *triples, kt_ref, v_ref, own_ref)
    interleave(
        attention_units(0, heads, q_ref, kt_ref, v_ref, ctx_ref), maxima_units(mine_ref.at[0], own_ref, peak_ref)
    )


def attend_last(
    first_head, heads, q_ref, kt_ref, v_ref, first_ref, w_ref, ctx_ref, far_ref, near_ref, square_ref
):
    interleave(attention_units(first_head, heads, q_ref, kt_ref, v_ref, ctx_ref))
    squares = square_sums(first_ref) + square_sums(ctx_ref)
    square_ref[...] = squares
    other = 1 - lax.rem(lax.axis_index("tp"), 2)
    project(first_ref, ctx_ref, w_ref, other, 1, squares, far_ref)
    project(first_ref, ctx_ref, w_ref, other, 0, squares, near_ref)


def weigh(w_ref, gain_ref, after, out_ref):
    features, columns = w_ref.shape
    for f in range(0, features, LANES):
        gain = jnp.broadcast_to(gain_ref[:, f:f + LANES].astype(F32), (LANES, LANES)).T
        for c in range(0, columns, LANES):
            out_ref[f:f + LANES, c:c + LANES] = (w_ref[f:f + LANES, c:c + LANES].astype(F32) * gain).astype(BF16)


def square_sums(ctx_ref):
    total = None
    for c in range(0, ctx_ref.shape[1], LANES):
        wide = ctx_ref[:, c:c + LANES].astype(F32)
        total = wide * wide if total is None else total + wide * wide
    return jnp.broadcast_to(jnp.sum(total, axis=1, keepdims=True), total.shape)


def columns_of(y, side, cols):
    return pl.ds(pl.multiple_of((2 * y + side) * cols, cols), cols)


def fill(ref, y, part, squares):
    rows, cols = part.shape
    lanes = squares.T[:SQUARE_ROWS, :]
    first = lanes.astype(BF16)
    rest = (lanes - first.astype(F32)).astype(BF16)
    ref[y, :rows, :] = part.astype(BF16)
    ref[y, rows:, :rows] = first
    ref[y, rows:, rows:2 * rows] = rest
    if cols > 2 * rows:
        ref[y, rows:, 2 * rows:] = jnp.zeros((SQUARE_ROWS, cols - 2 * rows), BF16)


def product(first_ref, last_ref, w_ref, at):
    cut = first_ref.shape[1]
    part = jnp.dot(first_ref[...], w_ref[:cut, at], preferred_element_type=F32)
    return part + jnp.dot(last_ref[...], w_ref[cut:, at], preferred_element_type=F32)


def project(first_ref, last_ref, w_ref, side, step, squares, out_ref):
    groups = w_ref.shape[1] // (2 * out_ref.shape[2])
    mine = lax.axis_index("tp") // 2
    for n in range(out_ref.shape[0]):
        at = columns_of(lax.rem(mine + step + n, groups), side, out_ref.shape[2])
        fill(out_ref, n, product(first_ref, last_ref, w_ref, at), squares)


def project_keep(step, first_ref, last_ref, w_ref, square_ref, out_ref):
    project(first_ref, last_ref, w_ref, lax.rem(lax.axis_index("tp"), 2), step, square_ref[...], out_ref)


def larger(left_ref, right_ref, after, out_ref):
    out_ref[...] = jnp.maximum(left_ref[...], right_ref[...])


def merge(keep_ref, got_ref, *give_refs):
    for n, ref in enumerate(give_refs):
        ref[...] = (keep_ref[n].astype(F32) + got_ref[n].astype(F32)).astype(ref.dtype)


def finish(features, peak_ref, peak_got, keep_ref, got_ref, *refs):
    peak_out, out_ref = refs[-2:]
    peak_out[...] = jnp.maximum(peak_ref[...], peak_got[...])
    rows = out_ref.shape[0]
    total = keep_ref[0].astype(F32) + got_ref[0].astype(F32)
    for ref in refs[:-2]:
        total = total + ref[...].astype(F32)
    squares = total[rows:rows + 8, :rows] + total[rows:rows + 8, rows:2 * rows]
    inverse = lax.rsqrt(squares / features + 1e-05)
    column = jnp.broadcast_to(inverse[:1, :], (rows, rows)).T[:, :1]
    out_ref[...] = (total[:rows, :] * column).astype(BF16)


def on_device(queries, key_vectors, value_vectors, block_order, norm_gain, kv_weight):
    rows, width = queries.shape[1:]
    heads = width // DH
    peers = lax.axis_size("tp")
    sources = lax.axis_size("cp")
    kv_width = key_vectors.shape[2]
    columns = kv_weight.shape[2]
    out_cols = columns // peers
    shape = jax.ShapeDtypeStruct
    steps = [2**i for i in range((sources - 1).bit_length())]

    pair_here = jnp.concatenate([key_vectors[0], value_vectors[0]], axis=1)
    pair = shifted(pair_here, "pp", 1)
    cut = heads * 3 // 8
    counts = [cut, heads - cut]
    starts = [0, cut]
    crossed = []

    def cross(start, count, after, micros):
        part = call(
            functools.partial(take, start * DH),
            shape((rows, count * DH), BF16),
            (queries, after),
            [WHOLE, OUTSIDE],
            name="take",
            micros=micros,
        )
        crossed.append(shifted(part, "pp", 1))

    mark = call(touch, shape((8, LANES), F32), (pair_here,), [OUTSIDE], name="touch", micros=3)
    cross(starts[0], counts[0], mark, 3)
    triple = call(join, shape((rows, 3 * kv_width), BF16), (pair, pair_here), name="join")
    moved = {d: swapped(triple, "cp", d) for d in reversed(range(1, sources))}
    triples = [triple] + [moved[d] for d in range(1, sources)]
    cross(starts[1], counts[1], triple, 0)
    features = call(
        prepare,
        shape((2, LANES, sources * rows), BF16),
        (block_order, mark),
        [SCALARS, OUTSIDE],
        name="prepare",
        micros=3,
    )
    w = call(
        weigh,
        shape((width, columns), BF16),
        (kv_weight[0], norm_gain, moved[sources - 1]),
        [WHOLE, WHOLE, OUTSIDE],
        name="weigh",
        micros=1,
    )
    kv_local = kv_width // DH
    turned = shape((kv_local, 2, DH + LANES, sources * rows), BF16)
    kt, v_all, first_context, peak = call(
        functools.partial(attend_first, heads),
        (
            turned,
            shape((kv_local, sources * rows, 2 * DH), BF16),
            shape((rows, counts[0] * DH), BF16),
            shape((1, heads), F32),
        ),
        (w, features, *reversed(triples), queries, crossed[0]),
        [OUTSIDE] + [WHOLE] * (3 + sources),
        scratch=[pltpu.VMEM(turned.shape, BF16)],
        limit=36,
        name="attend_first",
        micros=2,
    )
    def slabs(count):
        return shape((count, rows + SQUARE_ROWS, out_cols), BF16)

    def to_other_core(block):
        return lax.ppermute(block, "tp", [(i, i ^ 1) for i in range(peers)])

    last_context, give_far, give_near, squares = call(
        functools.partial(attend_last, starts[1], heads),
        (shape((rows, counts[1] * DH), BF16), slabs(peers // 2 - 1), slabs(1), shape((rows, LANES), F32)),
        (crossed[1], kt, v_all, first_context, w),
        limit=32,
        name="attend_last",
        micros=1.5,
    )
    keep_far, keep_near = [
        call(
            functools.partial(project_keep, step),
            slabs(count),
            (first_context, last_context, w, squares),
            name="project_keep",
            micros=3 if step else 0,
        )
        for step, count in ((1, peers // 2 - 1), (0, 1))
    ]
    got_far, got_near = to_other_core(give_far), to_other_core(give_near)
    for step in steps[:-1]:
        peak = call(
            larger,
            shape((1, heads), F32),
            (peak, swapped(peak, "cp", step), give_far),
            [WHOLE, WHOLE, OUTSIDE],
            name="larger",
            micros=5,
        )
    others = call(
        merge,
        [shape((rows + SQUARE_ROWS, out_cols), BF16)] * (peers // 2 - 1),
        (keep_far, got_far),
        name="merge",
    )
    others = [
        lax.ppermute(block, "tp", [(i, (i + 2 * (step + 1)) % peers) for i in range(peers)])
        for step, block in enumerate(others)
    ]
    max_logits, kv_next = call(
        functools.partial(finish, width * peers),
        (shape((1, heads), F32), shape((rows, out_cols), BF16)),
        (peak, swapped(peak, "cp", steps[-1]), keep_near, got_near, *others),
        name="finish",
    )
    return (max_logits, kv_next[None])


def solution(mesh):
    return jax.shard_map(
        on_device,
        mesh=mesh,
        in_specs=(
            P("pp", "cp", "tp"),
            P("pp", "cp", "tp"),
            P("pp", "cp", "tp"),
            P(),
            P("pp", "tp"),
            P("pp", "tp", None),
        ),
        out_specs=(P("pp", "tp"), P("pp", "cp", "tp")),
        check_vma=False,
    )
```

```python
import functools
import math

import jax
import jax.numpy as jnp
from jax import lax
from jax.experimental import pallas as pl
from jax.experimental.pallas import tpu as pltpu
from jax.sharding import PartitionSpec as P

DH = 128
LANES = 128
SQUARE_ROWS = 16
MASKED = -(2.0**100)
LOG2E = math.log2(math.e)
F32 = jnp.float32
BF16 = jnp.bfloat16
WHOLE = pl.BlockSpec(memory_space=pltpu.VMEM)
OUTSIDE = pl.BlockSpec(memory_space=pl.ANY)
SCALARS = pl.BlockSpec(memory_space=pltpu.SMEM)


def call(kernel, outs, args, specs=None, scratch=(), limit=16, name=None, aliases=None, micros=0):
    return pl.pallas_call(
        kernel,
        out_shape=outs,
        in_specs=specs or [WHOLE] * len(args),
        out_specs=jax.tree.map(lambda _: WHOLE, outs),
        scratch_shapes=scratch,
        name=name,
        input_output_aliases=aliases or {},
        cost_estimate=pl.CostEstimate(flops=int(micros * 1e9), bytes_accessed=0, transcendentals=0) if micros else None,
        compiler_params=pltpu.CompilerParams(vmem_limit_bytes=limit * 2**20),
    )(*args)


def partner(index, step, size):
    return (index + step) % size if size & (size - 1) else index ^ step


def swapped(block, axis, step):
    size = lax.axis_size(axis)
    return lax.ppermute(block, axis, [(i, partner(i, step, size)) for i in range(size)])


def shifted(block, axis, distance):
    size = lax.axis_size(axis)
    return lax.ppermute(block, axis, [((i - distance) % size, i) for i in range(size)])


def partner(index, step, size):
    return (index + step) % size if size & (size - 1) else index ^ step


def swapped(block, axis, step):
    size = lax.axis_size(axis)
    return lax.ppermute(block, axis, [(i, partner(i, step, size)) for i in range(size)])


def shifted(block, axis, distance):
    size = lax.axis_size(axis)
    return lax.ppermute(block, axis, [((i - distance) % size, i) for i in range(size)])


def bind_kernel(block_ref, after, out_ref):
    out_ref[...] = block_ref[...]


def bind(block, after):
    return call(
        bind_kernel, jax.ShapeDtypeStruct(block.shape, block.dtype), (block, after), [WHOLE, OUTSIDE], name="bind"
    )


def source_of(d, me, sources):
    return lax.rem(me - d + sources, sources) if sources & (sources - 1) else me ^ d


def take(first, q_ref, after, part_ref):
    part_ref[...] = q_ref[0, :, first:first + part_ref.shape[1]]


def prepare(order_ref, after, feature_ref):
    sources = lax.axis_size("cp")
    me = lax.axis_index("cp")
    rows = feature_ref.shape[2] // sources
    block = rows // 2
    feature = lax.broadcasted_iota(jnp.int32, (LANES, rows), 0)
    key = lax.broadcasted_iota(jnp.int32, (LANES, rows), 1)
    place = lax.rem(key, block)
    for side in range(2):
        mine = order_ref[2 * me + side]
        for d in range(sources):
            source = source_of(d, me, sources)
            other = jnp.where(key < block, order_ref[2 * source], order_ref[2 * source + 1])
            chosen = jnp.where(other == mine, place, jnp.where(other > mine, block, -1))
            feature_ref[side, :, d * rows:(d + 1) * rows] = jnp.where(feature == chosen, 1.0, 0.0).astype(BF16)


def touch(block_ref, out_ref):
    out_ref[...] = jnp.zeros(out_ref.shape, F32)


def join(pair_ref, here_ref, out_ref):
    width = pair_ref.shape[1]
    out_ref[:, :width] = pair_ref[...]
    out_ref[:, width:] = here_ref[:, :width // 2]


def arrange(after, feature_ref, *refs):
    triples, (kt_ref, v_ref, own_ref) = refs[-4::-1], refs[-3:]
    rows = triples[0].shape[0]
    kv_local = v_ref.shape[0]
    for g in range(kv_local):
        v_ref[g, :, DH:] = jnp.ones((v_ref.shape[1], DH), BF16)
        for ref in (kt_ref, own_ref):
            for side in range(2):
                ref[g, side, DH:, :] = feature_ref[side]
        for d, triple in enumerate(triples):
            part = slice(d * rows, (d + 1) * rows)
            for ref, first in ((kt_ref, g * DH), (own_ref, (2 * kv_local + g) * DH)):
                turned = triple[:, first:first + DH].astype(F32).T.astype(BF16)
                for side in range(2):
                    ref[g, side, :DH, part] = turned
            first = (kv_local + g) * DH
            v_ref[g, part, :DH] = triple[:, first:first + DH]


def spans(first_head, count, group, together):
    start = 0
    while start < count:
        g = (first_head + start) // group
        stop = min(start + together, count, (g + 1) * group - first_head)
        yield g, start, stop
        start = stop


def stacked(q_ref, start, stop, side):
    block = q_ref.shape[0] // 2
    shape = ((stop - start) * block, LANES)
    token = lax.rem(lax.broadcasted_iota(jnp.int32, shape, 0), block)
    lane = lax.broadcasted_iota(jnp.int32, shape, 1)
    blocked = jnp.where((lane > token) & (lane <= block), MASKED, 0.0).astype(BF16)
    tokens = slice(side * block, (side + 1) * block)
    q = jnp.concatenate([q_ref[tokens, h * DH:(h + 1) * DH] for h in range(start, stop)], axis=0)
    return jnp.concatenate([q, blocked], axis=1)


def attention_units(first_head, heads, q_ref, kt_ref, v_ref, ctx_ref):
    rows, width = q_ref.shape
    keys = v_ref.shape[1]
    block = rows // 2
    factor = LOG2E / math.sqrt(DH)
    units = [
        (g, start, stop, side)
        for g, start, stop in spans(first_head, width // DH, heads // v_ref.shape[0], max(1, 12 * 512 // keys))
        for side in range(2)
    ]

    def scores(unit):
        g, start, stop, side = unit
        return jnp.dot(stacked(q_ref, start, stop, side), kt_ref[g, side], preferred_element_type=F32)

    def finish_unit(unit, s):
        g, start, stop, side = unit
        m = jnp.max(s, axis=1, keepdims=True)
        p = jnp.exp2((s - m) * factor).astype(BF16)
        yield
        o = jnp.dot(p, v_ref[g], preferred_element_type=F32)
        o = (o[:, :DH] * (1.0 / o[:, DH:])).astype(BF16)
        for j in range(stop - start):
            ctx_ref[side * block:(side + 1) * block, (start + j) * DH:(start + j + 1) * DH] = o[
                j * block:(j + 1) * block, :
            ]

    ahead = [scores(unit) for unit in units[:2]]
    for n, unit in enumerate(units):
        yield from finish_unit(unit, ahead.pop(0))
        if n + 2 < len(units):
            ahead.append(scores(units[n + 2]))


def maxima_units(q_ref, own_ref, peak_ref):
    block = q_ref.shape[0] // 2
    heads = q_ref.shape[1] // DH
    keys = own_ref.shape[3]
    for g, start, stop in spans(0, heads, heads // own_ref.shape[0], max(1, 8 * 512 // keys)):
        tops = []
        for side in range(2):
            s = jnp.dot(stacked(q_ref, start, stop, side), own_ref[g, side], preferred_element_type=F32)
            yield
            top = s[:, :LANES]
            for c in range(LANES, keys, LANES):
                top = jnp.maximum(top, s[:, c:c + LANES])
            tops.append(top)
        top = jnp.maximum(*tops)
        for j in range(stop - start):
            one = jnp.max(top[j * block:(j + 1) * block, :], axis=0, keepdims=True)
            h = start + j
            peak_ref[:, h:h + 1] = jnp.max(one, axis=1, keepdims=True) * (1.0 / math.sqrt(DH))


def interleave(*streams):
    streams = list(streams)
    while streams:
        for stream in list(streams):
            if next(stream, stream) is stream:
                streams.remove(stream)


def attend_first(heads, w_ref, feature_ref, *refs):
    triples, refs = refs[:-7], refs[-7:]
    mine_ref, q_ref, kt_ref, v_ref, ctx_ref, peak_ref, own_ref = refs
    arrange(None, feature_ref, *triples, kt_ref, v_ref, own_ref)
    interleave(
        attention_units(0, heads, q_ref, kt_ref, v_ref, ctx_ref), maxima_units(mine_ref.at[0], own_ref, peak_ref)
    )


def attend_last(
    first_head, heads, q_ref, kt_ref, v_ref, first_ref, w_ref, ctx_ref, far_ref, near_ref, square_ref
):
    square_ref[...] = square_sums(first_ref)
    interleave(attention_units(first_head, heads, q_ref, kt_ref, v_ref, ctx_ref))
    squares = square_ref[...] + square_sums(ctx_ref)
    square_ref[...] = squares
    other = 1 - lax.rem(lax.axis_index("tp"), 2)
    project(first_ref, ctx_ref, w_ref, other, 1, squares, far_ref)
    project(first_ref, ctx_ref, w_ref, other, 0, squares, near_ref)


def weigh(w_ref, gain_ref, after, out_ref):
    features, columns = w_ref.shape
    for f in range(0, features, LANES):
        gain = jnp.broadcast_to(gain_ref[:, f:f + LANES].astype(F32), (LANES, LANES)).T
        for c in range(0, columns, LANES):
            out_ref[f:f + LANES, c:c + LANES] = (w_ref[f:f + LANES, c:c + LANES].astype(F32) * gain).astype(BF16)


def square_sums(ctx_ref):
    total = None
    for c in range(0, ctx_ref.shape[1], LANES):
        wide = ctx_ref[:, c:c + LANES].astype(F32)
        total = wide * wide if total is None else total + wide * wide
    return jnp.broadcast_to(jnp.sum(total, axis=1, keepdims=True), total.shape)


def columns_of(y, side, cols):
    return pl.ds(pl.multiple_of((2 * y + side) * cols, cols), cols)


def fill(ref, y, part, squares):
    rows, cols = part.shape
    lanes = squares.T[:SQUARE_ROWS, :]
    first = lanes.astype(BF16)
    rest = (lanes - first.astype(F32)).astype(BF16)
    ref[y, :rows, :] = part.astype(BF16)
    ref[y, rows:, :rows] = first
    ref[y, rows:, rows:2 * rows] = rest
    if cols > 2 * rows:
        ref[y, rows:, 2 * rows:] = jnp.zeros((SQUARE_ROWS, cols - 2 * rows), BF16)


def product(first_ref, last_ref, w_ref, at):
    cut = first_ref.shape[1]
    part = jnp.dot(first_ref[...], w_ref[:cut, at], preferred_element_type=F32)
    return part + jnp.dot(last_ref[...], w_ref[cut:, at], preferred_element_type=F32)


def project(first_ref, last_ref, w_ref, side, step, squares, out_ref):
    groups = w_ref.shape[1] // (2 * out_ref.shape[2])
    mine = lax.axis_index("tp") // 2
    for n in range(out_ref.shape[0]):
        at = columns_of(lax.rem(mine + step + n, groups), side, out_ref.shape[2])
        fill(out_ref, n, product(first_ref, last_ref, w_ref, at), squares)


def project_keep(step, first_ref, last_ref, w_ref, square_ref, out_ref):
    project(first_ref, last_ref, w_ref, lax.rem(lax.axis_index("tp"), 2), step, square_ref[...], out_ref)


def larger(left_ref, right_ref, after, out_ref):
    out_ref[...] = jnp.maximum(left_ref[...], right_ref[...])


def merge(keep_ref, got_ref, *give_refs):
    for n, ref in enumerate(give_refs):
        ref[...] = (keep_ref[n].astype(F32) + got_ref[n].astype(F32)).astype(ref.dtype)


def finish(features, peak_ref, peak_got, keep_ref, got_ref, *refs):
    peak_out, out_ref = refs[-2:]
    peak_out[...] = jnp.maximum(peak_ref[...], peak_got[...])
    rows = out_ref.shape[0]
    total = keep_ref[0].astype(F32) + got_ref[0].astype(F32)
    for ref in refs[:-2]:
        total = total + ref[...].astype(F32)
    squares = total[rows:rows + 8, :rows] + total[rows:rows + 8, rows:2 * rows]
    inverse = lax.rsqrt(squares / features + 1e-05)
    column = jnp.broadcast_to(inverse[:1, :], (rows, rows)).T[:, :1]
    out_ref[...] = (total[:rows, :] * column).astype(BF16)


def on_device(queries, key_vectors, value_vectors, block_order, norm_gain, kv_weight):
    rows, width = queries.shape[1:]
    heads = width // DH
    peers = lax.axis_size("tp")
    sources = lax.axis_size("cp")
    kv_width = key_vectors.shape[2]
    columns = kv_weight.shape[2]
    out_cols = columns // peers
    shape = jax.ShapeDtypeStruct
    steps = [2**i for i in range((sources - 1).bit_length())]

    pair_here = jnp.concatenate([key_vectors[0], value_vectors[0]], axis=1)
    pair = shifted(pair_here, "pp", 1)
    cut = heads * 3 // 8
    counts = [cut, heads - cut]
    starts = [0, cut]
    crossed = []

    def cross(start, count, after, micros):
        part = call(
            functools.partial(take, start * DH),
            shape((rows, count * DH), BF16),
            (queries, after),
            [WHOLE, OUTSIDE],
            name="take",
            micros=micros,
        )
        crossed.append(shifted(part, "pp", 1))

    mark = call(touch, shape((8, LANES), F32), (pair_here,), [OUTSIDE], name="touch", micros=3)
    cross(starts[0], counts[0], mark, 3)
    triple = call(join, shape((rows, 3 * kv_width), BF16), (pair, pair_here), name="join")
    moved = {d: swapped(triple, "cp", d) for d in reversed(range(1, sources))}
    triples = [triple] + [moved[d] for d in range(1, sources)]
    cross(starts[1], counts[1], triple, 0)
    features = call(
        prepare,
        shape((2, LANES, sources * rows), BF16),
        (block_order, mark),
        [SCALARS, OUTSIDE],
        name="prepare",
        micros=3,
    )
    w = call(
        weigh,
        shape((width, columns), BF16),
        (kv_weight[0], norm_gain, moved[sources - 1]),
        [WHOLE, WHOLE, OUTSIDE],
        name="weigh",
        micros=1,
    )
    kv_local = kv_width // DH
    turned = shape((kv_local, 2, DH + LANES, sources * rows), BF16)
    kt, v_all, first_context, peak = call(
        functools.partial(attend_first, heads),
        (
            turned,
            shape((kv_local, sources * rows, 2 * DH), BF16),
            shape((rows, counts[0] * DH), BF16),
            shape((1, heads), F32),
        ),
        (w, features, *reversed(triples), queries, crossed[0]),
        [OUTSIDE] + [WHOLE] * (3 + sources),
        scratch=[pltpu.VMEM(turned.shape, BF16)],
        limit=36,
        name="attend_first",
        micros=2,
    )
    def slabs(count):
        return shape((count, rows + SQUARE_ROWS, out_cols), BF16)

    def to_other_core(block):
        return lax.ppermute(block, "tp", [(i, i ^ 1) for i in range(peers)])

    last_context, give_far, give_near, squares = call(
        functools.partial(attend_last, starts[1], heads),
        (shape((rows, counts[1] * DH), BF16), slabs(peers // 2 - 1), slabs(1), shape((rows, LANES), F32)),
        (crossed[1], kt, v_all, first_context, w),
        limit=32,
        name="attend_last",
        micros=1.5,
    )
    keep_far, keep_near = [
        call(
            functools.partial(project_keep, step),
            slabs(count),
            (first_context, last_context, w, squares),
            name="project_keep",
            micros=3 if step else 0,
        )
        for step, count in ((1, peers // 2 - 1), (0, 1))
    ]
    got_far, got_near = to_other_core(give_far), to_other_core(give_near)
    for step in steps[:-1]:
        peak = call(
            larger,
            shape((1, heads), F32),
            (peak, swapped(peak, "cp", step), give_far),
            [WHOLE, WHOLE, OUTSIDE],
            name="larger",
            micros=5,
        )
    others = call(
        merge,
        [shape((rows + SQUARE_ROWS, out_cols), BF16)] * (peers // 2 - 1),
        (keep_far, got_far),
        name="merge",
    )
    others = [
        lax.ppermute(block, "tp", [(i, (i + 2 * (step + 1)) % peers) for i in range(peers)])
        for step, block in enumerate(others)
    ]
    max_logits, kv_next = call(
        functools.partial(finish, width * peers),
        (shape((1, heads), F32), shape((rows, out_cols), BF16)),
        (peak, swapped(peak, "cp", steps[-1]), keep_near, got_near, *others),
        name="finish",
    )
    return (max_logits, kv_next[None])


def solution(mesh):
    return jax.shard_map(
        on_device,
        mesh=mesh,
        in_specs=(
            P("pp", "cp", "tp"),
            P("pp", "cp", "tp"),
            P("pp", "cp", "tp"),
            P(),
            P("pp", "tp"),
            P("pp", "tp", None),
        ),
        out_specs=(P("pp", "tp"), P("pp", "cp", "tp")),
        check_vma=False,
    )
```

```python
import functools
import math

import jax
import jax.numpy as jnp
from jax import lax
from jax.experimental import pallas as pl
from jax.experimental.pallas import tpu as pltpu
from jax.sharding import PartitionSpec as P

DH = 128
LANES = 128
SQUARE_ROWS = 16
MASKED = -(2.0**100)
LOG2E = math.log2(math.e)
F32 = jnp.float32
BF16 = jnp.bfloat16
WHOLE = pl.BlockSpec(memory_space=pltpu.VMEM)
OUTSIDE = pl.BlockSpec(memory_space=pl.ANY)
SCALARS = pl.BlockSpec(memory_space=pltpu.SMEM)


def call(kernel, outs, args, specs=None, scratch=(), limit=16, name=None, aliases=None, micros=0):
    return pl.pallas_call(
        kernel,
        out_shape=outs,
        in_specs=specs or [WHOLE] * len(args),
        out_specs=jax.tree.map(lambda _: WHOLE, outs),
        scratch_shapes=scratch,
        name=name,
        input_output_aliases=aliases or {},
        cost_estimate=pl.CostEstimate(flops=int(micros * 1e9), bytes_accessed=0, transcendentals=0) if micros else None,
        compiler_params=pltpu.CompilerParams(vmem_limit_bytes=limit * 2**20),
    )(*args)


def partner(index, step, size):
    return (index + step) % size if size & (size - 1) else index ^ step


def swapped(block, axis, step):
    size = lax.axis_size(axis)
    return lax.ppermute(block, axis, [(i, partner(i, step, size)) for i in range(size)])


def shifted(block, axis, distance):
    size = lax.axis_size(axis)
    return lax.ppermute(block, axis, [((i - distance) % size, i) for i in range(size)])


def partner(index, step, size):
    return (index + step) % size if size & (size - 1) else index ^ step


def swapped(block, axis, step):
    size = lax.axis_size(axis)
    return lax.ppermute(block, axis, [(i, partner(i, step, size)) for i in range(size)])


def shifted(block, axis, distance):
    size = lax.axis_size(axis)
    return lax.ppermute(block, axis, [((i - distance) % size, i) for i in range(size)])


def bind_kernel(block_ref, after, out_ref):
    out_ref[...] = block_ref[...]


def bind(block, after):
    return call(
        bind_kernel, jax.ShapeDtypeStruct(block.shape, block.dtype), (block, after), [WHOLE, OUTSIDE], name="bind"
    )


def source_of(d, me, sources):
    return lax.rem(me - d + sources, sources) if sources & (sources - 1) else me ^ d


def take(first, q_ref, after, part_ref):
    part_ref[...] = q_ref[0, :, first:first + part_ref.shape[1]]


def prepare(order_ref, after, feature_ref):
    sources = lax.axis_size("cp")
    me = lax.axis_index("cp")
    rows = feature_ref.shape[2] // sources
    block = rows // 2
    feature = lax.broadcasted_iota(jnp.int32, (LANES, rows), 0)
    key = lax.broadcasted_iota(jnp.int32, (LANES, rows), 1)
    place = lax.rem(key, block)
    for side in range(2):
        mine = order_ref[2 * me + side]
        for d in range(sources):
            source = source_of(d, me, sources)
            other = jnp.where(key < block, order_ref[2 * source], order_ref[2 * source + 1])
            chosen = jnp.where(other == mine, place, jnp.where(other > mine, block, -1))
            feature_ref[side, :, d * rows:(d + 1) * rows] = jnp.where(feature == chosen, 1.0, 0.0).astype(BF16)


def touch(block_ref, out_ref):
    out_ref[...] = jnp.zeros(out_ref.shape, F32)


def join(pair_ref, here_ref, out_ref):
    width = pair_ref.shape[1]
    out_ref[:, :width] = pair_ref[...]
    out_ref[:, width:] = here_ref[:, :width // 2]


def arrange(after, feature_ref, *refs):
    triples, (kt_ref, v_ref, own_ref) = refs[-4::-1], refs[-3:]
    rows = triples[0].shape[0]
    kv_local = v_ref.shape[0]
    for g in range(kv_local):
        v_ref[g, :, DH:] = jnp.ones((v_ref.shape[1], DH), BF16)
        for ref in (kt_ref, own_ref):
            for side in range(2):
                ref[g, side, DH:, :] = feature_ref[side]
        for d, triple in enumerate(triples):
            part = slice(d * rows, (d + 1) * rows)
            for ref, first in ((kt_ref, g * DH), (own_ref, (2 * kv_local + g) * DH)):
                turned = triple[:, first:first + DH].astype(F32).T.astype(BF16)
                for side in range(2):
                    ref[g, side, :DH, part] = turned
            first = (kv_local + g) * DH
            v_ref[g, part, :DH] = triple[:, first:first + DH]


def spans(first_head, count, group, together):
    start = 0
    while start < count:
        g = (first_head + start) // group
        stop = min(start + together, count, (g + 1) * group - first_head)
        yield g, start, stop
        start = stop


def stacked(q_ref, start, stop, side):
    block = q_ref.shape[0] // 2
    shape = ((stop - start) * block, LANES)
    token = lax.rem(lax.broadcasted_iota(jnp.int32, shape, 0), block)
    lane = lax.broadcasted_iota(jnp.int32, shape, 1)
    blocked = jnp.where((lane > token) & (lane <= block), MASKED, 0.0).astype(BF16)
    tokens = slice(side * block, (side + 1) * block)
    q = jnp.concatenate([q_ref[tokens, h * DH:(h + 1) * DH] for h in range(start, stop)], axis=0)
    return jnp.concatenate([q, blocked], axis=1)


def attention_units(first_head, heads, q_ref, kt_ref, v_ref, ctx_ref):
    rows, width = q_ref.shape
    keys = v_ref.shape[1]
    block = rows // 2
    factor = LOG2E / math.sqrt(DH)
    units = [
        (g, start, stop, side)
        for g, start, stop in spans(first_head, width // DH, heads // v_ref.shape[0], max(1, 12 * 512 // keys))
        for side in range(2)
    ]

    def scores(unit):
        g, start, stop, side = unit
        return jnp.dot(stacked(q_ref, start, stop, side), kt_ref[g, side], preferred_element_type=F32)

    def finish_unit(unit, s):
        g, start, stop, side = unit
        m = jnp.max(s, axis=1, keepdims=True)
        p = jnp.exp2((s - m) * factor).astype(BF16)
        yield
        o = jnp.dot(p, v_ref[g], preferred_element_type=F32)
        o = (o[:, :DH] * (1.0 / o[:, DH:])).astype(BF16)
        for j in range(stop - start):
            ctx_ref[side * block:(side + 1) * block, (start + j) * DH:(start + j + 1) * DH] = o[
                j * block:(j + 1) * block, :
            ]

    ahead = [scores(unit) for unit in units[:2]]
    for n, unit in enumerate(units):
        yield from finish_unit(unit, ahead.pop(0))
        if n + 2 < len(units):
            ahead.append(scores(units[n + 2]))


def maxima_units(q_ref, own_ref, peak_ref):
    block = q_ref.shape[0] // 2
    heads = q_ref.shape[1] // DH
    keys = own_ref.shape[3]
    for g, start, stop in spans(0, heads, heads // own_ref.shape[0], max(1, 8 * 512 // keys)):
        tops = []
        for side in range(2):
            s = jnp.dot(stacked(q_ref, start, stop, side), own_ref[g, side], preferred_element_type=F32)
            yield
            top = s[:, :LANES]
            for c in range(LANES, keys, LANES):
                top = jnp.maximum(top, s[:, c:c + LANES])
            tops.append(top)
        top = jnp.maximum(*tops)
        for j in range(stop - start):
            one = jnp.max(top[j * block:(j + 1) * block, :], axis=0, keepdims=True)
            h = start + j
            peak_ref[:, h:h + 1] = jnp.max(one, axis=1, keepdims=True) * (1.0 / math.sqrt(DH))


def interleave(*streams):
    streams = list(streams)
    while streams:
        for stream in list(streams):
            if next(stream, stream) is stream:
                streams.remove(stream)


def attend_first(heads, w_ref, feature_ref, *refs):
    triples, refs = refs[:-7], refs[-7:]
    mine_ref, q_ref, kt_ref, v_ref, ctx_ref, peak_ref, own_ref = refs
    arrange(None, feature_ref, *triples, kt_ref, v_ref, own_ref)
    interleave(
        attention_units(0, heads, q_ref, kt_ref, v_ref, ctx_ref), maxima_units(mine_ref.at[0], own_ref, peak_ref)
    )


def attend_last(
    first_head, heads, q_ref, kt_ref, v_ref, first_ref, w_ref, ctx_ref, far_ref, near_ref, square_ref
):
    square_ref[...] = square_sums(first_ref)
    interleave(attention_units(first_head, heads, q_ref, kt_ref, v_ref, ctx_ref))
    squares = square_ref[...] + square_sums(ctx_ref)
    square_ref[...] = squares
    other = 1 - lax.rem(lax.axis_index("tp"), 2)
    project(first_ref, ctx_ref, w_ref, other, 1, squares, far_ref)
    project(first_ref, ctx_ref, w_ref, other, 0, squares, near_ref)


def weigh(w_ref, gain_ref, after, out_ref):
    features, columns = w_ref.shape
    for f in range(0, features, LANES):
        gain = jnp.broadcast_to(gain_ref[:, f:f + LANES].astype(F32), (LANES, LANES)).T
        for c in range(0, columns, LANES):
            out_ref[f:f + LANES, c:c + LANES] = (w_ref[f:f + LANES, c:c + LANES].astype(F32) * gain).astype(BF16)


def square_sums(ctx_ref):
    total = None
    for c in range(0, ctx_ref.shape[1], LANES):
        wide = ctx_ref[:, c:c + LANES].astype(F32)
        total = wide * wide if total is None else total + wide * wide
    return jnp.broadcast_to(jnp.sum(total, axis=1, keepdims=True), total.shape)


def columns_of(y, side, cols):
    return pl.ds(pl.multiple_of((2 * y + side) * cols, cols), cols)


def fill(ref, y, part, squares):
    rows, cols = part.shape
    lanes = squares.T[:SQUARE_ROWS, :]
    first = lanes.astype(BF16)
    rest = (lanes - first.astype(F32)).astype(BF16)
    ref[y, :rows, :] = part.astype(BF16)
    ref[y, rows:, :rows] = first
    ref[y, rows:, rows:2 * rows] = rest
    if cols > 2 * rows:
        ref[y, rows:, 2 * rows:] = jnp.zeros((SQUARE_ROWS, cols - 2 * rows), BF16)


def product(first_ref, last_ref, w_ref, at):
    cut = first_ref.shape[1]
    part = jnp.dot(first_ref[...], w_ref[:cut, at], preferred_element_type=F32)
    return part + jnp.dot(last_ref[...], w_ref[cut:, at], preferred_element_type=F32)


def project(first_ref, last_ref, w_ref, side, step, squares, out_ref):
    groups = w_ref.shape[1] // (2 * out_ref.shape[2])
    mine = lax.axis_index("tp") // 2
    for n in range(out_ref.shape[0]):
        at = columns_of(lax.rem(mine + step + n, groups), side, out_ref.shape[2])
        fill(out_ref, n, product(first_ref, last_ref, w_ref, at), squares)


def project_keep(step, first_ref, last_ref, w_ref, square_ref, out_ref):
    project(first_ref, last_ref, w_ref, lax.rem(lax.axis_index("tp"), 2), step, square_ref[...], out_ref)


def larger(left_ref, right_ref, after, out_ref):
    out_ref[...] = jnp.maximum(left_ref[...], right_ref[...])


def merge(keep_ref, got_ref, *give_refs):
    for n, ref in enumerate(give_refs):
        ref[...] = (keep_ref[n].astype(F32) + got_ref[n].astype(F32)).astype(ref.dtype)


def finish(features, peak_ref, peak_got, keep_ref, got_ref, *refs):
    peak_out, out_ref = refs[-2:]
    peak_out[...] = jnp.maximum(peak_ref[...], peak_got[...])
    rows = out_ref.shape[0]
    total = keep_ref[0].astype(F32) + got_ref[0].astype(F32)
    for ref in refs[:-2]:
        total = total + ref[...].astype(F32)
    squares = total[rows:rows + 8, :rows] + total[rows:rows + 8, rows:2 * rows]
    inverse = lax.rsqrt(squares / features + 1e-05)
    column = jnp.broadcast_to(inverse[:1, :], (rows, rows)).T[:, :1]
    out_ref[...] = (total[:rows, :] * column).astype(BF16)


def on_device(queries, key_vectors, value_vectors, block_order, norm_gain, kv_weight):
    rows, width = queries.shape[1:]
    heads = width // DH
    peers = lax.axis_size("tp")
    sources = lax.axis_size("cp")
    kv_width = key_vectors.shape[2]
    columns = kv_weight.shape[2]
    out_cols = columns // peers
    shape = jax.ShapeDtypeStruct
    steps = [2**i for i in range((sources - 1).bit_length())]

    pair_here = jnp.concatenate([key_vectors[0], value_vectors[0]], axis=1)
    pair = shifted(pair_here, "pp", 1)
    cut = heads * 7 // 16
    counts = [cut, heads - cut]
    starts = [0, cut]
    crossed = []

    def cross(start, count, after, micros):
        part = call(
            functools.partial(take, start * DH),
            shape((rows, count * DH), BF16),
            (queries, after),
            [WHOLE, OUTSIDE],
            name="take",
            micros=micros,
        )
        crossed.append(shifted(part, "pp", 1))

    mark = call(touch, shape((8, LANES), F32), (pair_here,), [OUTSIDE], name="touch", micros=3)
    cross(starts[0], counts[0], mark, 3)
    triple = call(join, shape((rows, 3 * kv_width), BF16), (pair, pair_here), name="join")
    moved = {d: swapped(triple, "cp", d) for d in reversed(range(1, sources))}
    triples = [triple] + [moved[d] for d in range(1, sources)]
    cross(starts[1], counts[1], triple, 0)
    features = call(
        prepare,
        shape((2, LANES, sources * rows), BF16),
        (block_order, mark),
        [SCALARS, OUTSIDE],
        name="prepare",
        micros=3,
    )
    w = call(
        weigh,
        shape((width, columns), BF16),
        (kv_weight[0], norm_gain, moved[sources - 1]),
        [WHOLE, WHOLE, OUTSIDE],
        name="weigh",
        micros=1,
    )
    kv_local = kv_width // DH
    turned = shape((kv_local, 2, DH + LANES, sources * rows), BF16)
    kt, v_all, first_context, peak = call(
        functools.partial(attend_first, heads),
        (
            turned,
            shape((kv_local, sources * rows, 2 * DH), BF16),
            shape((rows, counts[0] * DH), BF16),
            shape((1, heads), F32),
        ),
        (w, features, *reversed(triples), queries, crossed[0]),
        [OUTSIDE] + [WHOLE] * (3 + sources),
        scratch=[pltpu.VMEM(turned.shape, BF16)],
        limit=36,
        name="attend_first",
        micros=2,
    )
    def slabs(count):
        return shape((count, rows + SQUARE_ROWS, out_cols), BF16)

    def to_other_core(block):
        return lax.ppermute(block, "tp", [(i, i ^ 1) for i in range(peers)])

    last_context, give_far, give_near, squares = call(
        functools.partial(attend_last, starts[1], heads),
        (shape((rows, counts[1] * DH), BF16), slabs(peers // 2 - 1), slabs(1), shape((rows, LANES), F32)),
        (crossed[1], kt, v_all, first_context, w),
        limit=32,
        name="attend_last",
        micros=1.5,
    )
    keep_far, keep_near = [
        call(
            functools.partial(project_keep, step),
            slabs(count),
            (first_context, last_context, w, squares),
            name="project_keep",
            micros=3 if step else 0,
        )
        for step, count in ((1, peers // 2 - 1), (0, 1))
    ]
    got_far, got_near = to_other_core(give_far), to_other_core(give_near)
    for step in steps[:-1]:
        peak = call(
            larger,
            shape((1, heads), F32),
            (peak, swapped(peak, "cp", step), give_far),
            [WHOLE, WHOLE, OUTSIDE],
            name="larger",
            micros=5,
        )
    others = call(
        merge,
        [shape((rows + SQUARE_ROWS, out_cols), BF16)] * (peers // 2 - 1),
        (keep_far, got_far),
        name="merge",
    )
    others = [
        lax.ppermute(block, "tp", [(i, (i + 2 * (step + 1)) % peers) for i in range(peers)])
        for step, block in enumerate(others)
    ]
    max_logits, kv_next = call(
        functools.partial(finish, width * peers),
        (shape((1, heads), F32), shape((rows, out_cols), BF16)),
        (peak, swapped(peak, "cp", steps[-1]), keep_near, got_near, *others),
        name="finish",
    )
    return (max_logits, kv_next[None])


def solution(mesh):
    return jax.shard_map(
        on_device,
        mesh=mesh,
        in_specs=(
            P("pp", "cp", "tp"),
            P("pp", "cp", "tp"),
            P("pp", "cp", "tp"),
            P(),
            P("pp", "tp"),
            P("pp", "tp", None),
        ),
        out_specs=(P("pp", "tp"), P("pp", "cp", "tp")),
        check_vma=False,
    )
```
